128 devices in a mesh: leaf: 32 (over y, z, core), sub: 4 (over x).
Axes of the slice: x: 4, y: 4, z: 4, core: 2. Of those that a mesh axis runs over, the one named last changes fastest.
Arguments:
- coords: bfloat16 [8, 524288], P(None, ('leaf', 'sub')), may hold values from -6 to 6
- coefficients: bfloat16 [64, 524288], P(None, ('leaf', 'sub')), may hold values from -4 to 4
- targets: bfloat16 [64, 524288], P(None, ('leaf', 'sub')), may hold values from -6 to 6
- point_order: int32 [524288], P(('leaf', 'sub')), may hold values from 0 to 4095, as said below
- near_list: int32 [1024, 24], P(('leaf', 'sub')), may hold values from 0 to 31, as said below
- near_count: int32 [1024], P(('leaf', 'sub')), may hold values from 1 to 24, as said below
- leaf_basis: bfloat16 [1024, 512, 256], P(('leaf', 'sub')), may hold values from -0.375 to 0.375
- leaf_inverse: bfloat16 [1024, 512, 512], P(('leaf', 'sub')), may hold values from -0.25 to 0.25
- local_transfer: bfloat16 [896, 512, 256], P(('leaf', 'sub')), may hold values from -0.3125 to 0.3125
- local_couple: bfloat16 [896, 256, 256], P(('leaf', 'sub')), may hold values from -0.375 to 0.375
- sub_transfer: bfloat16 [96, 512, 256], P('leaf'), may hold values from -0.3125 to 0.3125
- sub_couple: bfloat16 [96, 256, 256], P('leaf'), may hold values from -0.375 to 0.375
- top_transfer: bfloat16 [30, 512, 256], replicated, may hold values from -0.3125 to 0.3125
- top_couple: bfloat16 [31, 256, 256], replicated, may hold values from -0.375 to 0.375
Outputs:
- product: bfloat16 [64, 524288], P(None, ('leaf', 'sub'))
- update: bfloat16 [64, 524288], P(None, ('leaf', 'sub'))
The draws below stay inside these ranges and needn't reach their ends.
Inputs may be any that keep to these rules, and one draw needn't show every extreme that they name: `point_order`: each aligned block of 4096 entries is a permutation of 0 to 4095. `near_list`: slot 0 holds the leaf itself; the used slots of a row are distinct; unused slots hold the leaf itself. Numbers are leaves of the same subtree of 32 leaves. `near_count`: the first leaf of every device uses all 24 slots.
All inputs are finite; a program needn't handle non-finite values.
Results may differ from the reference program's by a relative error of at most 0.0056.
Values may be sent and summed in bfloat16 or wider, within the bound.
No kernel may reach another device: no remote copies, remote signals or barrier semaphores. Data moves between devices by JAX's collectives and lax.ppermute only.
A program may use at most 128 MiB of HBM per device.

```python
import jax
import jax.numpy as jnp
from jax import lax

DIMS = 8
LEAF = 512
RANK = 256
RHS = 64
NEAR_SLOTS = 24
LEAVES_DEV = 8
PTS_DEV = 4096
N_LEAVES = 1024
N_PTS = 524288
GROUP_LEAVES = 32
N_LEAF = 32
N_SUB = 4


def near_tables(key):
    count_key = jax.random.fold_in(key, 11)
    offset_key = jax.random.fold_in(key, 12)
    counts = jax.random.randint(count_key, (N_LEAVES,), 1, NEAR_SLOTS + 1)
    leaf_ids = jnp.arange(N_LEAVES, dtype=jnp.int32)
    counts = jnp.where(leaf_ids % LEAVES_DEV == 0, NEAR_SLOTS, counts)
    key_list = jax.random.split(offset_key, N_LEAVES)
    offsets = jax.vmap(lambda single: jax.random.permutation(single, GROUP_LEAVES - 1))(key_list)[:, :NEAR_SLOTS - 1] + 1
    offsets = jnp.concatenate([jnp.zeros((N_LEAVES, 1), jnp.int32), offsets.astype(jnp.int32)], axis=1)
    slot_ids = jnp.arange(NEAR_SLOTS, dtype=jnp.int32)
    offsets = jnp.where(slot_ids[None, :] < counts[:, None], offsets, 0)
    own_ids = leaf_ids % GROUP_LEAVES
    lists = (own_ids[:, None] + offsets) % GROUP_LEAVES
    return (counts.astype(jnp.int32), lists.astype(jnp.int32))


def draw_near_list(key, part):
    return near_tables(key)[1]


def draw_near_count(key, part):
    return near_tables(key)[0]


def draw_point_order(key, part):
    key = jax.random.fold_in(key, 3)
    key_list = jax.random.split(key, N_LEAVES // LEAVES_DEV)
    blocks = jax.vmap(lambda single: jax.random.permutation(single, PTS_DEV))(key_list)
    return blocks.reshape(-1).astype(jnp.int32)


def block_levels(key, dims, shards, low, top_value):
    loudness, own = 1.0, jax.random.fold_in(key, 6)
    for position, shards_of in shards:
        steps = jnp.exp(jax.random.uniform(jax.random.fold_in(own, position), (shards_of,), jnp.float32, low / len(shards), top_value / len(shards)))
        loudness = loudness * jnp.repeat(steps, dims[position] // shards_of).reshape([-1 if axis == position else 1 for axis in range(len(dims))])
    return loudness


def scatter_about(stream_key, extent, deviation, reach, cuts=(), kind=jnp.bfloat16):
    values = jax.random.normal(stream_key, extent, jnp.float32) * deviation
    if len(cuts) > 0:
        values = block_levels(stream_key, extent, cuts, -0.22, 0.18) * values
    return jnp.clip(values, min=-reach, max=reach).astype(kind)


def setup_inputs(seed: int = 0) -> dict:
    splits = jax.random.split(jax.random.key(seed), 15)
    coords = scatter_about(splits[0], (DIMS, N_PTS), 1.0, 6.0, ((1, 128),))
    coefficients = scatter_about(splits[1], (RHS, N_PTS), 0.25, 4.0, ((1, 128),))
    targets = scatter_about(splits[2], (RHS, N_PTS), 1.0, 6.0, ((1, 128),))
    point_order = draw_point_order(jax.random.fold_in(splits[14], 71), 0)
    near_list = draw_near_list(jax.random.fold_in(splits[14], 71), 0)
    near_count = draw_near_count(jax.random.fold_in(splits[14], 71), 0)
    leaf_basis = scatter_about(splits[6], (N_LEAVES, LEAF, RANK), RANK ** -0.5, 0.375, ((0, 128),))
    leaf_inverse = scatter_about(splits[7], (N_LEAVES, LEAF, LEAF), LEAF ** -0.5, 0.25, ((0, 128),))
    local_transfer = scatter_about(splits[8], ((LEAVES_DEV - 1) * N_LEAF * N_SUB, 2 * RANK, RANK), (RANK * 3 // 2) ** -0.5, 0.3125, ((0, 128),))
    local_couple = scatter_about(splits[9], ((LEAVES_DEV - 1) * N_LEAF * N_SUB, RANK, RANK), RANK ** -0.5, 0.375, ((0, 128),))
    sub_transfer = scatter_about(splits[10], ((N_SUB - 1) * N_LEAF, 2 * RANK, RANK), (RANK * 3 // 2) ** -0.5, 0.3125, ((0, 32),))
    sub_couple = scatter_about(splits[11], ((N_SUB - 1) * N_LEAF, RANK, RANK), RANK ** -0.5, 0.375, ((0, 32),))
    top_transfer = scatter_about(splits[12], (N_LEAF - 2, 2 * RANK, RANK), (RANK * 3 // 2) ** -0.5, 0.3125)
    top_couple = scatter_about(splits[13], (N_LEAF - 1, RANK, RANK), RANK ** -0.5, 0.375)
    return {"coords": coords, "coefficients": coefficients, "targets": targets, "point_order": point_order, "near_list": near_list, "near_count": near_count, "leaf_basis": leaf_basis, "leaf_inverse": leaf_inverse, "local_transfer": local_transfer, "local_couple": local_couple, "sub_transfer": sub_transfer, "sub_couple": sub_couple, "top_transfer": top_transfer, "top_couple": top_couple}


RIDGE = 0.5
SHARPNESS = 0.25
HIGHEST = lax.Precision.HIGHEST


def reorder(values, point_order):
    blocks = values.reshape(values.shape[0], -1, PTS_DEV)
    indices = point_order.reshape(1, -1, PTS_DEV)
    return jnp.take_along_axis(blocks, indices, axis=2).reshape(values.shape[0], -1)


def invert(point_order):
    blocks = point_order.reshape(-1, PTS_DEV)
    row_ids = jnp.arange(blocks.shape[0], dtype=jnp.int32)[:, None]
    counter = jnp.broadcast_to(jnp.arange(PTS_DEV, dtype=jnp.int32)[None, :], blocks.shape)
    return jnp.zeros_like(blocks).at[row_ids, blocks].set(counter).reshape(-1)


def kernel_tiles(source_raw, source_sq, target_raw, target_sq):
    cross_term = jnp.einsum("dlj,dli->lji", source_raw.astype(jnp.float32), target_raw.astype(jnp.float32), precision=HIGHEST)
    distance = source_sq[:, :, None] + target_sq[:, None, :] - 2.0 * cross_term
    return jnp.exp(-SHARPNESS * distance).astype(jnp.bfloat16)


def near_field(coords, tree_x, near_list, near_count):
    raw_points = coords.reshape(DIMS, N_LEAVES, LEAF)
    points = raw_points.astype(jnp.float32)
    squares = jnp.sum(points * points, axis=0)
    leaves_x = tree_x.reshape(RHS, N_LEAVES, LEAF)
    devices = N_LEAVES // LEAVES_DEV
    all_lists = near_list.reshape(devices, LEAVES_DEV, NEAR_SLOTS)
    counts = near_count.reshape(devices, LEAVES_DEV)

    def one_device(inputs):
        device, device_list, device_count = inputs
        group_start = (device // N_SUB) * GROUP_LEAVES
        own_leaves = device * LEAVES_DEV + jnp.arange(LEAVES_DEV, dtype=jnp.int32)
        target_raw = jnp.take(raw_points, own_leaves, axis=1)
        target_sq = jnp.take(squares, own_leaves, axis=0)

        def one_slot(slot_index, running):
            source = group_start + lax.dynamic_index_in_dim(device_list, slot_index, 1, keepdims=False).astype(jnp.int32)
            tiles = kernel_tiles(jnp.take(raw_points, source, axis=1), jnp.take(squares, source, axis=0), target_raw, target_sq)
            source_x = jnp.take(leaves_x, source, axis=1).astype(jnp.float32)
            contribution = jnp.einsum("rlj,lji->lri", source_x, tiles.astype(jnp.float32), precision=HIGHEST)
            active = (device_count > slot_index).astype(jnp.float32)
            return running + active[:, None, None] * contribution

        return lax.fori_loop(0, NEAR_SLOTS, one_slot, jnp.zeros((LEAVES_DEV, RHS, LEAF), jnp.float32))

    mapped = lax.map(one_device, (jnp.arange(devices, dtype=jnp.int32), all_lists, counts))
    return mapped.reshape(N_LEAVES, RHS, LEAF)


def by_height(array, groups, per_group, skip_root):
    shaped = array.reshape((groups, array.shape[0] // groups) + array.shape[1:])
    pieces = []
    offset = 0
    node_count = per_group // 2
    lowest = 2 if skip_root else 1
    while node_count >= lowest:
        pieces.append(shaped[:, offset:offset + node_count].reshape((groups * node_count,) + array.shape[1:]))
        offset += node_count
        node_count //= 2
    return pieces


def lift_pairs(children, transfer):
    node_count = transfer.shape[0]
    joined = children.reshape(node_count, 2, children.shape[1], children.shape[2])
    joined = joined.transpose(0, 2, 1, 3).reshape(node_count, children.shape[1], 2 * children.shape[2])
    return jnp.einsum("nrk,nkq->nrq", joined, transfer.astype(jnp.float32), precision=HIGHEST)


def couple_pairs(children, coupling):
    node_count = coupling.shape[0]
    pairs = children.reshape(node_count, 2, children.shape[1], children.shape[2])
    matrices = coupling.astype(jnp.float32)
    left_term = jnp.einsum("nrk,nqk->nrq", pairs[:, 1], matrices, precision=HIGHEST)
    right_term = jnp.einsum("nrk,nkq->nrq", pairs[:, 0], matrices, precision=HIGHEST)
    return jnp.stack([left_term, right_term], axis=1).reshape(children.shape)


def lower_pairs(parents, transfer):
    node_count = transfer.shape[0]
    lowered = jnp.einsum("nrq,nkq->nrk", parents, transfer.astype(jnp.float32), precision=HIGHEST)
    lowered = lowered.reshape(node_count, parents.shape[1], 2, parents.shape[2]).transpose(0, 2, 1, 3)
    return lowered.reshape(2 * node_count, parents.shape[1], parents.shape[2])


def per_device(function, *arrays):
    devices = N_LEAVES // LEAVES_DEV
    shaped = tuple(item.reshape((devices, LEAVES_DEV) + item.shape[1:]) for item in arrays)
    mapped = lax.map(lambda group_items: function(*group_items), shaped)
    return mapped.reshape((N_LEAVES,) + mapped.shape[2:])


def project_leaves(leaves_x, basis):
    return jnp.einsum("lrp,lpk->lrk", leaves_x.astype(jnp.float32), basis.astype(jnp.float32), precision=HIGHEST)


def expand_leaves(terms, basis):
    return jnp.einsum("lrk,lpk->lrp", terms, basis.astype(jnp.float32), precision=HIGHEST)


def apply_inverse(resid, inverse):
    return jnp.einsum("lrp,lqp->lrq", resid.astype(jnp.float32), inverse.astype(jnp.float32), precision=HIGHEST)


def reference(coords, coefficients, targets, point_order, near_list, near_count, leaf_basis, leaf_inverse, local_transfer, local_couple, sub_transfer, sub_couple, top_transfer, top_couple):
    devices = N_LEAVES // LEAVES_DEV
    tree_x = reorder(coefficients, point_order)
    goal = reorder(targets, point_order)
    near = near_field(coords, tree_x, near_list, near_count)
    transfers = by_height(local_transfer, devices, LEAVES_DEV, False) + by_height(sub_transfer, N_LEAF, N_SUB, False) + by_height(top_transfer, 1, N_LEAF, True)
    couplings = by_height(local_couple, devices, LEAVES_DEV, False) + by_height(sub_couple, N_LEAF, N_SUB, False) + by_height(top_couple, 1, N_LEAF, False)
    leaves_x = tree_x.reshape(RHS, N_LEAVES, LEAF).transpose(1, 0, 2)
    coefs = [per_device(project_leaves, leaves_x, leaf_basis)]
    coupled = []
    for height_index in range(len(couplings)):
        coupled.append(couple_pairs(coefs[-1], couplings[height_index]))
        if height_index < len(transfers):
            coefs.append(lift_pairs(coefs[-1], transfers[height_index]))
    downward = coupled[-1]
    for height_index in range(len(transfers) - 1, -1, -1):
        downward = coupled[height_index] + lower_pairs(downward, transfers[height_index])
    far = per_device(expand_leaves, downward, leaf_basis)
    whole = RIDGE * leaves_x.astype(jnp.float32) + near + far
    goal_leaves = goal.reshape(RHS, N_LEAVES, LEAF).transpose(1, 0, 2).astype(jnp.float32)
    residual = (goal_leaves - whole).astype(jnp.bfloat16)
    correction = per_device(apply_inverse, residual, leaf_inverse)
    inverse_order = invert(point_order)
    whole_tree = whole.transpose(1, 0, 2).reshape(RHS, N_PTS)
    correction_tree = correction.transpose(1, 0, 2).reshape(RHS, N_PTS)
    product = reorder(whole_tree, inverse_order).astype(jnp.bfloat16)
    update = reorder(correction_tree, inverse_order).astype(jnp.bfloat16)
    return product, update
```

```python
import jax
import jax.numpy as jnp
from jax import lax
from jax.experimental import pallas as pl
from jax.experimental.pallas import tpu as pltpu
from jax.sharding import PartitionSpec as P

RIDGE = 0.5
SHARPNESS = 0.25
LOG2E = 1.4426950408889634
F32 = jnp.float32
BF16 = jnp.bfloat16

RHS = 64
DIMS = 8
LEAF = 512
RANK = 256
SLOTS = 24
LEAVES = 8
POINTS = LEAVES * LEAF
GROUP = 32
N_SUB = 4
PAYLOAD = POINTS + 2 * RANK + LEAF
FEATURES = 32
UNROLL = 8
ITEMS = LEAVES * SLOTS + UNROLL
FIRST_GROUPS = 4
TOP_BITS = 5
TOP_START = (0, 16, 24, 28, 30)
LEVEL_START = (0, 32, 48, 56, 60)
MIB = 2**20


def nn(left, right):
    return jnp.dot(left, right, preferred_element_type=F32)


def nt(left, right):
    return lax.dot_general(left, right, (((1,), (1,)), ((), ())), preferred_element_type=F32)


def halves(value):
    high = value.astype(BF16)
    return high, (value - high.astype(F32)).astype(BF16)


def stacked(value):
    return jnp.concatenate(halves(value), axis=0)


def fold(value):
    rows = value.shape[0] // 2
    return value[:rows] + value[rows:]


def nn2(value, matrix):
    return fold(nn(stacked(value), matrix))


def nt2(value, matrix):
    return fold(nt(stacked(value), matrix))


def thirds(value):
    high = value.astype(BF16).astype(F32)
    rest = value - high
    middle = rest.astype(BF16).astype(F32)
    return high, middle, rest - middle


def square_rows(points, first):
    high, middle, low = thirds(
        jnp.sum(points * points, axis=0, keepdims=True) * (-SHARPNESS * LOG2E)
    )
    row = lax.broadcasted_iota(jnp.int32, points.shape, 0) - first
    parts = jnp.where(row == 0, high, jnp.where(row == 1, middle, low))
    ones = ((row + first >= 0) & (row + first < 6)).astype(F32)
    return jnp.where((row >= 0) & (row < 3), parts, ones)


def source_features(points):
    return jnp.concatenate([points, points, points, square_rows(points, 0)], axis=0).astype(BF16)


def target_features(points):
    high, middle, low = thirds(points * (2.0 * SHARPNESS * LOG2E))
    return jnp.concatenate([high, middle, low, square_rows(points, 3)], axis=0)


def leaf_points(payload, leaf):
    start = 16 * (leaf // 2)
    pair = payload[start : start + 16, POINTS + 2 * RANK :].astype(F32)
    return pair[DIMS * (leaf % 2) : DIMS * (leaf % 2) + DIMS]


def rise_kernel(
    order, coefficients, targets, coords, basis_hbm, transfer_hbm, couple_hbm,
    payload, rows, terms,
    columns, basis, transfer, couple, arrived,
):
    copies = [
        pltpu.make_async_copy(source, target, arrived.at[number])
        for number, (source, target) in enumerate(
            ((basis_hbm, basis), (transfer_hbm, transfer), (couple_hbm, couple))
        )
    ]
    for copy in copies:
        copy.start()
    for leaf in range(LEAVES):
        span = slice(leaf * LEAF, (leaf + 1) * LEAF)
        values = coefficients[:, span].astype(F32)
        wanted = targets[:, span].astype(F32) - RIDGE * values
        columns[span, :] = jnp.concatenate([values, wanted], axis=0).T

    def pick(step, carry):
        first = pl.multiple_of(step * 16, 16)
        for offset in range(16):
            rows[pl.ds(first + offset, 1), :] = columns[pl.ds(order[first + offset], 1), :]
        return carry

    lax.fori_loop(0, POINTS // 16, pick, 0)
    copies[0].wait()
    coefs = []
    for leaf in range(LEAVES):
        span = slice(leaf * LEAF, (leaf + 1) * LEAF)
        values = rows[span, :].T[:RHS].astype(BF16)
        payload[:, span] = values
        coefs.append(nn(values, basis[leaf]))
    for pair in range(LEAVES // 2):
        both = [coords[:, leaf * LEAF : (leaf + 1) * LEAF].astype(F32) for leaf in (2 * pair, 2 * pair + 1)]
        payload[16 * pair : 16 * pair + 16, POINTS + 2 * RANK :] = jnp.concatenate(both, axis=0).astype(BF16)
    copies[1].wait()
    copies[2].wait()
    node = 0
    term = 0
    while len(coefs) > 1:
        parents = []
        for left in range(0, len(coefs), 2):
            terms[term + left] = nt2(coefs[left + 1], couple[node])
            terms[term + left + 1] = nn2(coefs[left], couple[node])
            joined = jnp.concatenate([coefs[left], coefs[left + 1]], axis=1)
            parents.append(nn2(joined, transfer[node]))
            node += 1
        term += len(coefs)
        coefs = parents
    high, low = halves(coefs[0])
    payload[:, POINTS : POINTS + RANK] = high
    payload[:, POINTS + RANK : POINTS + 2 * RANK] = low


def near_step(item, target, source, values, total):
    leaf = lax.shift_right_logical(item, 5)
    other = lax.bitwise_and(item, 31)
    tile = jnp.exp2(nn(target[leaf], source[other])).astype(BF16)
    total[leaf] += nt(tile, values[other])


def near_prepare(payload, first, source, values):
    for leaf in range(LEAVES):
        source[first + leaf] = source_features(leaf_points(payload, leaf))
        own = payload[:, leaf * LEAF : (leaf + 1) * LEAF]
        values[first + leaf] = jnp.concatenate([own, own], axis=0)


def near_targets(payload, target):
    for leaf in range(LEAVES):
        target[leaf] = target_features(leaf_points(payload, leaf)).T.astype(BF16)


def near_groups(items, start, stop, target, source, values, total):
    def group(step, carry):
        for offset in range(UNROLL):
            near_step(items[step * UNROLL + offset], target, source, values, total)
        return carry

    lax.fori_loop(start, stop, group, 0)


def near_first_kernel(
    place, near_list, near_count, payload,
    total, items, info,
    target, source, values, remote,
):
    me = place[1]
    near_local = jnp.int32(0)
    near_remote = jnp.int32(0)
    for leaf in range(LEAVES):

        def collect(slot, counts, leaf=leaf):
            local_count, remote_count = counts
            other = near_list[leaf * SLOTS + slot]
            item = leaf * GROUP + other
            items[local_count] = item
            remote[remote_count] = item
            here = (lax.shift_right_logical(other, 3) == me).astype(jnp.int32)
            return local_count + here, remote_count + 1 - here

        near_local, near_remote = lax.fori_loop(
            0, near_count[leaf], collect, (near_local, near_remote)
        )

    def append(slot, carry):
        items[near_local + slot] = remote[slot]
        return carry

    lax.fori_loop(0, near_remote, append, 0)
    used = near_local + near_remote
    items[used] = LEAVES * GROUP
    groups = jnp.minimum(near_local // UNROLL, FIRST_GROUPS)
    info[0] = groups
    info[1] = used
    total[...] = jnp.zeros_like(total)
    near_targets(payload, target)
    near_prepare(payload, me * LEAVES, source, values)
    near_groups(items, 0, groups, target, source, values, total)


def near_rest_kernel(
    place, items, info, own, right, across, left, running,
    total,
    target, source, values,
):
    me = place[1]
    near_targets(own, target)
    target[LEAVES] = jnp.zeros_like(target[LEAVES])
    for distance, payload in enumerate((own, right, across, left)):
        where = lax.bitwise_and(me + distance, 3)
        near_prepare(payload, where * LEAVES, source, values)
    total[...] = running[...]
    used = info[1]
    groups = used // UNROLL
    near_groups(items, info[0], groups, target, source, values, total)

    def pair(step, carry):
        for offset in range(2):
            near_step(items[groups * UNROLL + step * 2 + offset], target, source, values, total)
        return carry

    lax.fori_loop(0, (used - groups * UNROLL + 1) // 2, pair, 0)


def sub_kernel(
    place, own, right, across, left, transfer, couple,
    root, terms,
    coefs,
):
    me = place[1]
    for distance, pair in enumerate((own, right, across, left)):
        value = pair[:, :RANK].astype(F32) + pair[:, RANK:].astype(F32)
        coefs[lax.bitwise_and(me + distance, 3)] = value
    lower = nn2(jnp.concatenate([coefs[0], coefs[1]], axis=1), transfer[0])
    upper = nn2(jnp.concatenate([coefs[2], coefs[3]], axis=1), transfer[1])
    root[...] = nn2(jnp.concatenate([lower, upper], axis=1), transfer[2])
    half = lax.shift_right_logical(me, 1)
    sibling = stacked(coefs[lax.bitwise_xor(me, 1)])
    matrix = couple[half]
    is_left = lax.bitwise_and(me, 1) == 0
    terms[0] = fold(jnp.where(is_left, nt(sibling, matrix), nn(sibling, matrix)))
    terms[1] = jnp.where(half == 0, nt2(upper, couple[2]), nn2(lower, couple[2]))


def fall_kernel(
    place, order, gathered_hbm, top_transfer_hbm, top_couple_hbm, sub_terms, sub_transfer, terms,
    transfer_hbm, basis_hbm, inverse_hbm, near_hbm, rows_hbm,
    product, update,
    level, top_transfer, top_couple, transfer, basis, inverse, near, rows, moved, arrived, couple_arrived,
):
    leaf_place = place[0]
    me = place[1]
    copies = [
        pltpu.make_async_copy(gathered_hbm, level.at[pl.ds(0, 32)], arrived.at[0]),
        pltpu.make_async_copy(top_transfer_hbm.at[pl.ds(0, 8)], top_transfer.at[pl.ds(0, 8)], arrived.at[1]),
        pltpu.make_async_copy(top_transfer_hbm.at[pl.ds(8, 8)], top_transfer.at[pl.ds(8, 8)], arrived.at[2]),
        pltpu.make_async_copy(top_transfer_hbm.at[pl.ds(16, 14)], top_transfer.at[pl.ds(16, 14)], arrived.at[3]),
        pltpu.make_async_copy(transfer_hbm, transfer, arrived.at[4]),
        pltpu.make_async_copy(basis_hbm, basis, arrived.at[5]),
        pltpu.make_async_copy(near_hbm, near, arrived.at[6]),
        pltpu.make_async_copy(rows_hbm, rows, arrived.at[7]),
        pltpu.make_async_copy(inverse_hbm, inverse, arrived.at[8]),
    ]
    couples = [
        pltpu.make_async_copy(
            top_couple_hbm.at[TOP_START[bit] + lax.shift_right_logical(leaf_place, bit + 1)],
            top_couple.at[bit],
            couple_arrived.at[bit],
        )
        for bit in range(TOP_BITS)
    ]
    for copy in copies[:4] + couples + copies[4:]:
        copy.start()
    copies[0].wait()
    for height in range(TOP_BITS - 1):
        below = LEVEL_START[height]
        here = LEVEL_START[height + 1]
        for node in range(16 >> height):
            if height == 0 and node == 0:
                copies[1].wait()
            if height == 0 and node == 8:
                copies[2].wait()
            if height == 1 and node == 0:
                copies[3].wait()
            joined = jnp.concatenate([level[below + 2 * node], level[below + 2 * node + 1]], axis=1)
            level[here + node] = nn2(joined, top_transfer[TOP_START[height] + node])
    downward = None
    for bit in range(TOP_BITS - 1, -1, -1):
        couples[bit].wait()
        child = lax.shift_right_logical(leaf_place, bit)
        side = lax.bitwise_and(child, 1)
        sibling = stacked(level[LEVEL_START[bit] + lax.bitwise_xor(child, 1)])
        matrix = top_couple[bit]
        term = fold(jnp.where(side == 0, nt(sibling, matrix), nn(sibling, matrix)))
        if downward is None:
            downward = term
        else:
            position = TOP_START[bit] + lax.shift_right_logical(leaf_place, bit + 1)
            part = top_transfer[position, pl.ds(pl.multiple_of(side * RANK, RANK), RANK), :]
            downward = term + nt2(downward, part)
    half = lax.shift_right_logical(me, 1)
    part = sub_transfer[2, pl.ds(pl.multiple_of(half * RANK, RANK), RANK), :]
    downward = sub_terms[1] + nt2(downward, part)
    side = lax.bitwise_and(me, 1)
    part = sub_transfer[half, pl.ds(pl.multiple_of(side * RANK, RANK), RANK), :]
    downward = sub_terms[0] + nt2(downward, part)
    copies[4].wait()
    nodes = [downward]
    node_start = LEAVES - 1
    term_start = 2 * LEAVES - 2
    while len(nodes) < LEAVES:
        node_start -= len(nodes)
        term_start -= 2 * len(nodes)
        children = []
        for number, value in enumerate(nodes):
            lowered = nt2(value, transfer[node_start + number])
            children.append(terms[term_start + 2 * number] + lowered[:, :RANK])
            children.append(terms[term_start + 2 * number + 1] + lowered[:, RANK:])
        nodes = children
    for copy in copies[5:]:
        copy.wait()
    lane = lax.broadcasted_iota(jnp.int32, (LEAF, 2 * RHS), 1)
    is_whole = lane < RHS
    for leaf in range(LEAVES):
        span = slice(leaf * LEAF, (leaf + 1) * LEAF)
        high, low = halves(nodes[leaf])
        far = nt(basis[leaf], jnp.concatenate([high, high, low, low], axis=0))
        field = near[leaf] + far[:, : 2 * RHS] + far[:, 2 * RHS :]
        known = rows[span, :]
        both = jnp.where(is_whole, RIDGE * known + field, known - field)
        correction = nn(inverse[leaf], both.astype(BF16))
        rows[span, :] = jnp.where(is_whole, both, correction)

    def put(step, carry):
        first = pl.multiple_of(step * 16, 16)
        for offset in range(16):
            moved[pl.ds(order[first + offset], 1), :] = rows[pl.ds(first + offset, 1), :]
        return carry

    lax.fori_loop(0, POINTS // 16, put, 0)
    for leaf in range(LEAVES):
        span = slice(leaf * LEAF, (leaf + 1) * LEAF)
        turned = moved[span, :].T
        product[:, span] = turned[:RHS].astype(BF16)
        update[:, span] = turned[RHS:].astype(BF16)


VM = pl.BlockSpec(memory_space=pltpu.VMEM)
SM = pl.BlockSpec(memory_space=pltpu.SMEM)
HB = pl.BlockSpec(memory_space=pl.ANY)


def params(mib):
    return pltpu.CompilerParams(vmem_limit_bytes=mib * MIB)


def shape(dims, kind=F32):
    return jax.ShapeDtypeStruct(dims, kind)


def per_device(
    coords, coefficients, targets, point_order, near_list, near_count, leaf_basis, leaf_inverse,
    local_transfer, local_couple, sub_transfer, sub_couple, top_transfer, top_couple,
):
    place = jnp.stack([lax.axis_index("leaf"), lax.axis_index("sub")]).astype(jnp.int32)
    payload, rows, terms = pl.pallas_call(
        rise_kernel,
        out_shape=(
            shape((RHS, PAYLOAD), BF16),
            shape((POINTS, 2 * RHS)),
            shape((2 * LEAVES - 2, RHS, RANK)),
        ),
        in_specs=[SM, VM, VM, VM, HB, HB, HB],
        out_specs=(VM, VM, VM),
        scratch_shapes=[
            pltpu.VMEM((POINTS, 2 * RHS), F32),
            pltpu.VMEM(leaf_basis.shape, BF16),
            pltpu.VMEM(local_transfer.shape, BF16),
            pltpu.VMEM(local_couple.shape, BF16),
            pltpu.SemaphoreType.DMA((3,)),
        ],
        compiler_params=params(40),
        name="rise",
    )(point_order, coefficients, targets, coords, leaf_basis, local_transfer, local_couple)

    def from_distance(distance):
        pairs = [((place_to + distance) % N_SUB, place_to) for place_to in range(N_SUB)]
        return lax.ppermute(payload, "sub", pairs)

    right, across, left = from_distance(1), from_distance(2), from_distance(3)
    running, items, info = pl.pallas_call(
        near_first_kernel,
        out_shape=(
            shape((LEAVES + 1, LEAF, 2 * RHS)),
            shape((ITEMS,), jnp.int32),
            shape((2,), jnp.int32),
        ),
        in_specs=[SM, SM, SM, VM],
        out_specs=(VM, SM, SM),
        scratch_shapes=[
            pltpu.VMEM((LEAVES + 1, LEAF, FEATURES), BF16),
            pltpu.VMEM((GROUP, FEATURES, LEAF), BF16),
            pltpu.VMEM((GROUP, 2 * RHS, LEAF), BF16),
            pltpu.SMEM((ITEMS,), jnp.int32),
        ],
        compiler_params=params(40),
        cost_estimate=pl.CostEstimate(flops=10**10, bytes_accessed=3 * 10**6, transcendentals=0),
        name="near_first",
    )(place, near_list.reshape(-1), near_count, payload)
    pair = pl.BlockSpec((RHS, 2 * RANK), lambda step: (0, POINTS // (2 * RANK)))
    root, sub_terms = pl.pallas_call(
        sub_kernel,
        grid=(1,),
        out_shape=(shape((RHS, RANK)), shape((2, RHS, RANK))),
        in_specs=[SM, pair, pair, pair, pair, VM, VM],
        out_specs=(VM, VM),
        scratch_shapes=[pltpu.VMEM((N_SUB, RHS, RANK), F32)],
        compiler_params=params(32),
        name="sub_rise",
    )(place, payload, right, across, left, sub_transfer, sub_couple)
    gathered = lax.all_gather(root, "leaf")
    near = pl.pallas_call(
        near_rest_kernel,
        out_shape=shape((LEAVES + 1, LEAF, 2 * RHS)),
        in_specs=[SM, SM, SM, VM, VM, VM, VM, VM],
        out_specs=VM,
        scratch_shapes=[
            pltpu.VMEM((LEAVES + 1, LEAF, FEATURES), BF16),
            pltpu.VMEM((GROUP, FEATURES, LEAF), BF16),
            pltpu.VMEM((GROUP, 2 * RHS, LEAF), BF16),
        ],
        compiler_params=params(48),
        cost_estimate=pl.CostEstimate(flops=5 * 10**10, bytes_accessed=7 * 10**6, transcendentals=0),
        name="near_rest",
    )(place, items, info, payload, right, across, left, running)
    return pl.pallas_call(
        fall_kernel,
        out_shape=(shape((RHS, POINTS), BF16), shape((RHS, POINTS), BF16)),
        in_specs=[SM, SM, HB, HB, HB, VM, VM, VM, HB, HB, HB, HB, HB],
        out_specs=(VM, VM),
        scratch_shapes=[
            pltpu.VMEM((62, RHS, RANK), F32),
            pltpu.VMEM(top_transfer.shape, BF16),
            pltpu.VMEM((TOP_BITS, RANK, RANK), BF16),
            pltpu.VMEM(local_transfer.shape, BF16),
            pltpu.VMEM(leaf_basis.shape, BF16),
            pltpu.VMEM(leaf_inverse.shape, BF16),
            pltpu.VMEM((LEAVES + 1, LEAF, 2 * RHS), F32),
            pltpu.VMEM((POINTS, 2 * RHS), F32),
            pltpu.VMEM((POINTS, 2 * RHS), F32),
            pltpu.SemaphoreType.DMA((9,)),
            pltpu.SemaphoreType.DMA((TOP_BITS,)),
        ],
        compiler_params=params(56),
        name="fall",
    )(
        place, point_order, gathered, top_transfer, top_couple, sub_terms, sub_transfer, terms,
        local_transfer, leaf_basis, leaf_inverse, near, rows,
    )


def solution(mesh):
    both = ("leaf", "sub")
    in_specs = (
        P(None, both), P(None, both), P(None, both), P(both), P(both, None), P(both),
        P(both, None, None), P(both, None, None), P(both, None, None), P(both, None, None),
        P("leaf", None, None), P("leaf", None, None), P(), P(),
    )
    return jax.shard_map(
        per_device,
        mesh=mesh,
        in_specs=in_specs,
        out_specs=(P(None, both), P(None, both)),
        check_vma=False,
    )
```

```python
import functools

import jax
import jax.numpy as jnp
from jax import lax
from jax.experimental import pallas as pl
from jax.experimental.pallas import tpu as pltpu
from jax.sharding import PartitionSpec as P

RIDGE = 0.5
SHARPNESS = 0.25
LOG2E = 1.4426950408889634
F32 = jnp.float32
BF16 = jnp.bfloat16

RHS = 64
DIMS = 8
LEAF = 512
RANK = 256
SLOTS = 24
LEAVES = 8
POINTS = LEAVES * LEAF
GROUP = 32
N_SUB = 4
PAYLOAD = POINTS + LEAF
FEATURES = 32
UNROLL = 8
ITEMS = LEAVES * SLOTS + 2 * UNROLL
FIRST_GROUPS = 3
TOP_BITS = 5
TOP_START = (0, 16, 24, 28, 30)
LEVEL_START = (0, 32, 48, 56, 60)
MIB = 2**20


def nn(left, right):
    return jnp.dot(left, right, preferred_element_type=F32)


def nt(left, right):
    return lax.dot_general(left, right, (((1,), (1,)), ((), ())), preferred_element_type=F32)


def halves(value):
    high = value.astype(BF16)
    return high, (value - high.astype(F32)).astype(BF16)


def stacked(value):
    return jnp.concatenate(halves(value), axis=0)


def fold(value):
    rows = value.shape[0] // 2
    return value[:rows] + value[rows:]


def nn2(value, matrix):
    return fold(nn(stacked(value), matrix))


def nt2(value, matrix):
    return fold(nt(stacked(value), matrix))


def thirds(value):
    high = value.astype(BF16).astype(F32)
    rest = value - high
    middle = rest.astype(BF16).astype(F32)
    return high, middle, rest - middle


def square_rows(points, first):
    high, middle, low = thirds(
        jnp.sum(points * points, axis=0, keepdims=True) * (-SHARPNESS * LOG2E)
    )
    row = lax.broadcasted_iota(jnp.int32, points.shape, 0) - first
    parts = jnp.where(row == 0, high, jnp.where(row == 1, middle, low))
    ones = ((row + first >= 0) & (row + first < 6)).astype(F32)
    return jnp.where((row >= 0) & (row < 3), parts, ones)


def source_features(points):
    return jnp.concatenate([points, points, points, square_rows(points, 0)], axis=0).astype(BF16)


def target_features(points):
    high, middle, low = thirds(points * (2.0 * SHARPNESS * LOG2E))
    return jnp.concatenate([high, middle, low, square_rows(points, 3)], axis=0)


def leaf_points(payload, leaf):
    start = 16 * (leaf // 2)
    pair = payload[start : start + 16, POINTS:].astype(F32)
    return pair[DIMS * (leaf % 2) : DIMS * (leaf % 2) + DIMS]


def rise_kernel(
    order_hbm, coefficients_hbm, targets_hbm, coords_hbm, basis_hbm, transfer_hbm, couple_hbm,
    payload, skeleton, rows, terms,
    order, coefficients, targets, coords, columns, basis, transfer, couple, arrived,
):
    copies = [
        pltpu.make_async_copy(source, target, arrived.at[number])
        for number, (source, target) in enumerate(
            (
                (coefficients_hbm, coefficients),
                (targets_hbm, targets),
                (order_hbm, order),
                (basis_hbm, basis),
                (transfer_hbm, transfer),
                (couple_hbm, couple),
                (coords_hbm, coords),
            )
        )
    ]
    for copy in copies:
        copy.start()
    copies[0].wait()
    copies[1].wait()
    for leaf in range(LEAVES):
        span = slice(leaf * LEAF, (leaf + 1) * LEAF)
        values = coefficients[:, span].astype(F32)
        wanted = targets[:, span].astype(F32) - RIDGE * values
        columns[span, :] = jnp.concatenate([values, wanted], axis=0).T
    copies[2].wait()

    def pick(step, carry):
        first = pl.multiple_of(step * 16, 16)
        for offset in range(16):
            rows[pl.ds(first + offset, 1), :] = columns[pl.ds(order[first + offset], 1), :]
        return carry

    lax.fori_loop(0, POINTS // 16, pick, 0)
    copies[3].wait()
    coefs = []
    for leaf in range(LEAVES):
        span = slice(leaf * LEAF, (leaf + 1) * LEAF)
        values = rows[span, :].T[:RHS].astype(BF16)
        payload[:, span] = values
        coefs.append(nn(values, basis[leaf]))
    copies[6].wait()
    for pair in range(LEAVES // 2):
        both = [coords[:, leaf * LEAF : (leaf + 1) * LEAF].astype(F32) for leaf in (2 * pair, 2 * pair + 1)]
        payload[16 * pair : 16 * pair + 16, POINTS:] = jnp.concatenate(both, axis=0).astype(BF16)
    copies[4].wait()
    copies[5].wait()
    node = 0
    term = 0
    while len(coefs) > 1:
        parents = []
        for left in range(0, len(coefs), 2):
            terms[term + left] = nt2(coefs[left + 1], couple[node])
            terms[term + left + 1] = nn2(coefs[left], couple[node])
            joined = jnp.concatenate([coefs[left], coefs[left + 1]], axis=1)
            parents.append(nn2(joined, transfer[node]))
            node += 1
        term += len(coefs)
        coefs = parents
    high, low = halves(coefs[0])
    skeleton[:, :RANK] = high
    skeleton[:, RANK:] = low


def near_step(item, target, source, values, total):
    leaf = lax.shift_right_logical(item, 5)
    other = lax.bitwise_and(item, 31)
    tile = jnp.exp2(nn(target[leaf], source[other])).astype(BF16)
    block = values[other]
    total[leaf] += nt(tile, jnp.concatenate([block, block], axis=0))


def near_prepare(payload, first, source, values):
    for leaf in range(LEAVES):
        source[first + leaf] = source_features(leaf_points(payload, leaf))
        values[first + leaf] = payload[:, leaf * LEAF : (leaf + 1) * LEAF]


def near_groups(items, first, groups, target, source, values, total):
    def group(step, carry):
        for offset in range(UNROLL):
            near_step(items[first + step * UNROLL + offset], target, source, values, total)
        return carry

    lax.fori_loop(0, groups, group, 0)


def near_pairs(items, first, pairs, target, source, values, total):
    def pair(step, carry):
        for offset in range(2):
            near_step(items[first + step * 2 + offset], target, source, values, total)
        return carry

    lax.fori_loop(0, pairs, pair, 0)


def near_first_kernel(
    place, near_list, near_count, payload,
    total, target, relay, items, info,
    source, values,
):
    me = place[1]
    relay[...] = payload[...]
    zero = jnp.int32(0)
    counts = (zero, zero, zero)
    for leaf in range(LEAVES):

        def collect(slot, counts, leaf=leaf):
            local, beside, across = counts
            other = near_list[leaf * SLOTS + slot]
            distance = lax.bitwise_and(lax.shift_right_logical(other, 3) - me, 3)
            is_local = (distance == 0).astype(jnp.int32)
            is_across = (distance == 2).astype(jnp.int32)
            is_beside = 1 - is_local - is_across
            where = is_local * local + is_beside * (ITEMS + beside) + is_across * (2 * ITEMS + across)
            items[where] = leaf * GROUP + other
            return local + is_local, beside + is_beside, across + is_across

        counts = lax.fori_loop(0, near_count[leaf], collect, counts)
    local, beside, across = counts
    groups = jnp.minimum(local // UNROLL, FIRST_GROUPS)
    late = local - groups * UNROLL

    def append(slot, carry):
        items[ITEMS + beside + slot] = items[groups * UNROLL + slot]
        return carry

    lax.fori_loop(0, late, append, 0)
    items[ITEMS + beside + late] = LEAVES * GROUP + me * LEAVES
    items[2 * ITEMS + across] = LEAVES * GROUP + lax.bitwise_and(me + 2, 3) * LEAVES
    info[0] = beside + late
    info[1] = across
    total[...] = jnp.zeros_like(total)
    for leaf in range(LEAVES):
        target[leaf] = target_features(leaf_points(payload, leaf)).T.astype(BF16)
    target[LEAVES] = jnp.zeros_like(target[LEAVES])
    near_prepare(payload, me * LEAVES, source, values)
    near_groups(items, 0, groups, target, source, values, total)


def near_later_kernel(
    segment, distances, place, items, info, target, running, *refs,
):
    payloads, (total, source, values) = refs[: len(distances)], refs[len(distances) :]
    for distance, payload in zip(distances, payloads):
        where = lax.bitwise_and(place[1] + distance, 3)
        near_prepare(payload, where * LEAVES, source, values)
    total[...] = running[...]
    used = info[segment - 1]
    groups = used // UNROLL
    first = segment * ITEMS
    near_groups(items, first, groups, target, source, values, total)
    near_pairs(
        items, first + groups * UNROLL, (used - groups * UNROLL + 1) // 2,
        target, source, values, total,
    )


def sub_kernel(
    place, info, own, right, across, left, transfer_hbm, couple_hbm,
    root, terms,
    coefs, transfer, couple, arrived,
):
    copies = [
        pltpu.make_async_copy(transfer_hbm, transfer, arrived.at[0]),
        pltpu.make_async_copy(couple_hbm, couple, arrived.at[1]),
    ]
    for copy in copies:
        copy.start()
    me = place[1]
    for distance, pair in enumerate((own, right, across, left)):
        value = pair[:, :RANK].astype(F32) + pair[:, RANK:].astype(F32)
        coefs[lax.bitwise_and(me + distance, 3)] = value
    for copy in copies:
        copy.wait()
    lower = nn2(jnp.concatenate([coefs[0], coefs[1]], axis=1), transfer[0])
    upper = nn2(jnp.concatenate([coefs[2], coefs[3]], axis=1), transfer[1])
    root[...] = nn2(jnp.concatenate([lower, upper], axis=1), transfer[2])
    half = lax.shift_right_logical(me, 1)
    sibling = stacked(coefs[lax.bitwise_xor(me, 1)])
    matrix = couple[half]
    is_left = lax.bitwise_and(me, 1) == 0
    terms[0] = fold(jnp.where(is_left, nt(sibling, matrix), nn(sibling, matrix)))
    terms[1] = jnp.where(half == 0, nt2(upper, couple[2]), nn2(lower, couple[2]))


def fall_kernel(
    place, order, gathered_hbm, top_transfer_hbm, top_couple_hbm, sub_terms, terms,
    sub_transfer_hbm, transfer_hbm, basis_hbm, inverse_hbm, near, known_rows,
    product, update,
    level, top_transfer, top_couple, sub_transfer, transfer, basis, inverse, rows, moved, arrived, couple_arrived,
):
    leaf_place = place[0]
    me = place[1]
    copies = [
        pltpu.make_async_copy(gathered_hbm, level.at[pl.ds(0, 32)], arrived.at[0]),
        pltpu.make_async_copy(top_transfer_hbm.at[pl.ds(0, 8)], top_transfer.at[pl.ds(0, 8)], arrived.at[1]),
        pltpu.make_async_copy(top_transfer_hbm.at[pl.ds(8, 8)], top_transfer.at[pl.ds(8, 8)], arrived.at[2]),
        pltpu.make_async_copy(top_transfer_hbm.at[pl.ds(16, 14)], top_transfer.at[pl.ds(16, 14)], arrived.at[3]),
        pltpu.make_async_copy(transfer_hbm, transfer, arrived.at[4]),
        pltpu.make_async_copy(basis_hbm, basis, arrived.at[5]),
        pltpu.make_async_copy(inverse_hbm, inverse, arrived.at[6]),
        pltpu.make_async_copy(sub_transfer_hbm, sub_transfer, arrived.at[7]),
    ]
    couples = [
        pltpu.make_async_copy(
            top_couple_hbm.at[TOP_START[bit] + lax.shift_right_logical(leaf_place, bit + 1)],
            top_couple.at[bit],
            couple_arrived.at[bit],
        )
        for bit in range(TOP_BITS)
    ]
    for copy in copies[:4] + couples + copies[4:]:
        copy.start()
    copies[0].wait()
    for height in range(TOP_BITS - 1):
        below = LEVEL_START[height]
        here = LEVEL_START[height + 1]
        for node in range(16 >> height):
            if height == 0 and node == 0:
                copies[1].wait()
            if height == 0 and node == 8:
                copies[2].wait()
            if height == 1 and node == 0:
                copies[3].wait()
            joined = jnp.concatenate([level[below + 2 * node], level[below + 2 * node + 1]], axis=1)
            level[here + node] = nn2(joined, top_transfer[TOP_START[height] + node])
    downward = None
    for bit in range(TOP_BITS - 1, -1, -1):
        couples[bit].wait()
        child = lax.shift_right_logical(leaf_place, bit)
        side = lax.bitwise_and(child, 1)
        sibling = stacked(level[LEVEL_START[bit] + lax.bitwise_xor(child, 1)])
        matrix = top_couple[bit]
        term = fold(jnp.where(side == 0, nt(sibling, matrix), nn(sibling, matrix)))
        if downward is None:
            downward = term
        else:
            position = TOP_START[bit] + lax.shift_right_logical(leaf_place, bit + 1)
            part = top_transfer[position, pl.ds(pl.multiple_of(side * RANK, RANK), RANK), :]
            downward = term + nt2(downward, part)
    copies[7].wait()
    half = lax.shift_right_logical(me, 1)
    part = sub_transfer[2, pl.ds(pl.multiple_of(half * RANK, RANK), RANK), :]
    downward = sub_terms[1] + nt2(downward, part)
    side = lax.bitwise_and(me, 1)
    part = sub_transfer[half, pl.ds(pl.multiple_of(side * RANK, RANK), RANK), :]
    downward = sub_terms[0] + nt2(downward, part)
    copies[4].wait()
    nodes = [downward]
    node_start = LEAVES - 1
    term_start = 2 * LEAVES - 2
    while len(nodes) < LEAVES:
        node_start -= len(nodes)
        term_start -= 2 * len(nodes)
        children = []
        for number, value in enumerate(nodes):
            lowered = nt2(value, transfer[node_start + number])
            children.append(terms[term_start + 2 * number] + lowered[:, :RANK])
            children.append(terms[term_start + 2 * number + 1] + lowered[:, RANK:])
        nodes = children
    for copy in copies[5:7]:
        copy.wait()
    lane = lax.broadcasted_iota(jnp.int32, (LEAF, 2 * RHS), 1)
    is_whole = lane < RHS
    for leaf in range(LEAVES):
        span = slice(leaf * LEAF, (leaf + 1) * LEAF)
        high, low = halves(nodes[leaf])
        far = nt(basis[leaf], jnp.concatenate([high, high, low, low], axis=0))
        field = near[leaf] + far[:, : 2 * RHS] + far[:, 2 * RHS :]
        known = known_rows[span, :]
        both = jnp.where(is_whole, RIDGE * known + field, known - field)
        correction = nn(inverse[leaf], both.astype(BF16))
        rows[span, :] = jnp.where(is_whole, both, correction)

    def put(step, carry):
        first = pl.multiple_of(step * 16, 16)
        for offset in range(16):
            moved[pl.ds(order[first + offset], 1), :] = rows[pl.ds(first + offset, 1), :]
        return carry

    lax.fori_loop(0, POINTS // 16, put, 0)
    for leaf in range(LEAVES):
        span = slice(leaf * LEAF, (leaf + 1) * LEAF)
        turned = moved[span, :].T
        product[:, span] = turned[:RHS].astype(BF16)
        update[:, span] = turned[RHS:].astype(BF16)


VM = pl.BlockSpec(memory_space=pltpu.VMEM)
SM = pl.BlockSpec(memory_space=pltpu.SMEM)
HB = pl.BlockSpec(memory_space=pltpu.HBM)


def params(mib):
    return pltpu.CompilerParams(vmem_limit_bytes=mib * MIB)


def shape(dims, kind=F32):
    return jax.ShapeDtypeStruct(dims, kind)


def from_distance(value, distance):
    pairs = [((receiver + distance) % N_SUB, receiver) for receiver in range(N_SUB)]
    return lax.ppermute(value, "sub", pairs)


def per_device(
    coords, coefficients, targets, point_order, near_list, near_count, leaf_basis, leaf_inverse,
    local_transfer, local_couple, sub_transfer, sub_couple, top_transfer, top_couple,
):
    place = jnp.stack([lax.axis_index("leaf"), lax.axis_index("sub")]).astype(jnp.int32)
    payload, skeleton, rows, terms = pl.pallas_call(
        rise_kernel,
        out_shape=(
            shape((RHS, PAYLOAD), BF16),
            shape((RHS, 2 * RANK), BF16),
            shape((POINTS, 2 * RHS)),
            shape((2 * LEAVES - 2, RHS, RANK)),
        ),
        in_specs=[HB] * 7,
        out_specs=(VM, VM, VM, VM),
        scratch_shapes=[
            pltpu.SMEM(point_order.shape, jnp.int32),
            pltpu.VMEM(coefficients.shape, BF16),
            pltpu.VMEM(targets.shape, BF16),
            pltpu.VMEM(coords.shape, BF16),
            pltpu.VMEM((POINTS, 2 * RHS), F32),
            pltpu.VMEM(leaf_basis.shape, BF16),
            pltpu.VMEM(local_transfer.shape, BF16),
            pltpu.VMEM(local_couple.shape, BF16),
            pltpu.SemaphoreType.DMA((7,)),
        ],
        compiler_params=params(56),
        name="rise",
    )(point_order, coefficients, targets, coords, leaf_basis, local_transfer, local_couple)
    pieces = [skeleton] + [from_distance(skeleton, distance) for distance in (1, 2, 3)]
    right, left = from_distance(payload, 1), from_distance(payload, 3)
    total = shape((LEAVES + 1, LEAF, 2 * RHS))
    tables = [
        pltpu.VMEM((GROUP, FEATURES, LEAF), BF16),
        pltpu.VMEM((GROUP, RHS, LEAF), BF16),
    ]
    running, target, relay, items, info = pl.pallas_call(
        near_first_kernel,
        out_shape=(
            total,
            shape((LEAVES + 1, LEAF, FEATURES), BF16),
            shape((RHS, PAYLOAD), BF16),
            shape((3 * ITEMS,), jnp.int32),
            shape((2,), jnp.int32),
        ),
        in_specs=[SM, SM, SM, VM],
        out_specs=(VM, VM, VM, SM, SM),
        scratch_shapes=tables,
        compiler_params=params(16),
        cost_estimate=pl.CostEstimate(flops=10**10, bytes_accessed=10**6, transcendentals=0),
        name="near_first",
    )(place, near_list.reshape(-1), near_count, payload)
    root, sub_terms = pl.pallas_call(
        sub_kernel,
        out_shape=(shape((RHS, RANK)), shape((2, RHS, RANK))),
        in_specs=[SM, SM, VM, VM, VM, VM, HB, HB],
        out_specs=(VM, VM),
        scratch_shapes=[
            pltpu.VMEM((N_SUB, RHS, RANK), F32),
            pltpu.VMEM(sub_transfer.shape, BF16),
            pltpu.VMEM(sub_couple.shape, BF16),
            pltpu.SemaphoreType.DMA((2,)),
        ],
        compiler_params=params(16),
        name="sub_rise",
    )(place, info, *pieces, sub_transfer, sub_couple)
    gathered = lax.all_gather(root, "leaf")
    across = from_distance(relay, 2)

    def later(segment, distances, running, payloads):
        return pl.pallas_call(
            functools.partial(near_later_kernel, segment, distances),
            out_shape=total,
            in_specs=[SM, SM, SM, VM, VM] + [VM] * len(payloads),
            out_specs=VM,
            scratch_shapes=tables,
            compiler_params=params(16),
            cost_estimate=pl.CostEstimate(
                flops=10**11, bytes_accessed=10**6, transcendentals=0
            ),
            name="near_beside" if segment == 1 else "near_across",
        )(place, items, info, target, running, *payloads)

    running = later(1, (0, 1, 3), running, (payload, right, left))
    near = later(2, (2,), running, (across,))
    return pl.pallas_call(
        fall_kernel,
        out_shape=(shape((RHS, POINTS), BF16), shape((RHS, POINTS), BF16)),
        in_specs=[SM, SM, HB, HB, HB, VM, VM, HB, HB, HB, HB, VM, VM],
        out_specs=(VM, VM),
        scratch_shapes=[
            pltpu.VMEM((62, RHS, RANK), F32),
            pltpu.VMEM(top_transfer.shape, BF16),
            pltpu.VMEM((TOP_BITS, RANK, RANK), BF16),
            pltpu.VMEM(sub_transfer.shape, BF16),
            pltpu.VMEM(local_transfer.shape, BF16),
            pltpu.VMEM(leaf_basis.shape, BF16),
            pltpu.VMEM(leaf_inverse.shape, BF16),
            pltpu.VMEM((POINTS, 2 * RHS), F32),
            pltpu.VMEM((POINTS, 2 * RHS), F32),
            pltpu.SemaphoreType.DMA((8,)),
            pltpu.SemaphoreType.DMA((TOP_BITS,)),
        ],
        compiler_params=params(36),
        name="fall",
    )(
        place, point_order, gathered, top_transfer, top_couple, sub_terms, terms,
        sub_transfer, local_transfer, leaf_basis, leaf_inverse, near, rows,
    )


def solution(mesh):
    both = ("leaf", "sub")
    in_specs = (
        P(None, both), P(None, both), P(None, both), P(both), P(both, None), P(both),
        P(both, None, None), P(both, None, None), P(both, None, None), P(both, None, None),
        P("leaf", None, None), P("leaf", None, None), P(), P(),
    )
    return jax.shard_map(
        per_device,
        mesh=mesh,
        in_specs=in_specs,
        out_specs=(P(None, both), P(None, both)),
        check_vma=False,
    )
```

```python
import functools

import jax
import jax.numpy as jnp
from jax import lax
from jax.experimental import pallas as pl
from jax.experimental.pallas import tpu as pltpu
from jax.sharding import PartitionSpec as P

RIDGE = 0.5
SHARPNESS = 0.25
LOG2E = 1.4426950408889634
F32 = jnp.float32
BF16 = jnp.bfloat16

RHS = 64
DIMS = 8
LEAF = 512
RANK = 256
SLOTS = 24
LEAVES = 8
POINTS = LEAVES * LEAF
GROUP = 32
N_SUB = 4
PAYLOAD = POINTS + LEAF
FEATURES = 32
UNROLL = 8
ITEMS = LEAVES * SLOTS + 2 * UNROLL
FIRST_GROUPS = 3
TOP_BITS = 5
TOP_START = (0, 16, 24, 28, 30)
PAIRS = 16
LEVEL_START = (None, 0, 16, 24, 28)
VMEM_LIMIT = 56 * 2**20
FIRST_FLOPS = 10**10
LATER_FLOPS = 10**11


def nn(left, right):
    return jnp.dot(left, right, preferred_element_type=F32)


def nt(left, right):
    return lax.dot_general(left, right, (((1,), (1,)), ((), ())), preferred_element_type=F32)


def halves(value):
    high = value.astype(BF16)
    return high, (value - high.astype(F32)).astype(BF16)


def stacked(value):
    return jnp.concatenate(halves(value), axis=0)


def fold(value):
    rows = value.shape[0] // 2
    return value[:rows] + value[rows:]


def nn2(value, matrix):
    return fold(nn(stacked(value), matrix))


def nt2(value, matrix):
    return fold(nt(stacked(value), matrix))


def thirds(value):
    high = value.astype(BF16).astype(F32)
    rest = value - high
    middle = rest.astype(BF16).astype(F32)
    return high, middle, rest - middle


def square_rows(points, first):
    high, middle, low = thirds(
        jnp.sum(points * points, axis=0, keepdims=True) * (-SHARPNESS * LOG2E)
    )
    row = lax.broadcasted_iota(jnp.int32, points.shape, 0) - first
    parts = jnp.where(row == 0, high, jnp.where(row == 1, middle, low))
    ones = ((row + first >= 0) & (row + first < 6)).astype(F32)
    return jnp.where((row >= 0) & (row < 3), parts, ones)


def source_features(points):
    return jnp.concatenate([points, points, points, square_rows(points, 0)], axis=0).astype(BF16)


def target_features(points):
    high, middle, low = thirds(points * (2.0 * SHARPNESS * LOG2E))
    return jnp.concatenate([high, middle, low, square_rows(points, 3)], axis=0)


def leaf_points(payload, leaf):
    start = 16 * (leaf // 2)
    pair = payload[start : start + 16, POINTS:].astype(F32)
    return pair[DIMS * (leaf % 2) : DIMS * (leaf % 2) + DIMS]


def start_all(moves, arrived):
    copies = [
        pltpu.make_async_copy(source, target, arrived.at[number])
        for number, (source, target) in enumerate(moves)
    ]
    for copy in copies:
        copy.start()
    return copies


def wait_all(copies):
    for copy in copies:
        copy.wait()


def rise_kernel(
    order_hbm, coefficients_hbm, targets_hbm, coords_hbm, basis_hbm, transfer_hbm, couple_hbm,
    payload_hbm, skeleton, rows_hbm, terms_hbm,
    order, coefficients, targets, coords, columns, basis, transfer, couple,
    payload, rows, terms, arrived, left,
):
    copies = start_all(
        (
            (coefficients_hbm, coefficients),
            (targets_hbm, targets),
            (order_hbm, order),
            (basis_hbm, basis),
            (transfer_hbm, transfer),
            (couple_hbm, couple),
            (coords_hbm, coords),
        ),
        arrived,
    )
    wait_all(copies[:2])
    for leaf in range(LEAVES):
        span = slice(leaf * LEAF, (leaf + 1) * LEAF)
        values = coefficients[:, span].astype(F32)
        wanted = targets[:, span].astype(F32) - RIDGE * values
        columns[span, :] = jnp.concatenate([values, wanted], axis=0).T
    copies[2].wait()

    def pick(step, carry):
        first = pl.multiple_of(step * 16, 16)
        for offset in range(16):
            rows[pl.ds(first + offset, 1), :] = columns[pl.ds(order[first + offset], 1), :]
        return carry

    lax.fori_loop(0, POINTS // 16, pick, 0)
    sent = [pltpu.make_async_copy(rows, rows_hbm, left.at[0])]
    sent[0].start()
    copies[3].wait()
    coefs = []
    for leaf in range(LEAVES):
        span = slice(leaf * LEAF, (leaf + 1) * LEAF)
        values = rows[span, :].T[:RHS].astype(BF16)
        payload[:, span] = values
        coefs.append(nn(values, basis[leaf]))
    copies[6].wait()
    for pair in range(LEAVES // 2):
        both = [coords[:, leaf * LEAF : (leaf + 1) * LEAF].astype(F32) for leaf in (2 * pair, 2 * pair + 1)]
        payload[16 * pair : 16 * pair + 16, POINTS:] = jnp.concatenate(both, axis=0).astype(BF16)
    sent.append(pltpu.make_async_copy(payload, payload_hbm, left.at[1]))
    sent[1].start()
    wait_all(copies[4:6])
    node = 0
    term = 0
    while len(coefs) > 1:
        parents = []
        for left_child in range(0, len(coefs), 2):
            one, two = coefs[left_child], coefs[left_child + 1]
            terms[term + left_child] = nt2(two, couple[node])
            terms[term + left_child + 1] = nn2(one, couple[node])
            parents.append(nn2(jnp.concatenate([one, two], axis=1), transfer[node]))
            node += 1
        term += len(coefs)
        coefs = parents
    sent.append(pltpu.make_async_copy(terms, terms_hbm, left.at[2]))
    sent[2].start()
    high, low = halves(coefs[0])
    skeleton[:, :RANK] = high
    skeleton[:, RANK:] = low
    wait_all(sent)


def near_step(item, target, source, values, total):
    leaf = lax.shift_right_logical(item, 5)
    other = lax.bitwise_and(item, 31)
    tile = jnp.exp2(nn(target[leaf], source[other])).astype(BF16)
    block = values[other]
    total[leaf] += nt(tile, jnp.concatenate([block, block], axis=0))


def near_prepare(payload, first, source, values):
    for leaf in range(LEAVES):
        source[first + leaf] = source_features(leaf_points(payload, leaf))
        values[first + leaf] = payload[:, leaf * LEAF : (leaf + 1) * LEAF]


def near_groups(items, first, groups, target, source, values, total):
    def group(step, carry):
        for offset in range(UNROLL):
            near_step(items[first + step * UNROLL + offset], target, source, values, total)
        return carry

    lax.fori_loop(0, groups, group, 0)


def near_pairs(items, first, pairs, target, source, values, total):
    def pair(step, carry):
        for offset in range(2):
            near_step(items[first + step * 2 + offset], target, source, values, total)
        return carry

    lax.fori_loop(0, pairs, pair, 0)


def near_first_kernel(
    place, ticket, near_list, near_count, payload_hbm,
    total_hbm, target_hbm, relay_hbm, items, info,
    source, values, payload, total, target, arrived, left,
):
    copies = start_all(((payload_hbm, payload),), arrived)
    sent = start_all(((payload_hbm, relay_hbm),), left)
    me = place[1]
    zero = jnp.int32(0)
    counts = (zero, zero, zero)
    for leaf in range(LEAVES):

        def collect(slot, counts, leaf=leaf):
            local, beside, across = counts
            other = near_list[leaf * SLOTS + slot]
            distance = lax.bitwise_and(lax.shift_right_logical(other, 3) - me, 3)
            is_local = (distance == 0).astype(jnp.int32)
            is_across = (distance == 2).astype(jnp.int32)
            is_beside = 1 - is_local - is_across
            where = is_local * local + is_beside * (ITEMS + beside) + is_across * (2 * ITEMS + across)
            items[where] = leaf * GROUP + other
            return local + is_local, beside + is_beside, across + is_across

        counts = lax.fori_loop(0, near_count[leaf], collect, counts)
    local, beside, across = counts
    groups = jnp.minimum(local // UNROLL, FIRST_GROUPS)
    late = local - groups * UNROLL

    def append(slot, carry):
        items[ITEMS + beside + slot] = items[groups * UNROLL + slot]
        return carry

    lax.fori_loop(0, late, append, 0)
    items[ITEMS + beside + late] = LEAVES * GROUP + me * LEAVES
    items[2 * ITEMS + across] = LEAVES * GROUP + lax.bitwise_and(me + 2, 3) * LEAVES
    info[0] = beside + late
    info[1] = across
    total[...] = jnp.zeros_like(total)
    wait_all(copies)
    for leaf in range(LEAVES):
        target[leaf] = target_features(leaf_points(payload, leaf)).T.astype(BF16)
    target[LEAVES] = jnp.zeros_like(target[LEAVES])
    sent.append(pltpu.make_async_copy(target, target_hbm, left.at[1]))
    sent[1].start()
    near_prepare(payload, me * LEAVES, source, values)
    near_groups(items, 0, groups, target, source, values, total)
    sent.append(pltpu.make_async_copy(total, total_hbm, left.at[2]))
    sent[2].start()
    wait_all(sent)


def near_later_kernel(segment, distances, place, items, info, before, target_hbm, *refs):
    count = len(distances)
    payloads_hbm, total_hbm, ticket = refs[:count], refs[count], refs[count + 1]
    source, values, total, target, payloads, arrived, left = refs[count + 2 :]
    ticket[0] = segment
    copies = start_all(
        [(payload_hbm, payloads.at[number]) for number, payload_hbm in enumerate(payloads_hbm)]
        + [(target_hbm, target)],
        arrived,
    )
    total[...] = jnp.zeros_like(total)
    for number, distance in enumerate(distances):
        copies[number].wait()
        where = lax.bitwise_and(place[1] + distance, 3)
        near_prepare(payloads.at[number], where * LEAVES, source, values)
    copies[count].wait()
    used = info[segment - 1]
    groups = used // UNROLL
    first = segment * ITEMS
    near_groups(items, first, groups, target, source, values, total)
    near_pairs(
        items, first + groups * UNROLL, (used - groups * UNROLL + 1) // 2,
        target, source, values, total,
    )
    wait_all(start_all(((total, total_hbm),), left))


def sub_kernel(
    place, own, right, across, left, transfer_hbm, couple_hbm, payload_hbm,
    root, terms, relay_hbm, ticket,
    coefs, transfer, couple, arrived,
):
    copies = start_all(
        ((transfer_hbm, transfer), (couple_hbm, couple), (payload_hbm, relay_hbm)), arrived
    )
    me = place[1]
    ticket[0] = me
    for distance, pair in enumerate((own, right, across, left)):
        value = pair[:, :RANK].astype(F32) + pair[:, RANK:].astype(F32)
        coefs[lax.bitwise_and(me + distance, 3)] = value
    wait_all(copies[:2])
    lower = nn2(jnp.concatenate([coefs[0], coefs[1]], axis=1), transfer[0])
    upper = nn2(jnp.concatenate([coefs[2], coefs[3]], axis=1), transfer[1])
    root[...] = nn2(jnp.concatenate([lower, upper], axis=1), transfer[2])
    half = lax.shift_right_logical(me, 1)
    sibling = stacked(coefs[lax.bitwise_xor(me, 1)])
    matrix = couple[half]
    is_left = lax.bitwise_and(me, 1) == 0
    terms[0] = fold(jnp.where(is_left, nt(sibling, matrix), nn(sibling, matrix)))
    terms[1] = jnp.where(half == 0, nt2(upper, couple[2]), nn2(lower, couple[2]))
    copies[2].wait()


def pair_kernel(
    place, info, own, partner, transfer_hbm, couple_hbm,
    root, term,
    transfer, couple, arrived,
):
    node = lax.shift_right_logical(place[0], 1)
    is_left = lax.bitwise_and(place[0], 1) == 0
    copies = start_all(
        ((transfer_hbm.at[node], transfer), (couple_hbm.at[node], couple)), arrived
    )
    one = jnp.where(is_left, own[...], partner[...])
    two = jnp.where(is_left, partner[...], own[...])
    wait_all(copies)
    root[...] = nn2(jnp.concatenate([one, two], axis=1), transfer[...])
    sibling = stacked(partner[...])
    term[...] = fold(jnp.where(is_left, nt(sibling, couple[...]), nn(sibling, couple[...])))


def fall_kernel(
    place, order_hbm, gathered_hbm, top_transfer_hbm, top_couple_hbm, pair_term_hbm,
    sub_terms_hbm, terms_hbm, sub_transfer_hbm, transfer_hbm, basis_hbm, inverse_hbm,
    near_0_hbm, near_1_hbm, near_2_hbm, known_hbm,
    product, update,
    order, level, top_transfer, pair_transfer, top_couple, pair_term,
    sub_terms, terms, sub_transfer, transfer, basis, inverse,
    near, rows, moved, arrived, couple_arrived,
):
    leaf_place = place[0]
    me = place[1]
    copies = start_all(
        (
            (gathered_hbm, level.at[pl.ds(0, PAIRS)]),
            (top_transfer_hbm.at[pl.ds(TOP_START[1], 8)], top_transfer.at[pl.ds(0, 8)]),
            (top_transfer_hbm.at[pl.ds(TOP_START[2], 6)], top_transfer.at[pl.ds(8, 6)]),
        ),
        arrived,
    )
    couples = start_all(
        [
            (
                top_couple_hbm.at[TOP_START[bit] + lax.shift_right_logical(leaf_place, bit + 1)],
                top_couple.at[bit],
            )
            for bit in range(1, TOP_BITS)
        ],
        couple_arrived,
    )
    later = start_all(
        (
            (top_transfer_hbm.at[lax.shift_right_logical(leaf_place, 1)], pair_transfer),
            (pair_term_hbm, pair_term),
            (sub_terms_hbm, sub_terms),
            (sub_transfer_hbm, sub_transfer),
            (terms_hbm, terms),
            (transfer_hbm, transfer),
        ),
        arrived.at[pl.ds(3, 6)],
    )
    last = start_all(
        (
            (basis_hbm, basis),
            (near_0_hbm, near.at[0]),
            (near_1_hbm, near.at[1]),
            (near_2_hbm, near.at[2]),
            (known_hbm, rows),
            (inverse_hbm, inverse),
            (order_hbm, order),
        ),
        arrived.at[pl.ds(9, 7)],
    )
    copies[0].wait()
    for height in range(1, TOP_BITS - 1):
        below = LEVEL_START[height]
        here = LEVEL_START[height + 1]
        if height < 3:
            copies[height].wait()
        for node in range(PAIRS >> height):
            joined = jnp.concatenate([level[below + 2 * node], level[below + 2 * node + 1]], axis=1)
            level[here + node] = nn2(joined, top_transfer[TOP_START[height] - PAIRS + node])
    wait_all(couples)
    downward = None
    for bit in range(TOP_BITS - 1, 0, -1):
        child = lax.shift_right_logical(leaf_place, bit)
        side = lax.bitwise_and(child, 1)
        sibling = stacked(level[LEVEL_START[bit] + lax.bitwise_xor(child, 1)])
        matrix = top_couple[bit]
        term = fold(jnp.where(side == 0, nt(sibling, matrix), nn(sibling, matrix)))
        if downward is None:
            downward = term
        else:
            position = TOP_START[bit] - PAIRS + lax.shift_right_logical(leaf_place, bit + 1)
            part = top_transfer[position, pl.ds(pl.multiple_of(side * RANK, RANK), RANK), :]
            downward = term + nt2(downward, part)
    wait_all(later)
    side = lax.bitwise_and(leaf_place, 1)
    part = pair_transfer[pl.ds(pl.multiple_of(side * RANK, RANK), RANK), :]
    downward = pair_term[...] + nt2(downward, part)
    half = lax.shift_right_logical(me, 1)
    part = sub_transfer[2, pl.ds(pl.multiple_of(half * RANK, RANK), RANK), :]
    downward = sub_terms[1] + nt2(downward, part)
    side = lax.bitwise_and(me, 1)
    part = sub_transfer[half, pl.ds(pl.multiple_of(side * RANK, RANK), RANK), :]
    downward = sub_terms[0] + nt2(downward, part)
    nodes = [downward]
    node_start = LEAVES - 1
    term_start = 2 * LEAVES - 2
    while len(nodes) < LEAVES:
        node_start -= len(nodes)
        term_start -= 2 * len(nodes)
        children = []
        for number, value in enumerate(nodes):
            lowered = nt2(value, transfer[node_start + number])
            children.append(terms[term_start + 2 * number] + lowered[:, :RANK])
            children.append(terms[term_start + 2 * number + 1] + lowered[:, RANK:])
        nodes = children
    wait_all(last)
    lane = lax.broadcasted_iota(jnp.int32, (LEAF, 2 * RHS), 1)
    is_whole = lane < RHS
    for leaf in range(LEAVES):
        span = slice(leaf * LEAF, (leaf + 1) * LEAF)
        high, low = halves(nodes[leaf])
        far = nt(basis[leaf], jnp.concatenate([high, high, low, low], axis=0))
        field = near[0, leaf] + near[1, leaf] + near[2, leaf] + far[:, : 2 * RHS] + far[:, 2 * RHS :]
        known = rows[span, :]
        both = jnp.where(is_whole, RIDGE * known + field, known - field)
        correction = nn(inverse[leaf], both.astype(BF16))
        rows[span, :] = jnp.where(is_whole, both, correction)

    def put(step, carry):
        first = pl.multiple_of(step * 16, 16)
        for offset in range(16):
            moved[pl.ds(order[first + offset], 1), :] = rows[pl.ds(first + offset, 1), :]
        return carry

    lax.fori_loop(0, POINTS // 16, put, 0)
    for leaf in range(LEAVES):
        span = slice(leaf * LEAF, (leaf + 1) * LEAF)
        turned = moved[span, :].T
        product[:, span] = turned[:RHS].astype(BF16)
        update[:, span] = turned[RHS:].astype(BF16)


VM = pl.BlockSpec(memory_space=pltpu.VMEM)
SM = pl.BlockSpec(memory_space=pltpu.SMEM)
HB = pl.BlockSpec(memory_space=pltpu.HBM)
DMA = pltpu.SemaphoreType.DMA
TOTAL = (LEAVES + 1, LEAF, 2 * RHS)
TARGET = (LEAVES + 1, LEAF, FEATURES)
LEVEL = (RHS, RANK)


def call(kernel, name, inputs, outputs, scratch, flops=None):
    cost = None
    if flops is not None:
        cost = pl.CostEstimate(flops=flops, bytes_accessed=10**6, transcendentals=0)
    return pl.pallas_call(
        kernel,
        out_shape=tuple(jax.ShapeDtypeStruct(dims, kind) for _, dims, kind in outputs),
        in_specs=[spec for spec, _ in inputs],
        out_specs=tuple(spec for spec, _, _ in outputs),
        scratch_shapes=scratch,
        compiler_params=pltpu.CompilerParams(vmem_limit_bytes=VMEM_LIMIT),
        cost_estimate=cost,
        name=name,
    )(*[value for _, value in inputs])


def held(array):
    return pltpu.VMEM(array.shape, array.dtype)


def from_distance(value, distance):
    pairs = [((receiver + distance) % N_SUB, receiver) for receiver in range(N_SUB)]
    return lax.ppermute(value, "sub", pairs)


def per_device(
    coords, coefficients, targets, point_order, near_list, near_count, leaf_basis, leaf_inverse,
    local_transfer, local_couple, sub_transfer, sub_couple, top_transfer, top_couple,
):
    place = jnp.stack([lax.axis_index("leaf"), lax.axis_index("sub")]).astype(jnp.int32)
    point_rows = (POINTS, 2 * RHS)
    order_held = pltpu.SMEM(point_order.shape, jnp.int32)
    payload, skeleton, rows, terms = call(
        rise_kernel,
        "rise",
        [
            (HB, value)
            for value in (
                point_order, coefficients, targets, coords,
                leaf_basis, local_transfer, local_couple,
            )
        ],
        [
            (HB, (RHS, PAYLOAD), BF16),
            (VM, (RHS, 2 * RANK), BF16),
            (HB, point_rows, F32),
            (HB, (2 * LEAVES - 2, RHS, RANK), F32),
        ],
        [
            order_held, held(coefficients), held(targets), held(coords),
            pltpu.VMEM(point_rows, F32), held(leaf_basis), held(local_transfer), held(local_couple),
            pltpu.VMEM((RHS, PAYLOAD), BF16), pltpu.VMEM(point_rows, F32),
            pltpu.VMEM((2 * LEAVES - 2, RHS, RANK), F32), DMA((7,)), DMA((3,)),
        ],
    )
    pieces = [skeleton] + [from_distance(skeleton, distance) for distance in (1, 2, 3)]
    root, sub_terms, relay, ticket = call(
        sub_kernel,
        "sub_rise",
        [(SM, place)] + [(VM, piece) for piece in pieces]
        + [(HB, sub_transfer), (HB, sub_couple), (HB, payload)],
        [
            (VM, LEVEL, F32), (VM, (2,) + LEVEL, F32),
            (HB, payload.shape, BF16), (SM, (1,), jnp.int32),
        ],
        [pltpu.VMEM((N_SUB,) + LEVEL, F32), held(sub_transfer), held(sub_couple), DMA((3,))],
    )
    leaf_count = lax.axis_size("leaf")
    partner = lax.ppermute(root, "leaf", [(number, number ^ 1) for number in range(leaf_count)])
    right, left = from_distance(relay, 1), from_distance(relay, 3)
    tables = [
        pltpu.VMEM((GROUP, FEATURES, LEAF), BF16),
        pltpu.VMEM((GROUP, RHS, LEAF), BF16),
    ]
    near_0, target, relay, items, info = call(
        near_first_kernel,
        "near_first",
        [(SM, place), (SM, ticket), (SM, near_list.reshape(-1)), (SM, near_count), (HB, payload)],
        [
            (HB, TOTAL, F32), (HB, TARGET, BF16), (HB, payload.shape, BF16),
            (SM, (3 * ITEMS,), jnp.int32), (SM, (2,), jnp.int32),
        ],
        tables + [held(payload), pltpu.VMEM(TOTAL, F32), pltpu.VMEM(TARGET, BF16), DMA((1,)), DMA((3,))],
        FIRST_FLOPS,
    )
    pair_root, pair_term = call(
        pair_kernel,
        "pair_rise",
        [
            (SM, place), (SM, info), (VM, root), (VM, partner),
            (HB, top_transfer), (HB, top_couple),
        ],
        [(VM, LEVEL, F32), (VM, LEVEL, F32)],
        [pltpu.VMEM((2 * RANK, RANK), BF16), pltpu.VMEM((RANK, RANK), BF16), DMA((2,))],
    )
    same_side = [[side + 2 * pair for pair in range(leaf_count // 2)] for side in range(2)]
    gathered = lax.all_gather(pair_root, "leaf", axis_index_groups=same_side)
    across = from_distance(relay, 2)

    def later(segment, distances, payloads, before):
        return call(
            functools.partial(near_later_kernel, segment, distances),
            "near_beside" if segment == 1 else "near_across",
            [(SM, place), (SM, items), (SM, info), (SM, before), (HB, target)]
            + [(HB, value) for value in payloads],
            [(HB, TOTAL, F32), (SM, (1,), jnp.int32)],
            tables
            + [
                pltpu.VMEM(TOTAL, F32), pltpu.VMEM(TARGET, BF16),
                pltpu.VMEM((len(payloads), RHS, PAYLOAD), BF16),
                DMA((len(payloads) + 1,)), DMA((1,)),
            ],
            LATER_FLOPS,
        )

    near_1, done = later(1, (0, 1, 3), (payload, right, left), ticket)
    near_2, _ = later(2, (2,), (across,), done)
    return call(
        fall_kernel,
        "fall",
        [(SM, place)]
        + [
            (HB, value)
            for value in (
                point_order, gathered, top_transfer, top_couple, pair_term, sub_terms, terms,
                sub_transfer, local_transfer, leaf_basis, leaf_inverse, near_0, near_1, near_2, rows,
            )
        ],
        [(VM, (RHS, POINTS), BF16), (VM, (RHS, POINTS), BF16)],
        [
            order_held, pltpu.VMEM((30,) + LEVEL, F32),
            pltpu.VMEM((14, 2 * RANK, RANK), BF16), pltpu.VMEM((2 * RANK, RANK), BF16),
            pltpu.VMEM((TOP_BITS, RANK, RANK), BF16), pltpu.VMEM(LEVEL, F32),
            pltpu.VMEM((2,) + LEVEL, F32), pltpu.VMEM((2 * LEAVES - 2,) + LEVEL, F32),
            held(sub_transfer), held(local_transfer), held(leaf_basis), held(leaf_inverse),
            pltpu.VMEM((3,) + TOTAL, F32), pltpu.VMEM(point_rows, F32), pltpu.VMEM(point_rows, F32),
            DMA((16,)), DMA((TOP_BITS - 1,)),
        ],
    )


def solution(mesh):
    both = ("leaf", "sub")
    in_specs = (
        P(None, both), P(None, both), P(None, both), P(both), P(both, None), P(both),
        P(both, None, None), P(both, None, None), P(both, None, None), P(both, None, None),
        P("leaf", None, None), P("leaf", None, None), P(), P(),
    )
    return jax.shard_map(
        per_device,
        mesh=mesh,
        in_specs=in_specs,
        out_specs=(P(None, both), P(None, both)),
        check_vma=False,
    )
```

```python
import functools

import jax
import jax.numpy as jnp
from jax import lax
from jax.experimental import pallas as pl
from jax.experimental.pallas import tpu as pltpu
from jax.sharding import PartitionSpec as P

RIDGE = 0.5
SHARPNESS = 0.25
LOG2E = 1.4426950408889634
F32 = jnp.float32
BF16 = jnp.bfloat16

RHS = 64
DIMS = 8
LEAF = 512
RANK = 256
SLOTS = 24
LEAVES = 8
POINTS = LEAVES * LEAF
GROUP = 32
N_SUB = 4
PAYLOAD = POINTS + LEAF
FEATURES = 32
UNROLL = 8
ITEMS = LEAVES * SLOTS + 2 * UNROLL
FIRST_GROUPS = 3
TOP_BITS = 5
TOP_START = (0, 16, 24, 28, 30)
PAIRS = 16
LEVEL_START = (None, 0, 16, 24, 28)
VMEM_LIMIT = 56 * 2**20
FIRST_FLOPS = 10**10
LATER_FLOPS = 10**11


def nn(left, right):
    return jnp.dot(left, right, preferred_element_type=F32)


def nt(left, right):
    return lax.dot_general(left, right, (((1,), (1,)), ((), ())), preferred_element_type=F32)


def halves(value):
    high = value.astype(BF16)
    return high, (value - high.astype(F32)).astype(BF16)


def stacked(value):
    return jnp.concatenate(halves(value), axis=0)


def fold(value):
    rows = value.shape[0] // 2
    return value[:rows] + value[rows:]


def nn2(value, matrix):
    return fold(nn(stacked(value), matrix))


def nt2(value, matrix):
    return fold(nt(stacked(value), matrix))


def thirds(value):
    high = value.astype(BF16).astype(F32)
    rest = value - high
    middle = rest.astype(BF16).astype(F32)
    return high, middle, rest - middle


def square_rows(points, first):
    high, middle, low = thirds(
        jnp.sum(points * points, axis=0, keepdims=True) * (-SHARPNESS * LOG2E)
    )
    row = lax.broadcasted_iota(jnp.int32, points.shape, 0) - first
    parts = jnp.where(row == 0, high, jnp.where(row == 1, middle, low))
    ones = ((row + first >= 0) & (row + first < 6)).astype(F32)
    return jnp.where((row >= 0) & (row < 3), parts, ones)


def source_features(points):
    return jnp.concatenate([points, points, points, square_rows(points, 0)], axis=0).astype(BF16)


def target_features(points):
    high, middle, low = thirds(points * (2.0 * SHARPNESS * LOG2E))
    return jnp.concatenate([high, middle, low, square_rows(points, 3)], axis=0)


def leaf_points(payload, leaf):
    start = 16 * (leaf // 2)
    pair = payload[start : start + 16, POINTS:].astype(F32)
    return pair[DIMS * (leaf % 2) : DIMS * (leaf % 2) + DIMS]


def start_all(moves, arrived):
    copies = [
        pltpu.make_async_copy(source, target, arrived.at[number])
        for number, (source, target) in enumerate(moves)
    ]
    for copy in copies:
        copy.start()
    return copies


def wait_all(copies):
    for copy in copies:
        copy.wait()


def rise_kernel(
    order_hbm, coefficients_hbm, targets_hbm, coords_hbm, basis_hbm, transfer_hbm, couple_hbm,
    payload_hbm, skeleton, rows_hbm, terms_hbm,
    order, coefficients, targets, coords, columns, basis, transfer, couple,
    payload, rows, terms, arrived, left,
):
    copies = start_all(
        (
            (coefficients_hbm, coefficients),
            (targets_hbm, targets),
            (order_hbm, order),
            (basis_hbm, basis),
            (transfer_hbm, transfer),
            (couple_hbm, couple),
            (coords_hbm, coords),
        ),
        arrived,
    )
    wait_all(copies[:2])
    for leaf in range(LEAVES):
        span = slice(leaf * LEAF, (leaf + 1) * LEAF)
        values = coefficients[:, span].astype(F32)
        wanted = targets[:, span].astype(F32) - RIDGE * values
        columns[span, :] = jnp.concatenate([values, wanted], axis=0).T
    copies[2].wait()

    def pick(step, carry):
        first = pl.multiple_of(step * 16, 16)
        for offset in range(16):
            rows[pl.ds(first + offset, 1), :] = columns[pl.ds(order[first + offset], 1), :]
        return carry

    lax.fori_loop(0, POINTS // 16, pick, 0)
    sent = [pltpu.make_async_copy(rows, rows_hbm, left.at[0])]
    sent[0].start()
    copies[3].wait()
    coefs = []
    for leaf in range(LEAVES):
        span = slice(leaf * LEAF, (leaf + 1) * LEAF)
        values = rows[span, :].T[:RHS].astype(BF16)
        payload[:, span] = values
        coefs.append(nn(values, basis[leaf]))
    copies[6].wait()
    for pair in range(LEAVES // 2):
        both = [coords[:, leaf * LEAF : (leaf + 1) * LEAF].astype(F32) for leaf in (2 * pair, 2 * pair + 1)]
        payload[16 * pair : 16 * pair + 16, POINTS:] = jnp.concatenate(both, axis=0).astype(BF16)
    sent.append(pltpu.make_async_copy(payload, payload_hbm, left.at[1]))
    sent[1].start()
    wait_all(copies[4:6])
    node = 0
    term = 0
    while len(coefs) > 1:
        parents = []
        for left_child in range(0, len(coefs), 2):
            one, two = coefs[left_child], coefs[left_child + 1]
            terms[term + left_child] = nt2(two, couple[node])
            terms[term + left_child + 1] = nn2(one, couple[node])
            parents.append(nn2(jnp.concatenate([one, two], axis=1), transfer[node]))
            node += 1
        term += len(coefs)
        coefs = parents
    sent.append(pltpu.make_async_copy(terms, terms_hbm, left.at[2]))
    sent[2].start()
    high, low = halves(coefs[0])
    skeleton[:, :RANK] = high
    skeleton[:, RANK:] = low
    wait_all(sent)


def near_step(item, target, source, values, total):
    leaf = lax.shift_right_logical(item, 5)
    other = lax.bitwise_and(item, 31)
    tile = jnp.exp2(nn(target[leaf], source[other])).astype(BF16)
    block = values[other]
    total[leaf] += nt(tile, jnp.concatenate([block, block], axis=0))


def near_prepare(payload, first, source, values):
    for leaf in range(LEAVES):
        source[first + leaf] = source_features(leaf_points(payload, leaf))
        values[first + leaf] = payload[:, leaf * LEAF : (leaf + 1) * LEAF]


def near_groups(items, first, groups, target, source, values, total):
    def group(step, carry):
        for offset in range(UNROLL):
            near_step(items[first + step * UNROLL + offset], target, source, values, total)
        return carry

    lax.fori_loop(0, groups, group, 0)


def near_pairs(items, first, pairs, target, source, values, total):
    def pair(step, carry):
        for offset in range(2):
            near_step(items[first + step * 2 + offset], target, source, values, total)
        return carry

    lax.fori_loop(0, pairs, pair, 0)


def near_first_kernel(
    place, ticket, near_list, near_count, payload_hbm,
    total_hbm, target_hbm, relay_hbm, items, info,
    source, values, payload, total, target, arrived, left,
):
    copies = start_all(((payload_hbm, payload),), arrived)
    me = place[1]
    zero = jnp.int32(0)
    counts = (zero, zero, zero)
    for leaf in range(LEAVES):

        def collect(slot, counts, leaf=leaf):
            local, beside, across = counts
            other = near_list[leaf * SLOTS + slot]
            distance = lax.bitwise_and(lax.shift_right_logical(other, 3) - me, 3)
            is_local = (distance == 0).astype(jnp.int32)
            is_across = (distance == 2).astype(jnp.int32)
            is_beside = 1 - is_local - is_across
            where = is_local * local + is_beside * (ITEMS + beside) + is_across * (2 * ITEMS + across)
            items[where] = leaf * GROUP + other
            return local + is_local, beside + is_beside, across + is_across

        counts = lax.fori_loop(0, near_count[leaf], collect, counts)
    local, beside, across = counts
    groups = jnp.minimum(local // UNROLL, FIRST_GROUPS)
    late = local - groups * UNROLL

    def append(slot, carry):
        items[ITEMS + beside + slot] = items[groups * UNROLL + slot]
        return carry

    lax.fori_loop(0, late, append, 0)
    items[ITEMS + beside + late] = LEAVES * GROUP + me * LEAVES
    items[2 * ITEMS + across] = LEAVES * GROUP + lax.bitwise_and(me + 2, 3) * LEAVES
    info[0] = beside + late
    info[1] = across
    total[...] = jnp.zeros_like(total)
    wait_all(copies)
    sent = [pltpu.make_async_copy(payload, relay_hbm, left.at[0])]
    sent[0].start()
    for leaf in range(LEAVES):
        target[leaf] = target_features(leaf_points(payload, leaf)).T.astype(BF16)
    target[LEAVES] = jnp.zeros_like(target[LEAVES])
    sent.append(pltpu.make_async_copy(target, target_hbm, left.at[1]))
    sent[1].start()
    near_prepare(payload, me * LEAVES, source, values)
    near_groups(items, 0, groups, target, source, values, total)
    sent.append(pltpu.make_async_copy(total, total_hbm, left.at[2]))
    sent[2].start()
    wait_all(sent)


def near_later_kernel(segment, distances, place, items, info, before, target_hbm, running_hbm, *refs):
    count = len(distances)
    payloads_hbm, total_hbm, ticket = refs[:count], refs[count], refs[count + 1]
    source, values, total, target, payloads, arrived, left = refs[count + 2 :]
    ticket[0] = segment
    copies = start_all(
        [(payload_hbm, payloads.at[number]) for number, payload_hbm in enumerate(payloads_hbm)]
        + [(target_hbm, target), (running_hbm, total)],
        arrived,
    )
    for number, distance in enumerate(distances):
        copies[number].wait()
        where = lax.bitwise_and(place[1] + distance, 3)
        near_prepare(payloads.at[number], where * LEAVES, source, values)
    wait_all(copies[count:])
    used = info[segment - 1]
    groups = used // UNROLL
    first = segment * ITEMS
    near_groups(items, first, groups, target, source, values, total)
    near_pairs(
        items, first + groups * UNROLL, (used - groups * UNROLL + 1) // 2,
        target, source, values, total,
    )
    wait_all(start_all(((total, total_hbm),), left))


def sub_kernel(
    place, own, right, across, left, transfer_hbm, couple_hbm, payload_hbm,
    root, terms, relay_hbm, ticket,
    coefs, transfer, couple, payload, arrived, left_here,
):
    copies = start_all(
        ((transfer_hbm, transfer), (couple_hbm, couple), (payload_hbm, payload)), arrived
    )
    me = place[1]
    ticket[0] = me
    for distance, pair in enumerate((own, right, across, left)):
        value = pair[:, :RANK].astype(F32) + pair[:, RANK:].astype(F32)
        coefs[lax.bitwise_and(me + distance, 3)] = value
    wait_all(copies)
    sent = start_all(((payload, relay_hbm),), left_here)
    lower = nn2(jnp.concatenate([coefs[0], coefs[1]], axis=1), transfer[0])
    upper = nn2(jnp.concatenate([coefs[2], coefs[3]], axis=1), transfer[1])
    root[...] = nn2(jnp.concatenate([lower, upper], axis=1), transfer[2])
    half = lax.shift_right_logical(me, 1)
    sibling = stacked(coefs[lax.bitwise_xor(me, 1)])
    matrix = couple[half]
    is_left = lax.bitwise_and(me, 1) == 0
    terms[0] = fold(jnp.where(is_left, nt(sibling, matrix), nn(sibling, matrix)))
    terms[1] = jnp.where(half == 0, nt2(upper, couple[2]), nn2(lower, couple[2]))
    wait_all(sent)


def pair_kernel(
    place, info, own, partner, transfer_hbm, couple_hbm,
    root, term,
    transfer, couple, arrived,
):
    node = lax.shift_right_logical(place[0], 1)
    is_left = lax.bitwise_and(place[0], 1) == 0
    copies = start_all(
        ((transfer_hbm.at[node], transfer), (couple_hbm.at[node], couple)), arrived
    )
    one = jnp.where(is_left, own[...], partner[...])
    two = jnp.where(is_left, partner[...], own[...])
    wait_all(copies)
    root[...] = nn2(jnp.concatenate([one, two], axis=1), transfer[...])
    sibling = stacked(partner[...])
    term[...] = fold(jnp.where(is_left, nt(sibling, couple[...]), nn(sibling, couple[...])))


def fall_kernel(
    place, order_hbm, gathered_hbm, top_transfer_hbm, top_couple_hbm, pair_term_hbm,
    sub_terms_hbm, terms_hbm, sub_transfer_hbm, transfer_hbm, basis_hbm, inverse_hbm,
    near_hbm, known_hbm,
    product, update,
    order, level, top_transfer, pair_transfer, top_couple, pair_term,
    sub_terms, terms, sub_transfer, transfer, basis, inverse,
    near, rows, moved, arrived, couple_arrived,
):
    leaf_place = place[0]
    me = place[1]
    copies = start_all(
        (
            (gathered_hbm, level.at[pl.ds(0, PAIRS)]),
            (top_transfer_hbm.at[pl.ds(TOP_START[1], 8)], top_transfer.at[pl.ds(0, 8)]),
            (top_transfer_hbm.at[pl.ds(TOP_START[2], 6)], top_transfer.at[pl.ds(8, 6)]),
        ),
        arrived,
    )
    couples = start_all(
        [
            (
                top_couple_hbm.at[TOP_START[bit] + lax.shift_right_logical(leaf_place, bit + 1)],
                top_couple.at[bit],
            )
            for bit in range(1, TOP_BITS)
        ],
        couple_arrived,
    )
    later = start_all(
        (
            (top_transfer_hbm.at[lax.shift_right_logical(leaf_place, 1)], pair_transfer),
            (pair_term_hbm, pair_term),
            (sub_terms_hbm, sub_terms),
            (sub_transfer_hbm, sub_transfer),
            (terms_hbm, terms),
            (transfer_hbm, transfer),
        ),
        arrived.at[pl.ds(3, 6)],
    )
    last = start_all(
        (
            (basis_hbm, basis),
            (near_hbm, near),
            (known_hbm, rows),
            (inverse_hbm, inverse),
            (order_hbm, order),
        ),
        arrived.at[pl.ds(9, 5)],
    )
    copies[0].wait()
    for height in range(1, TOP_BITS - 1):
        below = LEVEL_START[height]
        here = LEVEL_START[height + 1]
        if height < 3:
            copies[height].wait()
        for node in range(PAIRS >> height):
            joined = jnp.concatenate([level[below + 2 * node], level[below + 2 * node + 1]], axis=1)
            level[here + node] = nn2(joined, top_transfer[TOP_START[height] - PAIRS + node])
    wait_all(couples)
    downward = None
    for bit in range(TOP_BITS - 1, 0, -1):
        child = lax.shift_right_logical(leaf_place, bit)
        side = lax.bitwise_and(child, 1)
        sibling = stacked(level[LEVEL_START[bit] + lax.bitwise_xor(child, 1)])
        matrix = top_couple[bit]
        term = fold(jnp.where(side == 0, nt(sibling, matrix), nn(sibling, matrix)))
        if downward is None:
            downward = term
        else:
            position = TOP_START[bit] - PAIRS + lax.shift_right_logical(leaf_place, bit + 1)
            part = top_transfer[position, pl.ds(pl.multiple_of(side * RANK, RANK), RANK), :]
            downward = term + nt2(downward, part)
    wait_all(later)
    side = lax.bitwise_and(leaf_place, 1)
    part = pair_transfer[pl.ds(pl.multiple_of(side * RANK, RANK), RANK), :]
    downward = pair_term[...] + nt2(downward, part)
    half = lax.shift_right_logical(me, 1)
    part = sub_transfer[2, pl.ds(pl.multiple_of(half * RANK, RANK), RANK), :]
    downward = sub_terms[1] + nt2(downward, part)
    side = lax.bitwise_and(me, 1)
    part = sub_transfer[half, pl.ds(pl.multiple_of(side * RANK, RANK), RANK), :]
    downward = sub_terms[0] + nt2(downward, part)
    nodes = [downward]
    node_start = LEAVES - 1
    term_start = 2 * LEAVES - 2
    while len(nodes) < LEAVES:
        node_start -= len(nodes)
        term_start -= 2 * len(nodes)
        children = []
        for number, value in enumerate(nodes):
            lowered = nt2(value, transfer[node_start + number])
            children.append(terms[term_start + 2 * number] + lowered[:, :RANK])
            children.append(terms[term_start + 2 * number + 1] + lowered[:, RANK:])
        nodes = children
    wait_all(last)
    lane = lax.broadcasted_iota(jnp.int32, (LEAF, 2 * RHS), 1)
    is_whole = lane < RHS
    for leaf in range(LEAVES):
        span = slice(leaf * LEAF, (leaf + 1) * LEAF)
        high, low = halves(nodes[leaf])
        far = nt(basis[leaf], jnp.concatenate([high, high, low, low], axis=0))
        field = near[leaf] + far[:, : 2 * RHS] + far[:, 2 * RHS :]
        known = rows[span, :]
        both = jnp.where(is_whole, RIDGE * known + field, known - field)
        correction = nn(inverse[leaf], both.astype(BF16))
        rows[span, :] = jnp.where(is_whole, both, correction)

    def put(step, carry):
        first = pl.multiple_of(step * 16, 16)
        for offset in range(16):
            moved[pl.ds(order[first + offset], 1), :] = rows[pl.ds(first + offset, 1), :]
        return carry

    lax.fori_loop(0, POINTS // 16, put, 0)
    for leaf in range(LEAVES):
        span = slice(leaf * LEAF, (leaf + 1) * LEAF)
        turned = moved[span, :].T
        product[:, span] = turned[:RHS].astype(BF16)
        update[:, span] = turned[RHS:].astype(BF16)


VM = pl.BlockSpec(memory_space=pltpu.VMEM)
SM = pl.BlockSpec(memory_space=pltpu.SMEM)
HB = pl.BlockSpec(memory_space=pltpu.HBM)
DMA = pltpu.SemaphoreType.DMA
TOTAL = (LEAVES + 1, LEAF, 2 * RHS)
TARGET = (LEAVES + 1, LEAF, FEATURES)
LEVEL = (RHS, RANK)


def call(kernel, name, inputs, outputs, scratch, flops=None):
    cost = None
    if flops is not None:
        cost = pl.CostEstimate(flops=flops, bytes_accessed=10**6, transcendentals=0)
    return pl.pallas_call(
        kernel,
        out_shape=tuple(jax.ShapeDtypeStruct(dims, kind) for _, dims, kind in outputs),
        in_specs=[spec for spec, _ in inputs],
        out_specs=tuple(spec for spec, _, _ in outputs),
        scratch_shapes=scratch,
        compiler_params=pltpu.CompilerParams(vmem_limit_bytes=VMEM_LIMIT),
        cost_estimate=cost,
        name=name,
    )(*[value for _, value in inputs])


def held(array):
    return pltpu.VMEM(array.shape, array.dtype)


def from_distance(value, distance):
    pairs = [((receiver + distance) % N_SUB, receiver) for receiver in range(N_SUB)]
    return lax.ppermute(value, "sub", pairs)


def per_device(
    coords, coefficients, targets, point_order, near_list, near_count, leaf_basis, leaf_inverse,
    local_transfer, local_couple, sub_transfer, sub_couple, top_transfer, top_couple,
):
    place = jnp.stack([lax.axis_index("leaf"), lax.axis_index("sub")]).astype(jnp.int32)
    point_rows = (POINTS, 2 * RHS)
    order_held = pltpu.SMEM(point_order.shape, jnp.int32)
    payload, skeleton, rows, terms = call(
        rise_kernel,
        "rise",
        [
            (HB, value)
            for value in (
                point_order, coefficients, targets, coords,
                leaf_basis, local_transfer, local_couple,
            )
        ],
        [
            (HB, (RHS, PAYLOAD), BF16),
            (VM, (RHS, 2 * RANK), BF16),
            (HB, point_rows, F32),
            (HB, (2 * LEAVES - 2, RHS, RANK), F32),
        ],
        [
            order_held, held(coefficients), held(targets), held(coords),
            pltpu.VMEM(point_rows, F32), held(leaf_basis), held(local_transfer), held(local_couple),
            pltpu.VMEM((RHS, PAYLOAD), BF16), pltpu.VMEM(point_rows, F32),
            pltpu.VMEM((2 * LEAVES - 2, RHS, RANK), F32), DMA((7,)), DMA((3,)),
        ],
    )
    pieces = [skeleton] + [from_distance(skeleton, distance) for distance in (1, 2, 3)]
    root, sub_terms, relay, ticket = call(
        sub_kernel,
        "sub_rise",
        [(SM, place)] + [(VM, piece) for piece in pieces]
        + [(HB, sub_transfer), (HB, sub_couple), (HB, payload)],
        [
            (VM, LEVEL, F32), (VM, (2,) + LEVEL, F32),
            (HB, payload.shape, BF16), (SM, (1,), jnp.int32),
        ],
        [pltpu.VMEM((N_SUB,) + LEVEL, F32), held(sub_transfer), held(sub_couple), held(payload), DMA((3,)), DMA((1,))],
    )
    leaf_count = lax.axis_size("leaf")
    partner = lax.ppermute(root, "leaf", [(number, number ^ 1) for number in range(leaf_count)])
    right, left = from_distance(relay, 1), from_distance(relay, 3)
    tables = [
        pltpu.VMEM((GROUP, FEATURES, LEAF), BF16),
        pltpu.VMEM((GROUP, RHS, LEAF), BF16),
    ]
    near, target, relay, items, info = call(
        near_first_kernel,
        "near_first",
        [(SM, place), (SM, ticket), (SM, near_list.reshape(-1)), (SM, near_count), (HB, payload)],
        [
            (HB, TOTAL, F32), (HB, TARGET, BF16), (HB, payload.shape, BF16),
            (SM, (3 * ITEMS,), jnp.int32), (SM, (2,), jnp.int32),
        ],
        tables + [held(payload), pltpu.VMEM(TOTAL, F32), pltpu.VMEM(TARGET, BF16), DMA((1,)), DMA((3,))],
        FIRST_FLOPS,
    )
    pair_root, pair_term = call(
        pair_kernel,
        "pair_rise",
        [
            (SM, place), (SM, info), (VM, root), (VM, partner),
            (HB, top_transfer), (HB, top_couple),
        ],
        [(VM, LEVEL, F32), (VM, LEVEL, F32)],
        [pltpu.VMEM((2 * RANK, RANK), BF16), pltpu.VMEM((RANK, RANK), BF16), DMA((2,))],
    )
    same_side = [[side + 2 * pair for pair in range(leaf_count // 2)] for side in range(2)]
    gathered = lax.all_gather(pair_root, "leaf", axis_index_groups=same_side)
    across = from_distance(relay, 2)

    def later(segment, distances, payloads, before, running):
        return call(
            functools.partial(near_later_kernel, segment, distances),
            "near_beside" if segment == 1 else "near_across",
            [(SM, place), (SM, items), (SM, info), (SM, before), (HB, target), (HB, running)]
            + [(HB, value) for value in payloads],
            [(HB, TOTAL, F32), (SM, (1,), jnp.int32)],
            tables
            + [
                pltpu.VMEM(TOTAL, F32), pltpu.VMEM(TARGET, BF16),
                pltpu.VMEM((len(payloads), RHS, PAYLOAD), BF16),
                DMA((len(payloads) + 2,)), DMA((1,)),
            ],
            LATER_FLOPS,
        )

    near, done = later(1, (0, 1, 3), (payload, right, left), ticket, near)
    near, _ = later(2, (2,), (across,), done, near)
    return call(
        fall_kernel,
        "fall",
        [(SM, place)]
        + [
            (HB, value)
            for value in (
                point_order, gathered, top_transfer, top_couple, pair_term, sub_terms, terms,
                sub_transfer, local_transfer, leaf_basis, leaf_inverse, near, rows,
            )
        ],
        [(VM, (RHS, POINTS), BF16), (VM, (RHS, POINTS), BF16)],
        [
            order_held, pltpu.VMEM((30,) + LEVEL, F32),
            pltpu.VMEM((14, 2 * RANK, RANK), BF16), pltpu.VMEM((2 * RANK, RANK), BF16),
            pltpu.VMEM((TOP_BITS, RANK, RANK), BF16), pltpu.VMEM(LEVEL, F32),
            pltpu.VMEM((2,) + LEVEL, F32), pltpu.VMEM((2 * LEAVES - 2,) + LEVEL, F32),
            held(sub_transfer), held(local_transfer), held(leaf_basis), held(leaf_inverse),
            pltpu.VMEM(TOTAL, F32), pltpu.VMEM(point_rows, F32), pltpu.VMEM(point_rows, F32),
            DMA((14,)), DMA((TOP_BITS - 1,)),
        ],
    )


def solution(mesh):
    both = ("leaf", "sub")
    in_specs = (
        P(None, both), P(None, both), P(None, both), P(both), P(both, None), P(both),
        P(both, None, None), P(both, None, None), P(both, None, None), P(both, None, None),
        P("leaf", None, None), P("leaf", None, None), P(), P(),
    )
    return jax.shard_map(
        per_device,
        mesh=mesh,
        in_specs=in_specs,
        out_specs=(P(None, both), P(None, both)),
        check_vma=False,
    )
```

```python
import functools

import jax
import jax.numpy as jnp
from jax import lax
from jax.experimental import pallas as pl
from jax.experimental.pallas import tpu as pltpu
from jax.sharding import PartitionSpec as P

RIDGE = 0.5
SHARPNESS = 0.25
LOG2E = 1.4426950408889634
F32 = jnp.float32
BF16 = jnp.bfloat16

RHS = 64
DIMS = 8
LEAF = 512
RANK = 256
SLOTS = 24
LEAVES = 8
POINTS = LEAVES * LEAF
GROUP = 32
N_SUB = 4
PAYLOAD = POINTS + LEAF
FEATURES = 32
UNROLL = 8
ITEMS = LEAVES * SLOTS + 2 * UNROLL
FIRST_GROUPS = 2
TOP_BITS = 5
TOP_START = (0, 16, 24, 28, 30)
PAIRS = 16
LEVEL_START = (None, 0, 16, 24, 28)
VMEM_LIMIT = 56 * 2**20
FIRST_FLOPS = 10**10
LATER_FLOPS = 10**11


def nn(left, right):
    return jnp.dot(left, right, preferred_element_type=F32)


def nt(left, right):
    return lax.dot_general(left, right, (((1,), (1,)), ((), ())), preferred_element_type=F32)


def halves(value):
    high = value.astype(BF16)
    return high, (value - high.astype(F32)).astype(BF16)


def stacked(value):
    return jnp.concatenate(halves(value), axis=0)


def fold(value):
    rows = value.shape[0] // 2
    return value[:rows] + value[rows:]


def nn2(value, matrix):
    return fold(nn(stacked(value), matrix))


def nt2(value, matrix):
    return fold(nt(stacked(value), matrix))


def thirds(value):
    high = value.astype(BF16).astype(F32)
    rest = value - high
    middle = rest.astype(BF16).astype(F32)
    return high, middle, rest - middle


def square_rows(points, first):
    high, middle, low = thirds(
        jnp.sum(points * points, axis=0, keepdims=True) * (-SHARPNESS * LOG2E)
    )
    row = lax.broadcasted_iota(jnp.int32, points.shape, 0) - first
    parts = jnp.where(row == 0, high, jnp.where(row == 1, middle, low))
    ones = ((row + first >= 0) & (row + first < 6)).astype(F32)
    return jnp.where((row >= 0) & (row < 3), parts, ones)


def source_features(points):
    return jnp.concatenate([points, points, points, square_rows(points, 0)], axis=0).astype(BF16)


def target_features(points):
    high, middle, low = thirds(points * (2.0 * SHARPNESS * LOG2E))
    return jnp.concatenate([high, middle, low, square_rows(points, 3)], axis=0)


def leaf_points(payload, leaf):
    start = 16 * (leaf // 2)
    pair = payload[start : start + 16, POINTS:].astype(F32)
    return pair[DIMS * (leaf % 2) : DIMS * (leaf % 2) + DIMS]


def start_all(moves, arrived):
    copies = [
        pltpu.make_async_copy(source, target, arrived.at[number])
        for number, (source, target) in enumerate(moves)
    ]
    for copy in copies:
        copy.start()
    return copies


def wait_all(copies):
    for copy in copies:
        copy.wait()


def rise_kernel(
    order_hbm, coefficients_hbm, targets_hbm, coords_hbm, basis_hbm, transfer_hbm, couple_hbm,
    payload_hbm, skeleton, rows_hbm, terms_hbm,
    order, coefficients, targets, coords, columns, basis, transfer, couple,
    payload, rows, terms, arrived, left,
):
    copies = start_all(
        (
            (coefficients_hbm, coefficients),
            (targets_hbm, targets),
            (order_hbm, order),
            (basis_hbm, basis),
            (transfer_hbm, transfer),
            (couple_hbm, couple),
            (coords_hbm, coords),
        ),
        arrived,
    )
    wait_all(copies[:2])
    for leaf in range(LEAVES):
        span = slice(leaf * LEAF, (leaf + 1) * LEAF)
        values = coefficients[:, span].astype(F32)
        wanted = targets[:, span].astype(F32) - RIDGE * values
        columns[span, :] = jnp.concatenate([values, wanted], axis=0).T
    copies[2].wait()

    def pick(step, carry):
        first = pl.multiple_of(step * 16, 16)
        for offset in range(16):
            rows[pl.ds(first + offset, 1), :] = columns[pl.ds(order[first + offset], 1), :]
        return carry

    lax.fori_loop(0, POINTS // 16, pick, 0)
    sent = [pltpu.make_async_copy(rows, rows_hbm, left.at[0])]
    sent[0].start()
    copies[3].wait()
    coefs = []
    for leaf in range(LEAVES):
        span = slice(leaf * LEAF, (leaf + 1) * LEAF)
        values = rows[span, :].T[:RHS].astype(BF16)
        payload[:, span] = values
        coefs.append(nn(values, basis[leaf]))
    copies[6].wait()
    for pair in range(LEAVES // 2):
        both = [coords[:, leaf * LEAF : (leaf + 1) * LEAF].astype(F32) for leaf in (2 * pair, 2 * pair + 1)]
        payload[16 * pair : 16 * pair + 16, POINTS:] = jnp.concatenate(both, axis=0).astype(BF16)
    sent.append(pltpu.make_async_copy(payload, payload_hbm, left.at[1]))
    sent[1].start()
    wait_all(copies[4:6])
    node = 0
    term = 0
    while len(coefs) > 1:
        parents = []
        for left_child in range(0, len(coefs), 2):
            one, two = coefs[left_child], coefs[left_child + 1]
            terms[term + left_child] = nt2(two, couple[node])
            terms[term + left_child + 1] = nn2(one, couple[node])
            parents.append(nn2(jnp.concatenate([one, two], axis=1), transfer[node]))
            node += 1
        term += len(coefs)
        coefs = parents
    sent.append(pltpu.make_async_copy(terms, terms_hbm, left.at[2]))
    sent[2].start()
    high, low = halves(coefs[0])
    skeleton[:, :RANK] = high
    skeleton[:, RANK:] = low
    wait_all(sent)


def near_step(item, target, source, values, total):
    leaf = lax.shift_right_logical(item, 5)
    other = lax.bitwise_and(item, 31)
    tile = jnp.exp2(nn(target[leaf], source[other])).astype(BF16)
    block = values[other]
    total[leaf] += nt(tile, jnp.concatenate([block, block], axis=0))


def near_prepare(payload, first, source, values):
    for leaf in range(LEAVES):
        source[first + leaf] = source_features(leaf_points(payload, leaf))
        values[first + leaf] = payload[:, leaf * LEAF : (leaf + 1) * LEAF]


def near_groups(items, first, groups, target, source, values, total):
    def group(step, carry):
        for offset in range(UNROLL):
            near_step(items[first + step * UNROLL + offset], target, source, values, total)
        return carry

    lax.fori_loop(0, groups, group, 0)


def near_pairs(items, first, pairs, target, source, values, total):
    def pair(step, carry):
        for offset in range(2):
            near_step(items[first + step * 2 + offset], target, source, values, total)
        return carry

    lax.fori_loop(0, pairs, pair, 0)


def near_first_kernel(
    ticket, near_list, near_count, payload_hbm,
    total_hbm, target_hbm, relay_hbm, items, info,
    source, values, payload, total, target, arrived, left,
):
    copies = start_all(((payload_hbm, payload),), arrived)
    me = lax.axis_index("sub")
    zero = jnp.int32(0)
    counts = (zero, zero, zero)
    for leaf in range(LEAVES):

        def collect(slot, counts, leaf=leaf):
            local, beside, across = counts
            other = near_list[leaf, slot]
            distance = lax.bitwise_and(lax.shift_right_logical(other, 3) - me, 3)
            is_local = (distance == 0).astype(jnp.int32)
            is_across = (distance == 2).astype(jnp.int32)
            is_beside = 1 - is_local - is_across
            where = is_local * local + is_beside * (ITEMS + beside) + is_across * (2 * ITEMS + across)
            items[where] = leaf * GROUP + other
            return local + is_local, beside + is_beside, across + is_across

        counts = lax.fori_loop(0, near_count[leaf], collect, counts)
    local, beside, across = counts
    groups = jnp.minimum(local // UNROLL, FIRST_GROUPS)
    late = local - groups * UNROLL

    def append(slot, carry):
        items[ITEMS + beside + slot] = items[groups * UNROLL + slot]
        return carry

    lax.fori_loop(0, late, append, 0)
    items[ITEMS + beside + late] = LEAVES * GROUP + me * LEAVES
    items[2 * ITEMS + across] = LEAVES * GROUP + lax.bitwise_and(me + 2, 3) * LEAVES
    info[0] = beside + late
    info[1] = across
    total[...] = jnp.zeros_like(total)
    wait_all(copies)
    sent = [pltpu.make_async_copy(payload, relay_hbm, left.at[0])]
    sent[0].start()
    for leaf in range(LEAVES):
        target[leaf] = target_features(leaf_points(payload, leaf)).T.astype(BF16)
    target[LEAVES] = jnp.zeros_like(target[LEAVES])
    sent.append(pltpu.make_async_copy(target, target_hbm, left.at[1]))
    sent[1].start()
    near_prepare(payload, me * LEAVES, source, values)
    near_groups(items, 0, groups, target, source, values, total)
    sent.append(pltpu.make_async_copy(total.at[pl.ds(0, LEAVES)], total_hbm, left.at[2]))
    sent[2].start()
    wait_all(sent)


def near_later_kernel(segment, distances, items, info, before, target_hbm, running_hbm, *refs):
    count = len(distances)
    payloads_hbm, total_hbm, ticket = refs[:count], refs[count], refs[count + 1]
    source, values, total, running, target, payloads, arrived, left = refs[count + 2 :]
    ticket[0] = segment
    copies = start_all(
        [(payload_hbm, payloads.at[number]) for number, payload_hbm in enumerate(payloads_hbm)]
        + [(target_hbm, target), (running_hbm, running)],
        arrived,
    )
    total[...] = jnp.zeros_like(total)
    for number, distance in enumerate(distances):
        copies[number].wait()
        where = lax.bitwise_and(lax.axis_index("sub") + distance, 3)
        near_prepare(payloads.at[number], where * LEAVES, source, values)
    copies[count].wait()
    used = info[segment - 1]
    groups = used // UNROLL
    first = segment * ITEMS
    near_groups(items, first, groups, target, source, values, total)
    near_pairs(
        items, first + groups * UNROLL, (used - groups * UNROLL + 1) // 2,
        target, source, values, total,
    )
    copies[count + 1].wait()
    sent = []
    for leaf in range(LEAVES):
        running[leaf] += total[leaf]
        sent.append(pltpu.make_async_copy(running.at[leaf], total_hbm.at[leaf], left.at[leaf]))
        sent[leaf].start()
    wait_all(sent)


def sub_kernel(
    own, right, across, left, transfer_hbm, couple_hbm, payload_hbm,
    root, terms, relay_hbm, ticket,
    coefs, transfer, couple, arrived,
):
    copies = start_all(((transfer_hbm, transfer), (couple_hbm, couple)), arrived)
    me = lax.axis_index("sub")
    ticket[0] = me
    for distance, pair in enumerate((own, right, across, left)):
        value = pair[:, :RANK].astype(F32) + pair[:, RANK:].astype(F32)
        coefs[lax.bitwise_and(me + distance, 3)] = value
    wait_all(copies)
    lower = nn2(jnp.concatenate([coefs[0], coefs[1]], axis=1), transfer[0])
    upper = nn2(jnp.concatenate([coefs[2], coefs[3]], axis=1), transfer[1])
    root[...] = nn2(jnp.concatenate([lower, upper], axis=1), transfer[2])
    half = lax.shift_right_logical(me, 1)
    sibling = stacked(coefs[lax.bitwise_xor(me, 1)])
    matrix = couple[half]
    is_left = lax.bitwise_and(me, 1) == 0
    terms[0] = fold(jnp.where(is_left, nt(sibling, matrix), nn(sibling, matrix)))
    terms[1] = jnp.where(half == 0, nt2(upper, couple[2]), nn2(lower, couple[2]))


def pair_kernel(
    info, own, partner, transfer_hbm, couple_hbm,
    root, term,
    transfer, couple, arrived,
):
    node = lax.shift_right_logical(lax.axis_index("leaf"), 1)
    is_left = lax.bitwise_and(lax.axis_index("leaf"), 1) == 0
    copies = start_all(
        ((transfer_hbm.at[node], transfer), (couple_hbm.at[node], couple)), arrived
    )
    one = jnp.where(is_left, own[...], partner[...])
    two = jnp.where(is_left, partner[...], own[...])
    wait_all(copies)
    root[...] = nn2(jnp.concatenate([one, two], axis=1), transfer[...])
    sibling = stacked(partner[...])
    term[...] = fold(jnp.where(is_left, nt(sibling, couple[...]), nn(sibling, couple[...])))


def fall_kernel(
    order_hbm, gathered_hbm, top_transfer_hbm, top_couple_hbm, pair_term_hbm,
    sub_terms_hbm, terms_hbm, sub_transfer_hbm, transfer_hbm, basis_hbm, inverse_hbm,
    near_hbm, known_hbm,
    product, update,
    order, level, top_transfer, pair_transfer, top_couple, pair_term,
    sub_terms, terms, sub_transfer, transfer, basis, inverse,
    near, rows, moved, arrived, couple_arrived, leaf_arrived,
):
    leaf_place = lax.axis_index("leaf")
    me = lax.axis_index("sub")
    copies = start_all(
        (
            (gathered_hbm, level.at[pl.ds(0, PAIRS)]),
            (top_transfer_hbm.at[pl.ds(TOP_START[1], 8)], top_transfer.at[pl.ds(0, 8)]),
            (top_transfer_hbm.at[pl.ds(TOP_START[2], 6)], top_transfer.at[pl.ds(8, 6)]),
        ),
        arrived,
    )
    couples = start_all(
        [
            (
                top_couple_hbm.at[TOP_START[bit] + lax.shift_right_logical(leaf_place, bit + 1)],
                top_couple.at[bit],
            )
            for bit in range(1, TOP_BITS)
        ],
        couple_arrived,
    )
    later = start_all(
        (
            (top_transfer_hbm.at[lax.shift_right_logical(leaf_place, 1)], pair_transfer),
            (pair_term_hbm, pair_term),
            (sub_terms_hbm, sub_terms),
            (sub_transfer_hbm, sub_transfer),
            (terms_hbm, terms),
            (transfer_hbm, transfer),
        ),
        arrived.at[pl.ds(3, 6)],
    )
    order_copy = start_all(((order_hbm, order),), arrived.at[pl.ds(9, 1)])
    last = []
    for leaf in range(LEAVES):
        span = pl.ds(leaf * LEAF, LEAF)
        last.append(
            start_all(
                (
                    (basis_hbm.at[leaf], basis.at[leaf]),
                    (near_hbm.at[leaf], near.at[leaf]),
                    (known_hbm.at[span], rows.at[span]),
                    (inverse_hbm.at[leaf], inverse.at[leaf]),
                ),
                leaf_arrived.at[leaf],
            )
        )
    copies[0].wait()
    for height in range(1, TOP_BITS - 1):
        below = LEVEL_START[height]
        here = LEVEL_START[height + 1]
        if height < 3:
            copies[height].wait()
        for node in range(PAIRS >> height):
            joined = jnp.concatenate([level[below + 2 * node], level[below + 2 * node + 1]], axis=1)
            level[here + node] = nn2(joined, top_transfer[TOP_START[height] - PAIRS + node])
    wait_all(couples)
    downward = None
    for bit in range(TOP_BITS - 1, 0, -1):
        child = lax.shift_right_logical(leaf_place, bit)
        side = lax.bitwise_and(child, 1)
        sibling = stacked(level[LEVEL_START[bit] + lax.bitwise_xor(child, 1)])
        matrix = top_couple[bit]
        term = fold(jnp.where(side == 0, nt(sibling, matrix), nn(sibling, matrix)))
        if downward is None:
            downward = term
        else:
            position = TOP_START[bit] - PAIRS + lax.shift_right_logical(leaf_place, bit + 1)
            part = top_transfer[position, pl.ds(pl.multiple_of(side * RANK, RANK), RANK), :]
            downward = term + nt2(downward, part)
    wait_all(later)
    side = lax.bitwise_and(leaf_place, 1)
    part = pair_transfer[pl.ds(pl.multiple_of(side * RANK, RANK), RANK), :]
    downward = pair_term[...] + nt2(downward, part)
    half = lax.shift_right_logical(me, 1)
    part = sub_transfer[2, pl.ds(pl.multiple_of(half * RANK, RANK), RANK), :]
    downward = sub_terms[1] + nt2(downward, part)
    side = lax.bitwise_and(me, 1)
    part = sub_transfer[half, pl.ds(pl.multiple_of(side * RANK, RANK), RANK), :]
    downward = sub_terms[0] + nt2(downward, part)
    nodes = [downward]
    node_start = LEAVES - 1
    term_start = 2 * LEAVES - 2
    while len(nodes) < LEAVES:
        node_start -= len(nodes)
        term_start -= 2 * len(nodes)
        children = []
        for number, value in enumerate(nodes):
            lowered = nt2(value, transfer[node_start + number])
            children.append(terms[term_start + 2 * number] + lowered[:, :RANK])
            children.append(terms[term_start + 2 * number + 1] + lowered[:, RANK:])
        nodes = children
    order_copy[0].wait()
    lane = lax.broadcasted_iota(jnp.int32, (LEAF, 2 * RHS), 1)
    is_whole = lane < RHS
    for leaf in range(LEAVES):
        span = slice(leaf * LEAF, (leaf + 1) * LEAF)
        high, low = halves(nodes[leaf])
        wait_all(last[leaf])
        far = nt(basis[leaf], jnp.concatenate([high, high, low, low], axis=0))
        field = near[leaf] + far[:, : 2 * RHS] + far[:, 2 * RHS :]
        known = rows[span, :]
        both = jnp.where(is_whole, RIDGE * known + field, known - field)
        correction = nn(inverse[leaf], both.astype(BF16))
        rows[span, :] = jnp.where(is_whole, both, correction)

        def put(step, carry, leaf=leaf):
            first = pl.multiple_of(leaf * LEAF + step * 16, 16)
            for offset in range(16):
                moved[pl.ds(order[first + offset], 1), :] = rows[pl.ds(first + offset, 1), :]
            return carry

        lax.fori_loop(0, LEAF // 16, put, 0)
    for leaf in range(LEAVES):
        span = slice(leaf * LEAF, (leaf + 1) * LEAF)
        turned = moved[span, :].T
        product[:, span] = turned[:RHS].astype(BF16)
        update[:, span] = turned[RHS:].astype(BF16)


VM = pl.BlockSpec(memory_space=pltpu.VMEM)
SM = pl.BlockSpec(memory_space=pltpu.SMEM)
HB = pl.BlockSpec(memory_space=pltpu.HBM)
DMA = pltpu.SemaphoreType.DMA
TOTAL = (LEAVES, LEAF, 2 * RHS)
PADDED_TOTAL = (LEAVES + 1, LEAF, 2 * RHS)
TARGET = (LEAVES + 1, LEAF, FEATURES)
LEVEL = (RHS, RANK)


def call(kernel, name, inputs, outputs, scratch, flops=None, aliases=None):
    cost = None
    if flops is not None:
        cost = pl.CostEstimate(flops=flops, bytes_accessed=10**6, transcendentals=0)
    return pl.pallas_call(
        kernel,
        out_shape=tuple(jax.ShapeDtypeStruct(dims, kind) for _, dims, kind in outputs),
        in_specs=[spec for spec, _ in inputs],
        out_specs=tuple(spec for spec, _, _ in outputs),
        scratch_shapes=scratch,
        compiler_params=pltpu.CompilerParams(vmem_limit_bytes=VMEM_LIMIT),
        cost_estimate=cost,
        input_output_aliases=aliases or {},
        name=name,
    )(*[value for _, value in inputs])


def held(array):
    return pltpu.VMEM(array.shape, array.dtype)


def from_distance(value, distance):
    pairs = [((receiver + distance) % N_SUB, receiver) for receiver in range(N_SUB)]
    return lax.ppermute(value, "sub", pairs)


def per_device(
    coords, coefficients, targets, point_order, near_list, near_count, leaf_basis, leaf_inverse,
    local_transfer, local_couple, sub_transfer, sub_couple, top_transfer, top_couple,
):
    point_rows = (POINTS, 2 * RHS)
    order_held = pltpu.SMEM(point_order.shape, jnp.int32)
    payload, skeleton, rows, terms = call(
        rise_kernel,
        "rise",
        [
            (HB, value)
            for value in (
                point_order, coefficients, targets, coords,
                leaf_basis, local_transfer, local_couple,
            )
        ],
        [
            (HB, (RHS, PAYLOAD), BF16),
            (VM, (RHS, 2 * RANK), BF16),
            (HB, point_rows, F32),
            (HB, (2 * LEAVES - 2, RHS, RANK), F32),
        ],
        [
            order_held, held(coefficients), held(targets), held(coords),
            pltpu.VMEM(point_rows, F32), held(leaf_basis), held(local_transfer), held(local_couple),
            pltpu.VMEM((RHS, PAYLOAD), BF16), pltpu.VMEM(point_rows, F32),
            pltpu.VMEM((2 * LEAVES - 2, RHS, RANK), F32), DMA((7,)), DMA((3,)),
        ],
    )
    pieces = [skeleton] + [from_distance(skeleton, distance) for distance in (1, 2, 3)]
    root, sub_terms, relay, ticket = call(
        sub_kernel,
        "sub_rise",
        [(VM, piece) for piece in pieces]
        + [(HB, sub_transfer), (HB, sub_couple), (HB, payload)],
        [
            (VM, LEVEL, F32), (VM, (2,) + LEVEL, F32),
            (HB, payload.shape, BF16), (SM, (1,), jnp.int32),
        ],
        [pltpu.VMEM((N_SUB,) + LEVEL, F32), held(sub_transfer), held(sub_couple), DMA((2,))],
        aliases={6: 2},
    )
    leaf_count = lax.axis_size("leaf")
    partner = lax.ppermute(root, "leaf", [(number, number ^ 1) for number in range(leaf_count)])
    right, left = from_distance(relay, 1), from_distance(relay, 3)
    tables = [
        pltpu.VMEM((GROUP, FEATURES, LEAF), BF16),
        pltpu.VMEM((GROUP, RHS, LEAF), BF16),
    ]
    near, target, relay, items, info = call(
        near_first_kernel,
        "near_first",
        [(SM, ticket), (SM, near_list), (SM, near_count), (HB, relay)],
        [
            (HB, TOTAL, F32), (HB, TARGET, BF16), (HB, payload.shape, BF16),
            (SM, (3 * ITEMS,), jnp.int32), (SM, (2,), jnp.int32),
        ],
        tables + [held(payload), pltpu.VMEM(PADDED_TOTAL, F32), pltpu.VMEM(TARGET, BF16), DMA((1,)), DMA((3,))],
        FIRST_FLOPS,
    )
    pair_root, pair_term = call(
        pair_kernel,
        "pair_rise",
        [
            (SM, info), (VM, root), (VM, partner),
            (HB, top_transfer), (HB, top_couple),
        ],
        [(VM, LEVEL, F32), (VM, LEVEL, F32)],
        [pltpu.VMEM((2 * RANK, RANK), BF16), pltpu.VMEM((RANK, RANK), BF16), DMA((2,))],
    )
    same_side = [[side + 2 * pair for pair in range(leaf_count // 2)] for side in range(2)]
    gathered = lax.all_gather(pair_root, "leaf", axis_index_groups=same_side)
    across = from_distance(relay, 2)

    def later(segment, distances, payloads, before, running):
        return call(
            functools.partial(near_later_kernel, segment, distances),
            "near_beside" if segment == 1 else "near_across",
            [(SM, items), (SM, info), (SM, before), (HB, target), (HB, running)]
            + [(HB, value) for value in payloads],
            [(HB, TOTAL, F32), (SM, (1,), jnp.int32)],
            tables
            + [
                pltpu.VMEM(PADDED_TOTAL, F32), pltpu.VMEM(TOTAL, F32), pltpu.VMEM(TARGET, BF16),
                pltpu.VMEM((len(payloads), RHS, PAYLOAD), BF16),
                DMA((len(payloads) + 2,)), DMA((LEAVES,)),
            ],
            LATER_FLOPS,
        )

    near, done = later(1, (0, 1, 3), (relay, right, left), ticket, near)
    near, _ = later(2, (2,), (across,), done, near)
    return call(
        fall_kernel,
        "fall",
        [
            (HB, value)
            for value in (
                point_order, gathered, top_transfer, top_couple, pair_term, sub_terms, terms,
                sub_transfer, local_transfer, leaf_basis, leaf_inverse, near, rows,
            )
        ],
        [(VM, (RHS, POINTS), BF16), (VM, (RHS, POINTS), BF16)],
        [
            order_held, pltpu.VMEM((30,) + LEVEL, F32),
            pltpu.VMEM((14, 2 * RANK, RANK), BF16), pltpu.VMEM((2 * RANK, RANK), BF16),
            pltpu.VMEM((TOP_BITS, RANK, RANK), BF16), pltpu.VMEM(LEVEL, F32),
            pltpu.VMEM((2,) + LEVEL, F32), pltpu.VMEM((2 * LEAVES - 2,) + LEVEL, F32),
            held(sub_transfer), held(local_transfer), held(leaf_basis), held(leaf_inverse),
            pltpu.VMEM(TOTAL, F32), pltpu.VMEM(point_rows, F32), pltpu.VMEM(point_rows, F32),
            DMA((10,)), DMA((TOP_BITS - 1,)), DMA((LEAVES, 4)),
        ],
    )


def solution(mesh):
    both = ("leaf", "sub")
    in_specs = (
        P(None, both), P(None, both), P(None, both), P(both), P(both, None), P(both),
        P(both, None, None), P(both, None, None), P(both, None, None), P(both, None, None),
        P("leaf", None, None), P("leaf", None, None), P(), P(),
    )
    return jax.shard_map(
        per_device,
        mesh=mesh,
        in_specs=in_specs,
        out_specs=(P(None, both), P(None, both)),
        check_vma=False,
    )
```

```python
import functools

import jax
import jax.numpy as jnp
from jax import lax
from jax.experimental import pallas as pl
from jax.experimental.pallas import tpu as pltpu
from jax.sharding import PartitionSpec as P

RIDGE = 0.5
SHARPNESS = 0.25
LOG2E = 1.4426950408889634
F32 = jnp.float32
BF16 = jnp.bfloat16

RHS = 64
DIMS = 8
LEAF = 512
RANK = 256
SLOTS = 24
LEAVES = 8
POINTS = LEAVES * LEAF
GROUP = 32
N_SUB = 4
PAYLOAD = POINTS + LEAF
FEATURES = 32
UNROLL = 8
ITEMS = LEAVES * SLOTS + 2 * UNROLL
TOP_BITS = 5
TOP_START = (0, 16, 24, 28, 30)
PAIRS = 16
LEVEL_START = (None, 0, 16, 24, 28)
VMEM_LIMIT = 56 * 2**20
FIRST_FLOPS = 10**10
LATER_FLOPS = 10**10


def nn(left, right):
    return jnp.dot(left, right, preferred_element_type=F32)


def nt(left, right):
    return lax.dot_general(left, right, (((1,), (1,)), ((), ())), preferred_element_type=F32)


def halves(value):
    high = value.astype(BF16)
    return high, (value - high.astype(F32)).astype(BF16)


def stacked(value):
    return jnp.concatenate(halves(value), axis=0)


def fold(value):
    rows = value.shape[0] // 2
    return value[:rows] + value[rows:]


def nn2(value, matrix):
    return fold(nn(stacked(value), matrix))


def nt2(value, matrix):
    return fold(nt(stacked(value), matrix))


def thirds(value):
    high = value.astype(BF16).astype(F32)
    rest = value - high
    middle = rest.astype(BF16).astype(F32)
    return high, middle, rest - middle


def square_rows(points, first):
    high, middle, low = thirds(
        jnp.sum(points * points, axis=0, keepdims=True) * (-SHARPNESS * LOG2E)
    )
    row = lax.broadcasted_iota(jnp.int32, points.shape, 0) - first
    parts = jnp.where(row == 0, high, jnp.where(row == 1, middle, low))
    ones = ((row + first >= 0) & (row + first < 6)).astype(F32)
    return jnp.where((row >= 0) & (row < 3), parts, ones)


def source_features(points):
    return jnp.concatenate([points, points, points, square_rows(points, 0)], axis=0).astype(BF16)


def target_features(points):
    high, middle, low = thirds(points * (2.0 * SHARPNESS * LOG2E))
    return jnp.concatenate([high, middle, low, square_rows(points, 3)], axis=0)


def leaf_points(payload, leaf):
    start = 16 * (leaf // 2)
    pair = payload[start : start + 16, POINTS:].astype(F32)
    return pair[DIMS * (leaf % 2) : DIMS * (leaf % 2) + DIMS]


def start_all(moves, arrived):
    copies = [
        pltpu.make_async_copy(source, target, arrived.at[number])
        for number, (source, target) in enumerate(moves)
    ]
    for copy in copies:
        copy.start()
    return copies


def wait_all(copies):
    for copy in copies:
        copy.wait()


def rise_kernel(
    order_hbm, coefficients_hbm, targets_hbm, coords_hbm, basis_hbm, transfer_hbm, couple_hbm,
    payload_hbm, skeleton, rows_hbm, terms_hbm,
    order, coefficients, targets, coords, columns, basis, transfer, couple,
    payload, rows, terms, arrived, left,
):
    copies = start_all(
        (
            (coefficients_hbm, coefficients),
            (targets_hbm, targets),
            (order_hbm, order),
            (basis_hbm, basis),
            (transfer_hbm, transfer),
            (couple_hbm, couple),
            (coords_hbm, coords),
        ),
        arrived,
    )
    wait_all(copies[:2])
    for leaf in range(LEAVES):
        span = slice(leaf * LEAF, (leaf + 1) * LEAF)
        values = coefficients[:, span].astype(F32)
        wanted = targets[:, span].astype(F32) - RIDGE * values
        columns[span, :] = jnp.concatenate([values, wanted], axis=0).T
    copies[2].wait()

    def pick(step, carry):
        first = pl.multiple_of(step * 16, 16)
        for offset in range(16):
            rows[pl.ds(first + offset, 1), :] = columns[pl.ds(order[first + offset], 1), :]
        return carry

    lax.fori_loop(0, POINTS // 16, pick, 0)
    sent = [pltpu.make_async_copy(rows, rows_hbm, left.at[0])]
    sent[0].start()
    copies[3].wait()
    coefs = []
    for leaf in range(LEAVES):
        span = slice(leaf * LEAF, (leaf + 1) * LEAF)
        values = rows[span, :].T[:RHS].astype(BF16)
        payload[:, span] = values
        coefs.append(nn(values, basis[leaf]))
    copies[6].wait()
    for pair in range(LEAVES // 2):
        both = [coords[:, leaf * LEAF : (leaf + 1) * LEAF].astype(F32) for leaf in (2 * pair, 2 * pair + 1)]
        payload[16 * pair : 16 * pair + 16, POINTS:] = jnp.concatenate(both, axis=0).astype(BF16)
    sent.append(pltpu.make_async_copy(payload, payload_hbm, left.at[1]))
    sent[1].start()
    wait_all(copies[4:6])
    node = 0
    term = 0
    while len(coefs) > 1:
        parents = []
        for left_child in range(0, len(coefs), 2):
            one, two = coefs[left_child], coefs[left_child + 1]
            terms[term + left_child] = nt2(two, couple[node])
            terms[term + left_child + 1] = nn2(one, couple[node])
            parents.append(nn2(jnp.concatenate([one, two], axis=1), transfer[node]))
            node += 1
        term += len(coefs)
        coefs = parents
    sent.append(pltpu.make_async_copy(terms, terms_hbm, left.at[2]))
    sent[2].start()
    high, low = halves(coefs[0])
    skeleton[:, :RANK] = high
    skeleton[:, RANK:] = low
    wait_all(sent)


def near_step(item, target, source, values, total):
    leaf = lax.shift_right_logical(item, 5)
    other = lax.bitwise_and(item, 31)
    tile = jnp.exp2(nn(target[leaf], source[other])).astype(BF16)
    block = values[other]
    total[leaf] += nt(tile, jnp.concatenate([block, block], axis=0))


def near_prepare(payload, first, source, values):
    for leaf in range(LEAVES):
        source[first + leaf] = source_features(leaf_points(payload, leaf))
        values[first + leaf] = payload[:, leaf * LEAF : (leaf + 1) * LEAF]


def near_groups(items, first, groups, target, source, values, total):
    def group(step, carry):
        for offset in range(UNROLL):
            near_step(items[first + step * UNROLL + offset], target, source, values, total)
        return carry

    lax.fori_loop(0, groups, group, 0)


def near_pairs(items, first, pairs, target, source, values, total):
    def pair(step, carry):
        for offset in range(2):
            near_step(items[first + step * 2 + offset], target, source, values, total)
        return carry

    lax.fori_loop(0, pairs, pair, 0)


def near_all(items, first, used, target, source, values, total):
    groups = used // UNROLL
    near_groups(items, first, groups, target, source, values, total)
    near_pairs(
        items, first + groups * UNROLL, (used - groups * UNROLL + 1) // 2,
        target, source, values, total,
    )


def near_first_kernel(
    ticket, near_list, near_count, payload_hbm,
    total_hbm, target_hbm, relay_hbm, items, info,
    source, values, payload, total, target, arrived, left,
):
    copies = start_all(((payload_hbm, payload),), arrived)
    me = lax.axis_index("sub")
    zero = jnp.int32(0)
    counts = (zero, zero, zero)
    for leaf in range(LEAVES):

        def collect(slot, counts, leaf=leaf):
            local, beside, across = counts
            other = near_list[leaf, slot]
            distance = lax.bitwise_and(lax.shift_right_logical(other, 3) - me, 3)
            is_local = (distance == 0).astype(jnp.int32)
            is_across = (distance == 2).astype(jnp.int32)
            is_beside = 1 - is_local - is_across
            where = is_local * local + is_beside * (ITEMS + beside) + is_across * (2 * ITEMS + across)
            items[where] = leaf * GROUP + other
            return local + is_local, beside + is_beside, across + is_across

        counts = lax.fori_loop(0, near_count[leaf], collect, counts)
    local, beside, across = counts
    items[local] = LEAVES * GROUP + me * LEAVES
    items[ITEMS + beside] = LEAVES * GROUP + lax.bitwise_and(me + 1, 3) * LEAVES
    items[2 * ITEMS + across] = LEAVES * GROUP + lax.bitwise_and(me + 2, 3) * LEAVES
    info[0] = beside
    info[1] = across
    total[...] = jnp.zeros_like(total)
    wait_all(copies)
    sent = [pltpu.make_async_copy(payload, relay_hbm, left.at[0])]
    sent[0].start()
    for leaf in range(LEAVES):
        target[leaf] = target_features(leaf_points(payload, leaf)).T.astype(BF16)
    target[LEAVES] = jnp.zeros_like(target[LEAVES])
    sent.append(pltpu.make_async_copy(target, target_hbm, left.at[1]))
    sent[1].start()
    near_prepare(payload, me * LEAVES, source, values)
    near_all(items, 0, local, target, source, values, total)
    sent.append(pltpu.make_async_copy(total.at[pl.ds(0, LEAVES)], total_hbm, left.at[2]))
    sent[2].start()
    wait_all(sent)


def near_beside_kernel(
    items, info, right_hbm, left_hbm, target_hbm, running_hbm,
    total_hbm, ticket,
    source, values, total, running, target, payloads, arrived, left,
):
    ticket[0] = info[0]
    copies = start_all(
        ((right_hbm, payloads.at[0]), (left_hbm, payloads.at[1]), (target_hbm, target)), arrived
    )
    total[...] = jnp.zeros_like(total)
    for number, distance in enumerate((1, 3)):
        copies[number].wait()
        where = lax.bitwise_and(lax.axis_index("sub") + distance, 3)
        near_prepare(payloads.at[number], where * LEAVES, source, values)
    copies[2].wait()
    copies = start_all(((running_hbm, running),), arrived.at[pl.ds(3, 1)])
    near_all(items, ITEMS, info[0], target, source, values, total)
    wait_all(copies)
    sent = []
    for leaf in range(LEAVES):
        running[leaf] += total[leaf]
        sent.append(pltpu.make_async_copy(running.at[leaf], total_hbm.at[leaf], left.at[leaf]))
        sent[leaf].start()
    wait_all(sent)


def sub_kernel(
    own, right, across, left, transfer_hbm, couple_hbm, payload_hbm,
    root, terms, relay_hbm, ticket,
    coefs, transfer, couple, arrived,
):
    copies = start_all(((transfer_hbm, transfer), (couple_hbm, couple)), arrived)
    me = lax.axis_index("sub")
    ticket[0] = me
    for distance, pair in enumerate((own, right, across, left)):
        value = pair[:, :RANK].astype(F32) + pair[:, RANK:].astype(F32)
        coefs[lax.bitwise_and(me + distance, 3)] = value
    wait_all(copies)
    lower = nn2(jnp.concatenate([coefs[0], coefs[1]], axis=1), transfer[0])
    upper = nn2(jnp.concatenate([coefs[2], coefs[3]], axis=1), transfer[1])
    root[...] = nn2(jnp.concatenate([lower, upper], axis=1), transfer[2])
    half = lax.shift_right_logical(me, 1)
    sibling = stacked(coefs[lax.bitwise_xor(me, 1)])
    matrix = couple[half]
    is_left = lax.bitwise_and(me, 1) == 0
    terms[0] = fold(jnp.where(is_left, nt(sibling, matrix), nn(sibling, matrix)))
    terms[1] = jnp.where(half == 0, nt2(upper, couple[2]), nn2(lower, couple[2]))


def pair_kernel(
    info, own, partner, transfer_hbm, couple_hbm,
    root, term, ticket,
    transfer, couple, arrived,
):
    ticket[0] = info[0]
    node = lax.shift_right_logical(lax.axis_index("leaf"), 1)
    is_left = lax.bitwise_and(lax.axis_index("leaf"), 1) == 0
    copies = start_all(
        ((transfer_hbm.at[node], transfer), (couple_hbm.at[node], couple)), arrived
    )
    one = jnp.where(is_left, own[...], partner[...])
    two = jnp.where(is_left, partner[...], own[...])
    wait_all(copies)
    root[...] = nn2(jnp.concatenate([one, two], axis=1), transfer[...])
    sibling = stacked(partner[...])
    term[...] = fold(jnp.where(is_left, nt(sibling, couple[...]), nn(sibling, couple[...])))


def near_fall_kernel(
    ticket, items, info, across_hbm, target_hbm,
    order_hbm, gathered_hbm, top_transfer_hbm, top_couple_hbm, pair_term_hbm,
    sub_terms_hbm, terms_hbm, sub_transfer_hbm, transfer_hbm, basis_hbm, inverse_hbm,
    near_hbm, known_hbm,
    product, update,
    source, values, total, target, payload, near_arrived,
    order, level, top_transfer, pair_transfer, top_couple, pair_term,
    sub_terms, terms, sub_transfer, transfer, basis, inverse,
    near, rows, moved, arrived, couple_arrived, leaf_arrived,
):
    first = start_all(((across_hbm, payload), (target_hbm, target)), near_arrived)
    total[...] = jnp.zeros_like(total)
    first[0].wait()
    across = lax.bitwise_and(lax.axis_index("sub") + 2, 3)
    near_prepare(payload, across * LEAVES, source, values)
    first[1].wait()
    leaf_place = lax.axis_index("leaf")
    me = lax.axis_index("sub")
    copies = start_all(
        (
            (gathered_hbm, level.at[pl.ds(0, PAIRS)]),
            (top_transfer_hbm.at[pl.ds(TOP_START[1], 8)], top_transfer.at[pl.ds(0, 8)]),
            (top_transfer_hbm.at[pl.ds(TOP_START[2], 6)], top_transfer.at[pl.ds(8, 6)]),
        ),
        arrived,
    )
    couples = start_all(
        [
            (
                top_couple_hbm.at[TOP_START[bit] + lax.shift_right_logical(leaf_place, bit + 1)],
                top_couple.at[bit],
            )
            for bit in range(1, TOP_BITS)
        ],
        couple_arrived,
    )
    later = start_all(
        (
            (top_transfer_hbm.at[lax.shift_right_logical(leaf_place, 1)], pair_transfer),
            (pair_term_hbm, pair_term),
            (sub_terms_hbm, sub_terms),
            (sub_transfer_hbm, sub_transfer),
            (terms_hbm, terms),
            (transfer_hbm, transfer),
        ),
        arrived.at[pl.ds(3, 6)],
    )
    last = start_all(
        (
            (order_hbm, order),
            (near_hbm, near),
            (known_hbm, rows),
            (basis_hbm, basis),
            (inverse_hbm, inverse),
        ),
        leaf_arrived,
    )
    near_all(items, 2 * ITEMS, info[1], target, source, values, total)
    copies[0].wait()
    for height in range(1, TOP_BITS - 1):
        below = LEVEL_START[height]
        here = LEVEL_START[height + 1]
        if height < 3:
            copies[height].wait()
        for node in range(PAIRS >> height):
            joined = jnp.concatenate([level[below + 2 * node], level[below + 2 * node + 1]], axis=1)
            level[here + node] = nn2(joined, top_transfer[TOP_START[height] - PAIRS + node])
    wait_all(couples)
    downward = None
    for bit in range(TOP_BITS - 1, 0, -1):
        child = lax.shift_right_logical(leaf_place, bit)
        side = lax.bitwise_and(child, 1)
        sibling = stacked(level[LEVEL_START[bit] + lax.bitwise_xor(child, 1)])
        matrix = top_couple[bit]
        term = fold(jnp.where(side == 0, nt(sibling, matrix), nn(sibling, matrix)))
        if downward is None:
            downward = term
        else:
            position = TOP_START[bit] - PAIRS + lax.shift_right_logical(leaf_place, bit + 1)
            part = top_transfer[position, pl.ds(pl.multiple_of(side * RANK, RANK), RANK), :]
            downward = term + nt2(downward, part)
    wait_all(later)
    side = lax.bitwise_and(leaf_place, 1)
    part = pair_transfer[pl.ds(pl.multiple_of(side * RANK, RANK), RANK), :]
    downward = pair_term[...] + nt2(downward, part)
    half = lax.shift_right_logical(me, 1)
    part = sub_transfer[2, pl.ds(pl.multiple_of(half * RANK, RANK), RANK), :]
    downward = sub_terms[1] + nt2(downward, part)
    side = lax.bitwise_and(me, 1)
    part = sub_transfer[half, pl.ds(pl.multiple_of(side * RANK, RANK), RANK), :]
    downward = sub_terms[0] + nt2(downward, part)
    nodes = [downward]
    node_start = LEAVES - 1
    term_start = 2 * LEAVES - 2
    while len(nodes) < LEAVES:
        node_start -= len(nodes)
        term_start -= 2 * len(nodes)
        children = []
        for number, value in enumerate(nodes):
            lowered = nt2(value, transfer[node_start + number])
            children.append(terms[term_start + 2 * number] + lowered[:, :RANK])
            children.append(terms[term_start + 2 * number + 1] + lowered[:, RANK:])
        nodes = children
    wait_all(last)
    lane = lax.broadcasted_iota(jnp.int32, (LEAF, 2 * RHS), 1)
    is_whole = lane < RHS
    for leaf in range(LEAVES):
        span = slice(leaf * LEAF, (leaf + 1) * LEAF)
        high, low = halves(nodes[leaf])
        far = nt(basis[leaf], jnp.concatenate([high, high, low, low], axis=0))
        field = near[leaf] + total[leaf] + far[:, : 2 * RHS] + far[:, 2 * RHS :]
        known = rows[span, :]
        both = jnp.where(is_whole, RIDGE * known + field, known - field)
        correction = nn(inverse[leaf], both.astype(BF16))
        rows[span, :] = jnp.where(is_whole, both, correction)

        def put(step, carry, leaf=leaf):
            first = pl.multiple_of(leaf * LEAF + step * 16, 16)
            for offset in range(16):
                moved[pl.ds(order[first + offset], 1), :] = rows[pl.ds(first + offset, 1), :]
            return carry

        lax.fori_loop(0, LEAF // 16, put, 0)
    for leaf in range(LEAVES):
        span = slice(leaf * LEAF, (leaf + 1) * LEAF)
        turned = moved[span, :].T
        product[:, span] = turned[:RHS].astype(BF16)
        update[:, span] = turned[RHS:].astype(BF16)


VM = pl.BlockSpec(memory_space=pltpu.VMEM)
SM = pl.BlockSpec(memory_space=pltpu.SMEM)
HB = pl.BlockSpec(memory_space=pltpu.HBM)
DMA = pltpu.SemaphoreType.DMA
TOTAL = (LEAVES, LEAF, 2 * RHS)
PADDED_TOTAL = (LEAVES + 1, LEAF, 2 * RHS)
TARGET = (LEAVES + 1, LEAF, FEATURES)
LEVEL = (RHS, RANK)


def call(kernel, name, inputs, outputs, scratch, flops=None, aliases=None):
    cost = None
    if flops is not None:
        cost = pl.CostEstimate(flops=flops, bytes_accessed=10**6, transcendentals=0)
    return pl.pallas_call(
        kernel,
        out_shape=tuple(jax.ShapeDtypeStruct(dims, kind) for _, dims, kind in outputs),
        in_specs=[spec for spec, _ in inputs],
        out_specs=tuple(spec for spec, _, _ in outputs),
        scratch_shapes=scratch,
        compiler_params=pltpu.CompilerParams(vmem_limit_bytes=VMEM_LIMIT),
        cost_estimate=cost,
        input_output_aliases=aliases or {},
        name=name,
    )(*[value for _, value in inputs])


def held(array):
    return pltpu.VMEM(array.shape, array.dtype)


def from_distance(value, distance):
    pairs = [((receiver + distance) % N_SUB, receiver) for receiver in range(N_SUB)]
    return lax.ppermute(value, "sub", pairs)


def per_device(
    coords, coefficients, targets, point_order, near_list, near_count, leaf_basis, leaf_inverse,
    local_transfer, local_couple, sub_transfer, sub_couple, top_transfer, top_couple,
):
    point_rows = (POINTS, 2 * RHS)
    order_held = pltpu.SMEM(point_order.shape, jnp.int32)
    payload, skeleton, rows, terms = call(
        rise_kernel,
        "rise",
        [
            (HB, value)
            for value in (
                point_order, coefficients, targets, coords,
                leaf_basis, local_transfer, local_couple,
            )
        ],
        [
            (HB, (RHS, PAYLOAD), BF16),
            (VM, (RHS, 2 * RANK), BF16),
            (HB, point_rows, F32),
            (HB, (2 * LEAVES - 2, RHS, RANK), F32),
        ],
        [
            order_held, held(coefficients), held(targets), held(coords),
            pltpu.VMEM(point_rows, F32), held(leaf_basis), held(local_transfer), held(local_couple),
            pltpu.VMEM((RHS, PAYLOAD), BF16), pltpu.VMEM(point_rows, F32),
            pltpu.VMEM((2 * LEAVES - 2, RHS, RANK), F32), DMA((7,)), DMA((3,)),
        ],
    )
    pieces = [skeleton] + [from_distance(skeleton, distance) for distance in (1, 2, 3)]
    root, sub_terms, relay, ticket = call(
        sub_kernel,
        "sub_rise",
        [(VM, piece) for piece in pieces]
        + [(HB, sub_transfer), (HB, sub_couple), (HB, payload)],
        [
            (VM, LEVEL, F32), (VM, (2,) + LEVEL, F32),
            (HB, payload.shape, BF16), (SM, (1,), jnp.int32),
        ],
        [pltpu.VMEM((N_SUB,) + LEVEL, F32), held(sub_transfer), held(sub_couple), DMA((2,))],
        aliases={6: 2},
    )
    leaf_count = lax.axis_size("leaf")
    partner = lax.ppermute(root, "leaf", [(number, number ^ 1) for number in range(leaf_count)])
    right, left = from_distance(relay, 1), from_distance(relay, 3)
    tables = [
        pltpu.VMEM((GROUP, FEATURES, LEAF), BF16),
        pltpu.VMEM((GROUP, RHS, LEAF), BF16),
    ]
    pair_root, pair_term, ticket = call(
        pair_kernel,
        "pair_rise",
        [
            (SM, ticket), (VM, root), (VM, partner),
            (HB, top_transfer), (HB, top_couple),
        ],
        [(VM, LEVEL, F32), (VM, LEVEL, F32), (SM, (1,), jnp.int32)],
        [pltpu.VMEM((2 * RANK, RANK), BF16), pltpu.VMEM((RANK, RANK), BF16), DMA((2,))],
    )
    same_side = [[side + 2 * pair for pair in range(leaf_count // 2)] for side in range(2)]
    gathered = lax.all_gather(pair_root, "leaf", axis_index_groups=same_side)
    near, target, relay, items, info = call(
        near_first_kernel,
        "near_first",
        [(SM, ticket), (SM, near_list), (SM, near_count), (HB, relay)],
        [
            (HB, TOTAL, F32), (HB, TARGET, BF16), (HB, payload.shape, BF16),
            (SM, (3 * ITEMS,), jnp.int32), (SM, (2,), jnp.int32),
        ],
        tables + [held(payload), pltpu.VMEM(PADDED_TOTAL, F32), pltpu.VMEM(TARGET, BF16), DMA((1,)), DMA((3,))],
        FIRST_FLOPS,
    )
    across = from_distance(relay, 2)

    near, ticket = call(
        near_beside_kernel,
        "near_beside",
        [(SM, items), (SM, info)] + [(HB, value) for value in (right, left, target, near)],
        [(HB, TOTAL, F32), (SM, (1,), jnp.int32)],
        tables
        + [
            pltpu.VMEM(PADDED_TOTAL, F32), pltpu.VMEM(TOTAL, F32), pltpu.VMEM(TARGET, BF16),
            pltpu.VMEM((2, RHS, PAYLOAD), BF16), DMA((4,)), DMA((LEAVES,)),
        ],
        LATER_FLOPS,
    )
    return call(
        near_fall_kernel,
        "near_fall",
        [(SM, ticket), (SM, items), (SM, info)]
        + [
            (HB, value)
            for value in (
                across, target,
                point_order, gathered, top_transfer, top_couple, pair_term, sub_terms, terms,
                sub_transfer, local_transfer, leaf_basis, leaf_inverse, near, rows,
            )
        ],
        [(VM, (RHS, POINTS), BF16), (VM, (RHS, POINTS), BF16)],
        tables
        + [
            pltpu.VMEM(PADDED_TOTAL, F32), pltpu.VMEM(TARGET, BF16), held(across), DMA((2,)),
            order_held, pltpu.VMEM((30,) + LEVEL, F32),
            pltpu.VMEM((14, 2 * RANK, RANK), BF16), pltpu.VMEM((2 * RANK, RANK), BF16),
            pltpu.VMEM((TOP_BITS, RANK, RANK), BF16), pltpu.VMEM(LEVEL, F32),
            pltpu.VMEM((2,) + LEVEL, F32), pltpu.VMEM((2 * LEAVES - 2,) + LEVEL, F32),
            held(sub_transfer), held(local_transfer), held(leaf_basis), held(leaf_inverse),
            pltpu.VMEM(TOTAL, F32), pltpu.VMEM(point_rows, F32), pltpu.VMEM(point_rows, F32),
            DMA((9,)), DMA((TOP_BITS - 1,)), DMA((5,)),
        ],
    )


def solution(mesh):
    both = ("leaf", "sub")
    in_specs = (
        P(None, both), P(None, both), P(None, both), P(both), P(both, None), P(both),
        P(both, None, None), P(both, None, None), P(both, None, None), P(both, None, None),
        P("leaf", None, None), P("leaf", None, None), P(), P(),
    )
    return jax.shard_map(
        per_device,
        mesh=mesh,
        in_specs=in_specs,
        out_specs=(P(None, both), P(None, both)),
        check_vma=False,
    )
```

```python
import functools

import jax
import jax.numpy as jnp
from jax import lax
from jax.experimental import pallas as pl
from jax.experimental.pallas import tpu as pltpu
from jax.sharding import PartitionSpec as P

RIDGE = 0.5
SHARPNESS = 0.25
LOG2E = 1.4426950408889634
F32 = jnp.float32
BF16 = jnp.bfloat16

RHS = 64
DIMS = 8
LEAF = 512
RANK = 256
SLOTS = 24
LEAVES = 8
POINTS = LEAVES * LEAF
GROUP = 32
N_SUB = 4
PAYLOAD = POINTS + LEAF
FEATURES = 32
UNROLL = 8
ROW_RUN = 64
ITEMS = LEAVES * SLOTS + 2 * UNROLL
TOP_BITS = 5
TOP_START = (0, 16, 24, 28, 30)
PAIRS = 16
LEVEL_START = (None, 0, 16, 24, 28)
VMEM_LIMIT = 56 * 2**20
PLAN_FLOPS = 10**9
FIRST_FLOPS = 10**10
LATER_FLOPS = 10**10


def nn(left, right):
    return jnp.dot(left, right, preferred_element_type=F32)


def nt(left, right):
    return lax.dot_general(left, right, (((1,), (1,)), ((), ())), preferred_element_type=F32)


def halves(value):
    high = value.astype(BF16)
    return high, (value - high.astype(F32)).astype(BF16)


def stacked(value):
    return jnp.concatenate(halves(value), axis=0)


def fold(value):
    rows = value.shape[0] // 2
    return value[:rows] + value[rows:]


def nn2(value, matrix):
    return fold(nn(stacked(value), matrix))


def nt2(value, matrix):
    return fold(nt(stacked(value), matrix))


def thirds(value):
    high = value.astype(BF16).astype(F32)
    rest = value - high
    middle = rest.astype(BF16).astype(F32)
    return high, middle, rest - middle


def square_rows(points, first):
    high, middle, low = thirds(
        jnp.sum(points * points, axis=0, keepdims=True) * (-SHARPNESS * LOG2E)
    )
    row = lax.broadcasted_iota(jnp.int32, points.shape, 0) - first
    parts = jnp.where(row == 0, high, jnp.where(row == 1, middle, low))
    ones = ((row + first >= 0) & (row + first < 6)).astype(F32)
    return jnp.where((row >= 0) & (row < 3), parts, ones)


def source_features(points):
    return jnp.concatenate([points, points, points, square_rows(points, 0)], axis=0).astype(BF16)


def target_features(points):
    high, middle, low = thirds(points * (2.0 * SHARPNESS * LOG2E))
    return jnp.concatenate([high, middle, low, square_rows(points, 3)], axis=0)


def leaf_points(payload, leaf):
    start = 16 * (leaf // 2)
    pair = payload[start : start + 16, POINTS:].astype(F32)
    return pair[DIMS * (leaf % 2) : DIMS * (leaf % 2) + DIMS]


def start_all(moves, arrived):
    copies = [
        pltpu.make_async_copy(source, target, arrived.at[number])
        for number, (source, target) in enumerate(moves)
    ]
    for copy in copies:
        copy.start()
    return copies


def wait_all(copies):
    for copy in copies:
        copy.wait()


def rise_kernel(
    order_hbm, coefficients_hbm, targets_hbm, coords_hbm, basis_hbm, transfer_hbm, couple_hbm,
    payload_hbm, skeleton, rows_hbm, terms_hbm,
    order, coefficients, targets, coords, columns, basis, transfer, couple,
    payload, rows, terms, arrived, left,
):
    copies = start_all(
        (
            (coefficients_hbm, coefficients),
            (targets_hbm, targets),
            (order_hbm, order),
            (basis_hbm, basis),
            (transfer_hbm, transfer),
            (couple_hbm, couple),
            (coords_hbm, coords),
        ),
        arrived,
    )
    wait_all(copies[:2])
    for leaf in range(LEAVES):
        span = slice(leaf * LEAF, (leaf + 1) * LEAF)
        values = coefficients[:, span].astype(F32)
        wanted = targets[:, span].astype(F32) - RIDGE * values
        columns[span, :] = jnp.concatenate([values, wanted], axis=0).T
    copies[2].wait()

    def pick(step, carry):
        first = pl.multiple_of(step * ROW_RUN, ROW_RUN)
        for offset in range(ROW_RUN):
            rows[pl.ds(first + offset, 1), :] = columns[pl.ds(order[first + offset], 1), :]
        return carry

    lax.fori_loop(0, POINTS // ROW_RUN, pick, 0)
    sent = [pltpu.make_async_copy(rows, rows_hbm, left.at[0])]
    sent[0].start()
    copies[3].wait()
    coefs = []
    for leaf in range(LEAVES):
        span = slice(leaf * LEAF, (leaf + 1) * LEAF)
        values = rows[span, :].T[:RHS].astype(BF16)
        payload[:, span] = values
        coefs.append(nn(values, basis[leaf]))
    copies[6].wait()
    for pair in range(LEAVES // 2):
        both = [coords[:, leaf * LEAF : (leaf + 1) * LEAF].astype(F32) for leaf in (2 * pair, 2 * pair + 1)]
        payload[16 * pair : 16 * pair + 16, POINTS:] = jnp.concatenate(both, axis=0).astype(BF16)
    sent.append(pltpu.make_async_copy(payload, payload_hbm, left.at[1]))
    sent[1].start()
    wait_all(copies[4:6])
    node = 0
    term = 0
    while len(coefs) > 1:
        parents = []
        for left_child in range(0, len(coefs), 2):
            one, two = coefs[left_child], coefs[left_child + 1]
            terms[term + left_child] = nt2(two, couple[node])
            terms[term + left_child + 1] = nn2(one, couple[node])
            parents.append(nn2(jnp.concatenate([one, two], axis=1), transfer[node]))
            node += 1
        term += len(coefs)
        coefs = parents
    sent.append(pltpu.make_async_copy(terms, terms_hbm, left.at[2]))
    sent[2].start()
    high, low = halves(coefs[0])
    skeleton[:, :RANK] = high
    skeleton[:, RANK:] = low
    wait_all(sent)


def near_step(item, target, source, values, total):
    leaf = lax.shift_right_logical(item, 5)
    other = lax.bitwise_and(item, 31)
    tile = jnp.exp2(nn(target[leaf], source[other])).astype(BF16)
    block = values[other]
    total[leaf] += nt(tile, jnp.concatenate([block, block], axis=0))


def near_prepare(payload, first, source, values):
    for leaf in range(LEAVES):
        source[first + leaf] = source_features(leaf_points(payload, leaf))
        values[first + leaf] = payload[:, leaf * LEAF : (leaf + 1) * LEAF]


def near_groups(items, first, groups, target, source, values, total):
    def group(step, carry):
        for offset in range(UNROLL):
            near_step(items[first + step * UNROLL + offset], target, source, values, total)
        return carry

    lax.fori_loop(0, groups, group, 0)


def near_pairs(items, first, pairs, target, source, values, total):
    def pair(step, carry):
        for offset in range(2):
            near_step(items[first + step * 2 + offset], target, source, values, total)
        return carry

    lax.fori_loop(0, pairs, pair, 0)


def near_all(items, first, used, target, source, values, total):
    groups = used // UNROLL
    near_groups(items, first, groups, target, source, values, total)
    near_pairs(
        items, first + groups * UNROLL, (used - groups * UNROLL + 1) // 2,
        target, source, values, total,
    )


def near_plan_kernel(
    near_list, near_count, coords_hbm, skeleton_hbm,
    target_hbm, items, info,
    coords, target, arrived, left,
):
    copies = start_all(((coords_hbm, coords),), arrived)
    me = lax.axis_index("sub")
    zero = jnp.int32(0)
    counts = (zero, zero, zero)
    for leaf in range(LEAVES):

        def collect(slot, counts, leaf=leaf):
            local, beside, across = counts
            other = near_list[leaf, slot]
            distance = lax.bitwise_and(lax.shift_right_logical(other, 3) - me, 3)
            is_local = (distance == 0).astype(jnp.int32)
            is_across = (distance == 2).astype(jnp.int32)
            is_beside = 1 - is_local - is_across
            where = is_local * local + is_beside * (ITEMS + beside) + is_across * (2 * ITEMS + across)
            items[where] = leaf * GROUP + other
            return local + is_local, beside + is_beside, across + is_across

        counts = lax.fori_loop(0, near_count[leaf], collect, counts)
    local, beside, across = counts
    items[local] = LEAVES * GROUP + me * LEAVES
    items[ITEMS + beside] = LEAVES * GROUP + lax.bitwise_and(me + 1, 3) * LEAVES
    items[2 * ITEMS + across] = LEAVES * GROUP + lax.bitwise_and(me + 2, 3) * LEAVES
    info[0] = beside
    info[1] = across
    info[2] = local
    wait_all(copies)
    for leaf in range(LEAVES):
        points = coords[:, leaf * LEAF : (leaf + 1) * LEAF].astype(F32)
        target[leaf] = target_features(points).T.astype(BF16)
    target[LEAVES] = jnp.zeros_like(target[LEAVES])
    wait_all(start_all(((target, target_hbm),), left))


def near_first_kernel(
    ticket, items, info, payload_hbm, target_hbm,
    total_hbm, relay_hbm, after,
    source, values, payload, total, target, arrived, left,
):
    after[0] = ticket[0]
    copies = start_all(((payload_hbm, payload), (target_hbm, target)), arrived)
    total[...] = jnp.zeros_like(total)
    copies[0].wait()
    sent = start_all(((payload, relay_hbm),), left)
    near_prepare(payload, lax.axis_index("sub") * LEAVES, source, values)
    copies[1].wait()
    near_all(items, 0, info[2], target, source, values, total)
    sent += start_all(((total.at[pl.ds(0, LEAVES)], total_hbm),), left.at[pl.ds(1, 1)])
    wait_all(sent)


def near_beside_kernel(
    before, items, info, right_hbm, left_hbm, target_hbm,
    total_hbm, ticket,
    source, values, total, target, payloads, arrived, left,
):
    ticket[0] = before[0]
    copies = start_all(
        ((right_hbm, payloads.at[0]), (left_hbm, payloads.at[1]), (target_hbm, target)), arrived
    )
    total[...] = jnp.zeros_like(total)
    for number, distance in enumerate((1, 3)):
        copies[number].wait()
        where = lax.bitwise_and(lax.axis_index("sub") + distance, 3)
        near_prepare(payloads.at[number], where * LEAVES, source, values)
    copies[2].wait()
    near_all(items, ITEMS, info[0], target, source, values, total)
    wait_all(start_all(((total.at[pl.ds(0, LEAVES)], total_hbm),), left))


def sub_kernel(
    info, own, right, across, left, transfer_hbm, couple_hbm, payload_hbm,
    root, terms, relay_hbm, ticket,
    coefs, transfer, couple, arrived,
):
    copies = start_all(((transfer_hbm, transfer), (couple_hbm, couple)), arrived)
    me = lax.axis_index("sub")
    ticket[0] = info[0]
    for distance, pair in enumerate((own, right, across, left)):
        value = pair[:, :RANK].astype(F32) + pair[:, RANK:].astype(F32)
        coefs[lax.bitwise_and(me + distance, 3)] = value
    wait_all(copies)
    lower = nn2(jnp.concatenate([coefs[0], coefs[1]], axis=1), transfer[0])
    upper = nn2(jnp.concatenate([coefs[2], coefs[3]], axis=1), transfer[1])
    root[...] = nn2(jnp.concatenate([lower, upper], axis=1), transfer[2])
    half = lax.shift_right_logical(me, 1)
    sibling = stacked(coefs[lax.bitwise_xor(me, 1)])
    matrix = couple[half]
    is_left = lax.bitwise_and(me, 1) == 0
    terms[0] = fold(jnp.where(is_left, nt(sibling, matrix), nn(sibling, matrix)))
    terms[1] = jnp.where(half == 0, nt2(upper, couple[2]), nn2(lower, couple[2]))


def pair_kernel(
    info, own, partner, transfer_hbm, couple_hbm,
    root, term, ticket,
    transfer, couple, arrived,
):
    ticket[0] = info[0]
    node = lax.shift_right_logical(lax.axis_index("leaf"), 1)
    is_left = lax.bitwise_and(lax.axis_index("leaf"), 1) == 0
    copies = start_all(
        ((transfer_hbm.at[node], transfer), (couple_hbm.at[node], couple)), arrived
    )
    one = jnp.where(is_left, own[...], partner[...])
    two = jnp.where(is_left, partner[...], own[...])
    wait_all(copies)
    root[...] = nn2(jnp.concatenate([one, two], axis=1), transfer[...])
    sibling = stacked(partner[...])
    term[...] = fold(jnp.where(is_left, nt(sibling, couple[...]), nn(sibling, couple[...])))


def near_fall_kernel(
    ticket, items, info, across_hbm, target_hbm,
    order_hbm, gathered_hbm, top_transfer_hbm, top_couple_hbm, pair_term_hbm,
    sub_terms_hbm, terms_hbm, sub_transfer_hbm, transfer_hbm, basis_hbm, inverse_hbm,
    near_own_hbm, near_beside_hbm, known_hbm,
    product, update,
    source, values, total, target, payload, near_arrived,
    order, level, top_transfer, pair_transfer, top_couple, pair_term,
    sub_terms, terms, sub_transfer, transfer, basis, inverse,
    near, rows, moved, arrived, couple_arrived, leaf_arrived,
):
    first = start_all(((across_hbm, payload), (target_hbm, target)), near_arrived)
    total[...] = jnp.zeros_like(total)
    first[0].wait()
    across = lax.bitwise_and(lax.axis_index("sub") + 2, 3)
    near_prepare(payload, across * LEAVES, source, values)
    first[1].wait()
    leaf_place = lax.axis_index("leaf")
    me = lax.axis_index("sub")
    copies = start_all(
        (
            (gathered_hbm, level.at[pl.ds(0, PAIRS)]),
            (top_transfer_hbm.at[pl.ds(TOP_START[1], 8)], top_transfer.at[pl.ds(0, 8)]),
            (top_transfer_hbm.at[pl.ds(TOP_START[2], 6)], top_transfer.at[pl.ds(8, 6)]),
        ),
        arrived,
    )
    couples = start_all(
        [
            (
                top_couple_hbm.at[TOP_START[bit] + lax.shift_right_logical(leaf_place, bit + 1)],
                top_couple.at[bit],
            )
            for bit in range(1, TOP_BITS)
        ],
        couple_arrived,
    )
    later = start_all(
        (
            (top_transfer_hbm.at[lax.shift_right_logical(leaf_place, 1)], pair_transfer),
            (pair_term_hbm, pair_term),
            (sub_terms_hbm, sub_terms),
            (sub_transfer_hbm, sub_transfer),
            (terms_hbm, terms),
            (transfer_hbm, transfer),
        ),
        arrived.at[pl.ds(3, 6)],
    )
    last = start_all(
        (
            (order_hbm, order),
            (near_own_hbm, near.at[0]),
            (near_beside_hbm, near.at[1]),
            (known_hbm, rows),
            (basis_hbm, basis),
            (inverse_hbm, inverse),
        ),
        leaf_arrived,
    )
    near_all(items, 2 * ITEMS, info[1], target, source, values, total)
    copies[0].wait()
    for height in range(1, TOP_BITS - 1):
        below = LEVEL_START[height]
        here = LEVEL_START[height + 1]
        if height < 3:
            copies[height].wait()
        for node in range(PAIRS >> height):
            joined = jnp.concatenate([level[below + 2 * node], level[below + 2 * node + 1]], axis=1)
            level[here + node] = nn2(joined, top_transfer[TOP_START[height] - PAIRS + node])
    wait_all(couples)
    downward = None
    for bit in range(TOP_BITS - 1, 0, -1):
        child = lax.shift_right_logical(leaf_place, bit)
        side = lax.bitwise_and(child, 1)
        sibling = stacked(level[LEVEL_START[bit] + lax.bitwise_xor(child, 1)])
        matrix = top_couple[bit]
        term = fold(jnp.where(side == 0, nt(sibling, matrix), nn(sibling, matrix)))
        if downward is None:
            downward = term
        else:
            position = TOP_START[bit] - PAIRS + lax.shift_right_logical(leaf_place, bit + 1)
            part = top_transfer[position, pl.ds(pl.multiple_of(side * RANK, RANK), RANK), :]
            downward = term + nt2(downward, part)
    wait_all(later)
    side = lax.bitwise_and(leaf_place, 1)
    part = pair_transfer[pl.ds(pl.multiple_of(side * RANK, RANK), RANK), :]
    downward = pair_term[...] + nt2(downward, part)
    half = lax.shift_right_logical(me, 1)
    part = sub_transfer[2, pl.ds(pl.multiple_of(half * RANK, RANK), RANK), :]
    downward = sub_terms[1] + nt2(downward, part)
    side = lax.bitwise_and(me, 1)
    part = sub_transfer[half, pl.ds(pl.multiple_of(side * RANK, RANK), RANK), :]
    downward = sub_terms[0] + nt2(downward, part)
    nodes = [downward]
    node_start = LEAVES - 1
    term_start = 2 * LEAVES - 2
    while len(nodes) < LEAVES:
        node_start -= len(nodes)
        term_start -= 2 * len(nodes)
        children = []
        for number, value in enumerate(nodes):
            lowered = nt2(value, transfer[node_start + number])
            children.append(terms[term_start + 2 * number] + lowered[:, :RANK])
            children.append(terms[term_start + 2 * number + 1] + lowered[:, RANK:])
        nodes = children
    wait_all(last)
    lane = lax.broadcasted_iota(jnp.int32, (LEAF, 2 * RHS), 1)
    is_whole = lane < RHS
    for leaf in range(LEAVES):
        span = slice(leaf * LEAF, (leaf + 1) * LEAF)
        high, low = halves(nodes[leaf])
        far = nt(basis[leaf], jnp.concatenate([high, high, low, low], axis=0))
        field = near[0, leaf] + near[1, leaf] + total[leaf] + far[:, : 2 * RHS] + far[:, 2 * RHS :]
        known = rows[span, :]
        both = jnp.where(is_whole, RIDGE * known + field, known - field)
        correction = nn(inverse[leaf], both.astype(BF16))
        rows[span, :] = jnp.where(is_whole, both, correction)

        def put(step, carry, leaf=leaf):
            first = pl.multiple_of(leaf * LEAF + step * ROW_RUN, ROW_RUN)
            for offset in range(ROW_RUN):
                moved[pl.ds(order[first + offset], 1), :] = rows[pl.ds(first + offset, 1), :]
            return carry

        lax.fori_loop(0, LEAF // ROW_RUN, put, 0)
    for leaf in range(LEAVES):
        span = slice(leaf * LEAF, (leaf + 1) * LEAF)
        turned = moved[span, :].T
        product[:, span] = turned[:RHS].astype(BF16)
        update[:, span] = turned[RHS:].astype(BF16)


VM = pl.BlockSpec(memory_space=pltpu.VMEM)
SM = pl.BlockSpec(memory_space=pltpu.SMEM)
HB = pl.BlockSpec(memory_space=pltpu.HBM)
DMA = pltpu.SemaphoreType.DMA
TOTAL = (LEAVES, LEAF, 2 * RHS)
PADDED_TOTAL = (LEAVES + 1, LEAF, 2 * RHS)
TARGET = (LEAVES + 1, LEAF, FEATURES)
LEVEL = (RHS, RANK)


def call(kernel, name, inputs, outputs, scratch, flops=None, aliases=None):
    cost = None
    if flops is not None:
        cost = pl.CostEstimate(flops=flops, bytes_accessed=10**6, transcendentals=0)
    return pl.pallas_call(
        kernel,
        out_shape=tuple(jax.ShapeDtypeStruct(dims, kind) for _, dims, kind in outputs),
        in_specs=[spec for spec, _ in inputs],
        out_specs=tuple(spec for spec, _, _ in outputs),
        scratch_shapes=scratch,
        compiler_params=pltpu.CompilerParams(vmem_limit_bytes=VMEM_LIMIT),
        cost_estimate=cost,
        input_output_aliases=aliases or {},
        name=name,
    )(*[value for _, value in inputs])


def held(array):
    return pltpu.VMEM(array.shape, array.dtype)


def from_distance(value, distance):
    pairs = [((receiver + distance) % N_SUB, receiver) for receiver in range(N_SUB)]
    return lax.ppermute(value, "sub", pairs)


def per_device(
    coords, coefficients, targets, point_order, near_list, near_count, leaf_basis, leaf_inverse,
    local_transfer, local_couple, sub_transfer, sub_couple, top_transfer, top_couple,
):
    point_rows = (POINTS, 2 * RHS)
    order_held = pltpu.SMEM(point_order.shape, jnp.int32)
    payload, skeleton, rows, terms = call(
        rise_kernel,
        "rise",
        [
            (HB, value)
            for value in (
                point_order, coefficients, targets, coords,
                leaf_basis, local_transfer, local_couple,
            )
        ],
        [
            (HB, (RHS, PAYLOAD), BF16),
            (VM, (RHS, 2 * RANK), BF16),
            (HB, point_rows, F32),
            (HB, (2 * LEAVES - 2, RHS, RANK), F32),
        ],
        [
            order_held, held(coefficients), held(targets), held(coords),
            pltpu.VMEM(point_rows, F32), held(leaf_basis), held(local_transfer), held(local_couple),
            pltpu.VMEM((RHS, PAYLOAD), BF16), pltpu.VMEM(point_rows, F32),
            pltpu.VMEM((2 * LEAVES - 2, RHS, RANK), F32), DMA((7,)), DMA((3,)),
        ],
    )
    pieces = [skeleton] + [from_distance(skeleton, distance) for distance in (1, 2, 3)]
    target, items, info = call(
        near_plan_kernel,
        "near_plan",
        [(SM, near_list), (SM, near_count), (HB, coords), (HB, skeleton)],
        [(HB, TARGET, BF16), (SM, (3 * ITEMS,), jnp.int32), (SM, (3,), jnp.int32)],
        [held(coords), pltpu.VMEM(TARGET, BF16), DMA((1,)), DMA((1,))],
        PLAN_FLOPS,
    )
    root, sub_terms, relay, ticket = call(
        sub_kernel,
        "sub_rise",
        [(SM, info)] + [(VM, piece) for piece in pieces]
        + [(HB, sub_transfer), (HB, sub_couple), (HB, payload)],
        [
            (VM, LEVEL, F32), (VM, (2,) + LEVEL, F32),
            (HB, payload.shape, BF16), (SM, (1,), jnp.int32),
        ],
        [pltpu.VMEM((N_SUB,) + LEVEL, F32), held(sub_transfer), held(sub_couple), DMA((2,))],
        aliases={7: 2},
    )
    leaf_count = lax.axis_size("leaf")
    partner = lax.ppermute(root, "leaf", [(number, number ^ 1) for number in range(leaf_count)])
    right, left = from_distance(relay, 1), from_distance(relay, 3)
    tables = [
        pltpu.VMEM((GROUP, FEATURES, LEAF), BF16),
        pltpu.VMEM((GROUP, RHS, LEAF), BF16),
    ]
    pair_root, pair_term, ticket = call(
        pair_kernel,
        "pair_rise",
        [
            (SM, ticket), (VM, root), (VM, partner),
            (HB, top_transfer), (HB, top_couple),
        ],
        [(VM, LEVEL, F32), (VM, LEVEL, F32), (SM, (1,), jnp.int32)],
        [pltpu.VMEM((2 * RANK, RANK), BF16), pltpu.VMEM((RANK, RANK), BF16), DMA((2,))],
    )
    same_side = [[side + 2 * pair for pair in range(leaf_count // 2)] for side in range(2)]
    gathered = lax.all_gather(pair_root, "leaf", axis_index_groups=same_side)
    near_own, relay, ticket = call(
        near_first_kernel,
        "near_first",
        [(SM, ticket), (SM, items), (SM, info), (HB, relay), (HB, target)],
        [(HB, TOTAL, F32), (HB, payload.shape, BF16), (SM, (1,), jnp.int32)],
        tables
        + [held(payload), pltpu.VMEM(PADDED_TOTAL, F32), pltpu.VMEM(TARGET, BF16), DMA((2,)), DMA((2,))],
        FIRST_FLOPS,
    )
    across = from_distance(relay, 2)

    near_beside, ticket = call(
        near_beside_kernel,
        "near_beside",
        [(SM, ticket), (SM, items), (SM, info)] + [(HB, value) for value in (right, left, target)],
        [(HB, TOTAL, F32), (SM, (1,), jnp.int32)],
        tables
        + [
            pltpu.VMEM(PADDED_TOTAL, F32), pltpu.VMEM(TARGET, BF16),
            pltpu.VMEM((2, RHS, PAYLOAD), BF16), DMA((3,)), DMA((1,)),
        ],
        LATER_FLOPS,
    )
    return call(
        near_fall_kernel,
        "near_fall",
        [(SM, ticket), (SM, items), (SM, info)]
        + [
            (HB, value)
            for value in (
                across, target,
                point_order, gathered, top_transfer, top_couple, pair_term, sub_terms, terms,
                sub_transfer, local_transfer, leaf_basis, leaf_inverse, near_own, near_beside, rows,
            )
        ],
        [(VM, (RHS, POINTS), BF16), (VM, (RHS, POINTS), BF16)],
        tables
        + [
            pltpu.VMEM(PADDED_TOTAL, F32), pltpu.VMEM(TARGET, BF16), held(across), DMA((2,)),
            order_held, pltpu.VMEM((30,) + LEVEL, F32),
            pltpu.VMEM((14, 2 * RANK, RANK), BF16), pltpu.VMEM((2 * RANK, RANK), BF16),
            pltpu.VMEM((TOP_BITS, RANK, RANK), BF16), pltpu.VMEM(LEVEL, F32),
            pltpu.VMEM((2,) + LEVEL, F32), pltpu.VMEM((2 * LEAVES - 2,) + LEVEL, F32),
            held(sub_transfer), held(local_transfer), held(leaf_basis), held(leaf_inverse),
            pltpu.VMEM((2,) + TOTAL, F32), pltpu.VMEM(point_rows, F32), pltpu.VMEM(point_rows, F32),
            DMA((9,)), DMA((TOP_BITS - 1,)), DMA((6,)),
        ],
    )


def solution(mesh):
    both = ("leaf", "sub")
    in_specs = (
        P(None, both), P(None, both), P(None, both), P(both), P(both, None), P(both),
        P(both, None, None), P(both, None, None), P(both, None, None), P(both, None, None),
        P("leaf", None, None), P("leaf", None, None), P(), P(),
    )
    return jax.shard_map(
        per_device,
        mesh=mesh,
        in_specs=in_specs,
        out_specs=(P(None, both), P(None, both)),
        check_vma=False,
    )
```

```python
import functools

import jax
import jax.numpy as jnp
from jax import lax
from jax.experimental import pallas as pl
from jax.experimental.pallas import tpu as pltpu
from jax.sharding import PartitionSpec as P

RIDGE = 0.5
SHARPNESS = 0.25
LOG2E = 1.4426950408889634
F32 = jnp.float32
BF16 = jnp.bfloat16

RHS = 64
DIMS = 8
LEAF = 512
RANK = 256
SLOTS = 24
LEAVES = 8
POINTS = LEAVES * LEAF
GROUP = 32
N_SUB = 4
PAYLOAD = POINTS + LEAF
FEATURES = 32
UNROLL = 8
EARLY = 6
ROW_RUN = 64
ITEMS = LEAVES * SLOTS + 2 * UNROLL
TOP_BITS = 5
TOP_START = (0, 16, 24, 28, 30)
PAIRS = 16
LEVEL_START = (None, 0, 16, 24, 28)
VMEM_LIMIT = 56 * 2**20
PLAN_FLOPS = 10**9
FIRST_FLOPS = 10**10
LATER_FLOPS = 10**10


def nn(left, right):
    return jnp.dot(left, right, preferred_element_type=F32)


def nt(left, right):
    return lax.dot_general(left, right, (((1,), (1,)), ((), ())), preferred_element_type=F32)


def halves(value):
    high = value.astype(BF16)
    return high, (value - high.astype(F32)).astype(BF16)


def stacked(value):
    return jnp.concatenate(halves(value), axis=0)


def fold(value):
    rows = value.shape[0] // 2
    return value[:rows] + value[rows:]


def nn2(value, matrix):
    return fold(nn(stacked(value), matrix))


def nt2(value, matrix):
    return fold(nt(stacked(value), matrix))


def thirds(value):
    high = value.astype(BF16).astype(F32)
    rest = value - high
    middle = rest.astype(BF16).astype(F32)
    return high, middle, rest - middle


def square_rows(points, first):
    high, middle, low = thirds(
        jnp.sum(points * points, axis=0, keepdims=True) * (-SHARPNESS * LOG2E)
    )
    row = lax.broadcasted_iota(jnp.int32, points.shape, 0) - first
    parts = jnp.where(row == 0, high, jnp.where(row == 1, middle, low))
    ones = ((row + first >= 0) & (row + first < 6)).astype(F32)
    return jnp.where((row >= 0) & (row < 3), parts, ones)


def source_features(points):
    return jnp.concatenate([points, points, points, square_rows(points, 0)], axis=0).astype(BF16)


def target_features(points):
    high, middle, low = thirds(points * (2.0 * SHARPNESS * LOG2E))
    return jnp.concatenate([high, middle, low, square_rows(points, 3)], axis=0)


def leaf_points(payload, leaf):
    start = 16 * (leaf // 2)
    pair = payload[start : start + 16, POINTS:].astype(F32)
    return pair[DIMS * (leaf % 2) : DIMS * (leaf % 2) + DIMS]


def start_all(moves, arrived):
    copies = [
        pltpu.make_async_copy(source, target, arrived.at[number])
        for number, (source, target) in enumerate(moves)
    ]
    for copy in copies:
        copy.start()
    return copies


def wait_all(copies):
    for copy in copies:
        copy.wait()


def rise_kernel(
    order_hbm, coefficients_hbm, targets_hbm, coords_hbm, basis_hbm, transfer_hbm, couple_hbm,
    payload_hbm, skeleton, rows_hbm, terms_hbm,
    order, coefficients, targets, coords, columns, basis, transfer, couple,
    payload, rows, terms, arrived, left,
):
    copies = start_all(
        (
            (coefficients_hbm, coefficients),
            (targets_hbm, targets),
            (order_hbm, order),
            (basis_hbm, basis),
            (transfer_hbm, transfer),
            (couple_hbm, couple),
            (coords_hbm, coords),
        ),
        arrived,
    )
    wait_all(copies[:2])
    for leaf in range(LEAVES):
        span = slice(leaf * LEAF, (leaf + 1) * LEAF)
        values = coefficients[:, span].astype(F32)
        wanted = targets[:, span].astype(F32) - RIDGE * values
        columns[span, :] = jnp.concatenate([values, wanted], axis=0).T
    copies[2].wait()

    def pick(step, carry):
        first = pl.multiple_of(step * ROW_RUN, ROW_RUN)
        for offset in range(ROW_RUN):
            rows[pl.ds(first + offset, 1), :] = columns[pl.ds(order[first + offset], 1), :]
        return carry

    lax.fori_loop(0, POINTS // ROW_RUN, pick, 0)
    sent = [pltpu.make_async_copy(rows, rows_hbm, left.at[0])]
    sent[0].start()
    copies[3].wait()
    coefs = []
    for leaf in range(LEAVES):
        span = slice(leaf * LEAF, (leaf + 1) * LEAF)
        values = rows[span, :].T[:RHS].astype(BF16)
        payload[:, span] = values
        coefs.append(nn(values, basis[leaf]))
    copies[6].wait()
    for pair in range(LEAVES // 2):
        both = [coords[:, leaf * LEAF : (leaf + 1) * LEAF].astype(F32) for leaf in (2 * pair, 2 * pair + 1)]
        payload[16 * pair : 16 * pair + 16, POINTS:] = jnp.concatenate(both, axis=0).astype(BF16)
    sent.append(pltpu.make_async_copy(payload, payload_hbm, left.at[1]))
    sent[1].start()
    wait_all(copies[4:6])
    node = 0
    term = 0
    while len(coefs) > 1:
        parents = []
        for left_child in range(0, len(coefs), 2):
            one, two = coefs[left_child], coefs[left_child + 1]
            terms[term + left_child] = nt2(two, couple[node])
            terms[term + left_child + 1] = nn2(one, couple[node])
            parents.append(nn2(jnp.concatenate([one, two], axis=1), transfer[node]))
            node += 1
        term += len(coefs)
        coefs = parents
    sent.append(pltpu.make_async_copy(terms, terms_hbm, left.at[2]))
    sent[2].start()
    high, low = halves(coefs[0])
    skeleton[:, :RANK] = high
    skeleton[:, RANK:] = low
    wait_all(sent)


def near_step(item, target, source, values, total, base):
    leaf = lax.shift_right_logical(item, 5)
    other = lax.bitwise_and(item, 31)
    tile = jnp.exp2(nn(target[leaf], source[other])).astype(BF16)
    block = values[other]
    total[leaf - base] += nt(tile, jnp.concatenate([block, block], axis=0))


def near_prepare(payload, first, source, values):
    for leaf in range(LEAVES):
        source[first + leaf] = source_features(leaf_points(payload, leaf))
        values[first + leaf] = payload[:, leaf * LEAF : (leaf + 1) * LEAF]


def near_runs(items, first, count, length, target, source, values, total, base=0):
    def run(step, carry):
        for offset in range(length):
            near_step(items[first + step * length + offset], target, source, values, total, base)
        return carry

    lax.fori_loop(0, count, run, 0)


def near_all(items, first, used, target, source, values, total, base=0):
    groups = used // UNROLL
    near_runs(items, first, groups, UNROLL, target, source, values, total, base)
    first = first + groups * UNROLL
    used = used - groups * UNROLL
    near_runs(items, first, (used + 1) // 2, 2, target, source, values, total, base)


def near_sent(items, first, used, early, target, source, values, total, late, total_hbm, left):
    runs = jnp.minimum((early + UNROLL - 1) // UNROLL, used // UNROLL)
    done = runs * UNROLL
    near_runs(items, first, runs, UNROLL, target, source, values, total)
    rest = jnp.maximum(early - done, 0)
    near_runs(items, first + done, rest, 1, target, source, values, total)
    done = done + rest
    sent = start_all(((total.at[pl.ds(0, EARLY)], total_hbm.at[pl.ds(0, EARLY)]),), left)
    near_all(items, first + done, used - done, target, source, values, late, EARLY)
    for leaf in range(LEAVES - EARLY):
        late[leaf] += total[EARLY + leaf]
    sent += start_all(
        (
            (
                late.at[pl.ds(0, LEAVES - EARLY)],
                total_hbm.at[pl.ds(EARLY, LEAVES - EARLY)],
            ),
        ),
        left.at[pl.ds(1, 1)],
    )
    return sent


def near_plan_kernel(
    near_list, near_count, coords_hbm, skeleton_hbm,
    target_hbm, items, info,
    coords, target, arrived, left,
):
    copies = start_all(((coords_hbm, coords),), arrived)
    me = lax.axis_index("sub")
    zero = jnp.int32(0)
    counts = (zero, zero, zero)
    for leaf in range(LEAVES):

        def collect(slot, counts, leaf=leaf):
            local, beside, across = counts
            other = near_list[leaf, slot]
            distance = lax.bitwise_and(lax.shift_right_logical(other, 3) - me, 3)
            is_local = (distance == 0).astype(jnp.int32)
            is_across = (distance == 2).astype(jnp.int32)
            is_beside = 1 - is_local - is_across
            where = is_local * local + is_beside * (ITEMS + beside) + is_across * (2 * ITEMS + across)
            items[where] = leaf * GROUP + other
            return local + is_local, beside + is_beside, across + is_across

        counts = lax.fori_loop(0, near_count[leaf], collect, counts)
        if leaf == EARLY - 1:
            info[3] = counts[0]
            info[4] = counts[1]
    local, beside, across = counts
    items[local] = LEAVES * GROUP + me * LEAVES
    items[ITEMS + beside] = LEAVES * GROUP + lax.bitwise_and(me + 1, 3) * LEAVES
    items[2 * ITEMS + across] = LEAVES * GROUP + lax.bitwise_and(me + 2, 3) * LEAVES
    info[0] = beside
    info[1] = across
    info[2] = local
    wait_all(copies)
    for leaf in range(LEAVES):
        points = coords[:, leaf * LEAF : (leaf + 1) * LEAF].astype(F32)
        target[leaf] = target_features(points).T.astype(BF16)
    target[LEAVES] = jnp.zeros_like(target[LEAVES])
    wait_all(start_all(((target, target_hbm),), left))


def near_first_kernel(
    ticket, items, info, payload_hbm, target_hbm,
    total_hbm, relay_hbm, after,
    source, values, payload, total, late, target, arrived, left,
):
    after[0] = ticket[0]
    copies = start_all(((payload_hbm, payload), (target_hbm, target)), arrived)
    total[...] = jnp.zeros_like(total)
    late[...] = jnp.zeros_like(late)
    copies[0].wait()
    sent = start_all(((payload, relay_hbm),), left)
    near_prepare(payload, lax.axis_index("sub") * LEAVES, source, values)
    copies[1].wait()
    sent += near_sent(
        items, 0, info[2], info[3], target, source, values, total, late, total_hbm,
        left.at[pl.ds(1, 2)],
    )
    wait_all(sent)


def near_beside_kernel(
    before, items, info, right_hbm, left_hbm, target_hbm,
    total_hbm, ticket,
    source, values, total, late, target, payloads, arrived, left,
):
    ticket[0] = before[0]
    copies = start_all(
        ((right_hbm, payloads.at[0]), (left_hbm, payloads.at[1]), (target_hbm, target)), arrived
    )
    total[...] = jnp.zeros_like(total)
    late[...] = jnp.zeros_like(late)
    for number, distance in enumerate((1, 3)):
        copies[number].wait()
        where = lax.bitwise_and(lax.axis_index("sub") + distance, 3)
        near_prepare(payloads.at[number], where * LEAVES, source, values)
    copies[2].wait()
    wait_all(
        near_sent(
            items, ITEMS, info[0], info[4], target, source, values, total, late, total_hbm, left
        )
    )


def sub_kernel(
    info, own, right, across, left, transfer_hbm, couple_hbm, payload_hbm,
    root, terms, relay_hbm, ticket,
    coefs, transfer, couple, arrived,
):
    copies = start_all(((transfer_hbm, transfer), (couple_hbm, couple)), arrived)
    me = lax.axis_index("sub")
    ticket[0] = info[0]
    for distance, pair in enumerate((own, right, across, left)):
        value = pair[:, :RANK].astype(F32) + pair[:, RANK:].astype(F32)
        coefs[lax.bitwise_and(me + distance, 3)] = value
    wait_all(copies)
    lower = nn2(jnp.concatenate([coefs[0], coefs[1]], axis=1), transfer[0])
    upper = nn2(jnp.concatenate([coefs[2], coefs[3]], axis=1), transfer[1])
    root[...] = nn2(jnp.concatenate([lower, upper], axis=1), transfer[2])
    half = lax.shift_right_logical(me, 1)
    sibling = stacked(coefs[lax.bitwise_xor(me, 1)])
    matrix = couple[half]
    is_left = lax.bitwise_and(me, 1) == 0
    terms[0] = fold(jnp.where(is_left, nt(sibling, matrix), nn(sibling, matrix)))
    terms[1] = jnp.where(half == 0, nt2(upper, couple[2]), nn2(lower, couple[2]))


def pair_kernel(
    info, own, partner, transfer_hbm, couple_hbm,
    root, term, ticket,
    transfer, couple, arrived,
):
    ticket[0] = info[0]
    node = lax.shift_right_logical(lax.axis_index("leaf"), 1)
    is_left = lax.bitwise_and(lax.axis_index("leaf"), 1) == 0
    copies = start_all(
        ((transfer_hbm.at[node], transfer), (couple_hbm.at[node], couple)), arrived
    )
    one = jnp.where(is_left, own[...], partner[...])
    two = jnp.where(is_left, partner[...], own[...])
    wait_all(copies)
    root[...] = nn2(jnp.concatenate([one, two], axis=1), transfer[...])
    sibling = stacked(partner[...])
    term[...] = fold(jnp.where(is_left, nt(sibling, couple[...]), nn(sibling, couple[...])))


def near_fall_kernel(
    ticket, items, info, across_hbm, target_hbm,
    order_hbm, gathered_hbm, top_transfer_hbm, top_couple_hbm, pair_term_hbm,
    sub_terms_hbm, terms_hbm, sub_transfer_hbm, transfer_hbm, basis_hbm, inverse_hbm,
    near_own_hbm, near_beside_hbm, known_hbm,
    product, update,
    source, values, total, target, payload, near_arrived,
    order, level, top_transfer, pair_transfer, top_couple, pair_term,
    sub_terms, terms, sub_transfer, transfer, basis, inverse,
    near, rows, moved, arrived, couple_arrived, leaf_arrived,
):
    first = start_all(((across_hbm, payload), (target_hbm, target)), near_arrived)
    total[...] = jnp.zeros_like(total)
    first[0].wait()
    across = lax.bitwise_and(lax.axis_index("sub") + 2, 3)
    near_prepare(payload, across * LEAVES, source, values)
    first[1].wait()
    leaf_place = lax.axis_index("leaf")
    me = lax.axis_index("sub")
    copies = start_all(
        (
            (gathered_hbm, level.at[pl.ds(0, PAIRS)]),
            (top_transfer_hbm.at[pl.ds(TOP_START[1], 8)], top_transfer.at[pl.ds(0, 8)]),
            (top_transfer_hbm.at[pl.ds(TOP_START[2], 6)], top_transfer.at[pl.ds(8, 6)]),
        ),
        arrived,
    )
    couples = start_all(
        [
            (
                top_couple_hbm.at[TOP_START[bit] + lax.shift_right_logical(leaf_place, bit + 1)],
                top_couple.at[bit],
            )
            for bit in range(1, TOP_BITS)
        ],
        couple_arrived,
    )
    later = start_all(
        (
            (top_transfer_hbm.at[lax.shift_right_logical(leaf_place, 1)], pair_transfer),
            (pair_term_hbm, pair_term),
            (sub_terms_hbm, sub_terms),
            (sub_transfer_hbm, sub_transfer),
            (terms_hbm, terms),
            (transfer_hbm, transfer),
        ),
        arrived.at[pl.ds(3, 6)],
    )
    last = start_all(
        (
            (order_hbm, order),
            (near_own_hbm, near.at[0]),
            (near_beside_hbm, near.at[1]),
            (known_hbm, rows),
            (basis_hbm, basis),
            (inverse_hbm, inverse),
        ),
        leaf_arrived,
    )
    near_all(items, 2 * ITEMS, info[1], target, source, values, total)
    copies[0].wait()
    for height in range(1, TOP_BITS - 1):
        below = LEVEL_START[height]
        here = LEVEL_START[height + 1]
        if height < 3:
            copies[height].wait()
        for node in range(PAIRS >> height):
            joined = jnp.concatenate([level[below + 2 * node], level[below + 2 * node + 1]], axis=1)
            level[here + node] = nn2(joined, top_transfer[TOP_START[height] - PAIRS + node])
    wait_all(couples)
    downward = None
    for bit in range(TOP_BITS - 1, 0, -1):
        child = lax.shift_right_logical(leaf_place, bit)
        side = lax.bitwise_and(child, 1)
        sibling = stacked(level[LEVEL_START[bit] + lax.bitwise_xor(child, 1)])
        matrix = top_couple[bit]
        term = fold(jnp.where(side == 0, nt(sibling, matrix), nn(sibling, matrix)))
        if downward is None:
            downward = term
        else:
            position = TOP_START[bit] - PAIRS + lax.shift_right_logical(leaf_place, bit + 1)
            part = top_transfer[position, pl.ds(pl.multiple_of(side * RANK, RANK), RANK), :]
            downward = term + nt2(downward, part)
    wait_all(later)
    side = lax.bitwise_and(leaf_place, 1)
    part = pair_transfer[pl.ds(pl.multiple_of(side * RANK, RANK), RANK), :]
    downward = pair_term[...] + nt2(downward, part)
    half = lax.shift_right_logical(me, 1)
    part = sub_transfer[2, pl.ds(pl.multiple_of(half * RANK, RANK), RANK), :]
    downward = sub_terms[1] + nt2(downward, part)
    side = lax.bitwise_and(me, 1)
    part = sub_transfer[half, pl.ds(pl.multiple_of(side * RANK, RANK), RANK), :]
    downward = sub_terms[0] + nt2(downward, part)
    nodes = [downward]
    node_start = LEAVES - 1
    term_start = 2 * LEAVES - 2
    while len(nodes) < LEAVES:
        node_start -= len(nodes)
        term_start -= 2 * len(nodes)
        children = []
        for number, value in enumerate(nodes):
            lowered = nt2(value, transfer[node_start + number])
            children.append(terms[term_start + 2 * number] + lowered[:, :RANK])
            children.append(terms[term_start + 2 * number + 1] + lowered[:, RANK:])
        nodes = children
    wait_all(last)
    lane = lax.broadcasted_iota(jnp.int32, (LEAF, 2 * RHS), 1)
    is_whole = lane < RHS
    for leaf in range(LEAVES):
        span = slice(leaf * LEAF, (leaf + 1) * LEAF)
        high, low = halves(nodes[leaf])
        far = nt(basis[leaf], jnp.concatenate([high, high, low, low], axis=0))
        field = near[0, leaf] + near[1, leaf] + total[leaf] + far[:, : 2 * RHS] + far[:, 2 * RHS :]
        known = rows[span, :]
        both = jnp.where(is_whole, RIDGE * known + field, known - field)
        correction = nn(inverse[leaf], both.astype(BF16))
        rows[span, :] = jnp.where(is_whole, both, correction)

        def put(step, carry, leaf=leaf):
            first = pl.multiple_of(leaf * LEAF + step * ROW_RUN, ROW_RUN)
            for offset in range(ROW_RUN):
                moved[pl.ds(order[first + offset], 1), :] = rows[pl.ds(first + offset, 1), :]
            return carry

        lax.fori_loop(0, LEAF // ROW_RUN, put, 0)
    for leaf in range(LEAVES):
        span = slice(leaf * LEAF, (leaf + 1) * LEAF)
        turned = moved[span, :].T
        product[:, span] = turned[:RHS].astype(BF16)
        update[:, span] = turned[RHS:].astype(BF16)


VM = pl.BlockSpec(memory_space=pltpu.VMEM)
SM = pl.BlockSpec(memory_space=pltpu.SMEM)
HB = pl.BlockSpec(memory_space=pltpu.HBM)
DMA = pltpu.SemaphoreType.DMA
TOTAL = (LEAVES, LEAF, 2 * RHS)
PADDED_TOTAL = (LEAVES + 1, LEAF, 2 * RHS)
TARGET = (LEAVES + 1, LEAF, FEATURES)
LEVEL = (RHS, RANK)
LATE = pltpu.VMEM((LEAVES + 1 - EARLY, LEAF, 2 * RHS), F32)


def call(kernel, name, inputs, outputs, scratch, flops=None, aliases=None):
    cost = None
    if flops is not None:
        cost = pl.CostEstimate(flops=flops, bytes_accessed=10**6, transcendentals=0)
    return pl.pallas_call(
        kernel,
        out_shape=tuple(jax.ShapeDtypeStruct(dims, kind) for _, dims, kind in outputs),
        in_specs=[spec for spec, _ in inputs],
        out_specs=tuple(spec for spec, _, _ in outputs),
        scratch_shapes=scratch,
        compiler_params=pltpu.CompilerParams(vmem_limit_bytes=VMEM_LIMIT),
        cost_estimate=cost,
        input_output_aliases=aliases or {},
        name=name,
    )(*[value for _, value in inputs])


def held(array):
    return pltpu.VMEM(array.shape, array.dtype)


def from_distance(value, distance):
    pairs = [((receiver + distance) % N_SUB, receiver) for receiver in range(N_SUB)]
    return lax.ppermute(value, "sub", pairs)


def per_device(
    coords, coefficients, targets, point_order, near_list, near_count, leaf_basis, leaf_inverse,
    local_transfer, local_couple, sub_transfer, sub_couple, top_transfer, top_couple,
):
    point_rows = (POINTS, 2 * RHS)
    order_held = pltpu.SMEM(point_order.shape, jnp.int32)
    payload, skeleton, rows, terms = call(
        rise_kernel,
        "rise",
        [
            (HB, value)
            for value in (
                point_order, coefficients, targets, coords,
                leaf_basis, local_transfer, local_couple,
            )
        ],
        [
            (HB, (RHS, PAYLOAD), BF16),
            (VM, (RHS, 2 * RANK), BF16),
            (HB, point_rows, F32),
            (HB, (2 * LEAVES - 2, RHS, RANK), F32),
        ],
        [
            order_held, held(coefficients), held(targets), held(coords),
            pltpu.VMEM(point_rows, F32), held(leaf_basis), held(local_transfer), held(local_couple),
            pltpu.VMEM((RHS, PAYLOAD), BF16), pltpu.VMEM(point_rows, F32),
            pltpu.VMEM((2 * LEAVES - 2, RHS, RANK), F32), DMA((7,)), DMA((3,)),
        ],
    )
    pieces = [skeleton] + [from_distance(skeleton, distance) for distance in (1, 2, 3)]
    target, items, info = call(
        near_plan_kernel,
        "near_plan",
        [(SM, near_list), (SM, near_count), (HB, coords), (HB, skeleton)],
        [(HB, TARGET, BF16), (SM, (3 * ITEMS,), jnp.int32), (SM, (5,), jnp.int32)],
        [held(coords), pltpu.VMEM(TARGET, BF16), DMA((1,)), DMA((1,))],
        PLAN_FLOPS,
    )
    root, sub_terms, relay, ticket = call(
        sub_kernel,
        "sub_rise",
        [(SM, info)] + [(VM, piece) for piece in pieces]
        + [(HB, sub_transfer), (HB, sub_couple), (HB, payload)],
        [
            (VM, LEVEL, F32), (VM, (2,) + LEVEL, F32),
            (HB, payload.shape, BF16), (SM, (1,), jnp.int32),
        ],
        [pltpu.VMEM((N_SUB,) + LEVEL, F32), held(sub_transfer), held(sub_couple), DMA((2,))],
        aliases={7: 2},
    )
    leaf_count = lax.axis_size("leaf")
    partner = lax.ppermute(root, "leaf", [(number, number ^ 1) for number in range(leaf_count)])
    right, left = from_distance(relay, 1), from_distance(relay, 3)
    tables = [
        pltpu.VMEM((GROUP, FEATURES, LEAF), BF16),
        pltpu.VMEM((GROUP, RHS, LEAF), BF16),
    ]
    pair_root, pair_term, ticket = call(
        pair_kernel,
        "pair_rise",
        [
            (SM, ticket), (VM, root), (VM, partner),
            (HB, top_transfer), (HB, top_couple),
        ],
        [(VM, LEVEL, F32), (VM, LEVEL, F32), (SM, (1,), jnp.int32)],
        [pltpu.VMEM((2 * RANK, RANK), BF16), pltpu.VMEM((RANK, RANK), BF16), DMA((2,))],
    )
    same_side = [[side + 2 * pair for pair in range(leaf_count // 2)] for side in range(2)]
    gathered = lax.all_gather(pair_root, "leaf", axis_index_groups=same_side)
    near_own, relay, ticket = call(
        near_first_kernel,
        "near_first",
        [(SM, ticket), (SM, items), (SM, info), (HB, relay), (HB, target)],
        [(HB, TOTAL, F32), (HB, payload.shape, BF16), (SM, (1,), jnp.int32)],
        tables
        + [held(payload), pltpu.VMEM(PADDED_TOTAL, F32), LATE, pltpu.VMEM(TARGET, BF16), DMA((2,)), DMA((3,))],
        FIRST_FLOPS,
    )
    across = from_distance(relay, 2)

    near_beside, ticket = call(
        near_beside_kernel,
        "near_beside",
        [(SM, ticket), (SM, items), (SM, info)] + [(HB, value) for value in (right, left, target)],
        [(HB, TOTAL, F32), (SM, (1,), jnp.int32)],
        tables
        + [
            pltpu.VMEM(PADDED_TOTAL, F32), LATE, pltpu.VMEM(TARGET, BF16),
            pltpu.VMEM((2, RHS, PAYLOAD), BF16), DMA((3,)), DMA((2,)),
        ],
        LATER_FLOPS,
    )
    return call(
        near_fall_kernel,
        "near_fall",
        [(SM, ticket), (SM, items), (SM, info)]
        + [
            (HB, value)
            for value in (
                across, target,
                point_order, gathered, top_transfer, top_couple, pair_term, sub_terms, terms,
                sub_transfer, local_transfer, leaf_basis, leaf_inverse, near_own, near_beside, rows,
            )
        ],
        [(VM, (RHS, POINTS), BF16), (VM, (RHS, POINTS), BF16)],
        tables
        + [
            pltpu.VMEM(PADDED_TOTAL, F32), pltpu.VMEM(TARGET, BF16), held(across), DMA((2,)),
            order_held, pltpu.VMEM((30,) + LEVEL, F32),
            pltpu.VMEM((14, 2 * RANK, RANK), BF16), pltpu.VMEM((2 * RANK, RANK), BF16),
            pltpu.VMEM((TOP_BITS, RANK, RANK), BF16), pltpu.VMEM(LEVEL, F32),
            pltpu.VMEM((2,) + LEVEL, F32), pltpu.VMEM((2 * LEAVES - 2,) + LEVEL, F32),
            held(sub_transfer), held(local_transfer), held(leaf_basis), held(leaf_inverse),
            pltpu.VMEM((2,) + TOTAL, F32), pltpu.VMEM(point_rows, F32), pltpu.VMEM(point_rows, F32),
            DMA((9,)), DMA((TOP_BITS - 1,)), DMA((6,)),
        ],
    )


def solution(mesh):
    both = ("leaf", "sub")
    in_specs = (
        P(None, both), P(None, both), P(None, both), P(both), P(both, None), P(both),
        P(both, None, None), P(both, None, None), P(both, None, None), P(both, None, None),
        P("leaf", None, None), P("leaf", None, None), P(), P(),
    )
    return jax.shard_map(
        per_device,
        mesh=mesh,
        in_specs=in_specs,
        out_specs=(P(None, both), P(None, both)),
        check_vma=False,
    )
```
